32 devices in a mesh: ctx: 8 (over z, core), tp: 4 (over y, x).
Axes of the slice: x: 2, y: 2, z: 4, core: 2. Of those that a mesh axis runs over, the one named last changes fastest.
Arguments:
- hyena_in: bfloat16 [3072, 3, 8192], P(('ctx', 'tp')), may hold values from -6 to 6
- attn_in: bfloat16 [3072, 3, 4096], P(('ctx', 'tp')), may hold values from -8 to 8
- short_taps: float32 [3, 3, 8192], P(None, None, 'tp'), may hold values from -3.5 to 3.5
- decay_rate: float32 [16, 8192], P(None, 'tp'), may hold values from 0 to 1, as said below
- residue: float32 [16, 8192], P(None, 'tp'), may hold values from -1.5 to 1.5
- lengths: int32 [32], replicated, may hold values from 1 to 1920, 3072 in all
Outputs:
- hyena_out: bfloat16 [3072, 8192], P(('ctx', 'tp'))
- attn_out: bfloat16 [3072, 4096], P(('ctx', 'tp'))
The draws below stay inside these ranges and needn't reach their ends.
Inputs may be any that keep to these rules, and one draw needn't show every extreme that they name: `lengths`: segments are packed in order and sum to 3072; the longest has exactly 1920 tokens. `decay_rate`: positive rates.
All inputs are finite; a program needn't handle non-finite values.
Results may differ from the reference program's by a relative error of at most 0.0026.
Values may be sent and summed in bfloat16 or wider, within the bound.
No kernel may reach another device: no remote copies, remote signals or barrier semaphores. Data moves between devices by JAX's collectives and lax.ppermute only.
A program may use at most 192 MiB of HBM per device.

```python
import math
import jax
import jax.numpy as jnp
import numpy as np
from jax import lax

D = 8192
DH = 128
HEADS = 32
STATES = 16
SHORT = 3
SEGS = 32
TOKENS = 3072
MOST = 1920


def draw_decay_rate(key, part):
    keys = jax.random.split(key, 3)
    share = 0.5
    slow_pick = jax.random.uniform(keys[0], (STATES, D)) < share
    slow = jnp.exp(jax.random.uniform(keys[1], (STATES, D), minval=math.log(0.1 / TOKENS), maxval=math.log(2.0 / TOKENS)))
    fast = jnp.exp(jax.random.uniform(keys[2], (STATES, D), minval=math.log(2.0 / TOKENS), maxval=math.log(1.0 / 30.0)))
    return jnp.where(slow_pick, slow, fast).astype(jnp.float32)


def draw_attn_in(key, part):
    keys = jax.random.split(key, 1)
    base = jnp.clip(jax.random.normal(keys[0], (TOKENS, 3, HEADS, DH), jnp.float32), -8.0, 8.0)
    joined = base
    return jnp.clip(joined, -8.0, 8.0).reshape(TOKENS, 3, HEADS * DH).astype(jnp.bfloat16)


def block_levels(stream_key, extent, pieces, least, largest):
    def one(position, blocks):
        steps = jax.random.uniform(jax.random.fold_in(jax.random.fold_in(stream_key, 6), position), (blocks,), jnp.float32, least / len(pieces), largest / len(pieces))
        return jnp.repeat(jnp.exp(steps), extent[position] // blocks).reshape((-1,) + (1,) * (len(extent) - position - 1))

    gain = one(*pieces[0])
    for cut in pieces[1:]:
        gain = gain * one(*cut)
    return gain


def profile(count, total, most, skew):
    loads = [(1 << 20) // math.isqrt(grade ** skew) + 1 for grade in range(2, count + 1)]
    spare, holding = total - most - (count - 1), [1] * (count - 1)
    while spare > 0:
        free = [i for i in range(count - 1) if holding[i] < most]
        mass, budget = sum([loads[i] for i in free]), spare
        for i in free:
            extra = min(most - holding[i], max(1, budget * loads[i] // mass), spare)
            holding[i] = holding[i] + extra
            spare = spare - extra
    return np.array([most] + holding)


def uneven(stream_key, amount, total, most, skew):
    if amount == 2:
        one = jax.random.randint(stream_key, (), max(1, total - most), min(most, total - 1) + 1)
        return jnp.stack([one, total - one])
    sizes = jnp.asarray(profile(amount, total, most, skew), jnp.int32)
    twos = (amount - 1) // 2
    donor, taker = sizes[1:1 + 2 * twos:2], sizes[2:2 + 2 * twos:2]
    room = jnp.minimum(donor - 1, most - taker)
    moved = jax.random.randint(jax.random.fold_in(stream_key, 1), (twos,), 0, 1 << 20) % (room + 1)
    sizes = sizes.at[1:1 + 2 * twos:2].set(donor - moved).at[2:2 + 2 * twos:2].set(taker + moved)
    return sizes[jax.random.permutation(jax.random.fold_in(stream_key, 2), amount)]


def bell_draw(key, dims, scale, limit, pieces=(), kind=jnp.bfloat16):
    gain = block_levels(key, dims, pieces, -0.22, 0.18) if pieces else 1.0
    entries = jax.random.normal(key, dims, jnp.float32) * scale * gain
    return jnp.minimum(jnp.maximum(entries, -limit), limit).astype(kind)


def setup_inputs(seed: int = 0) -> dict:
    arg_keys = jax.random.split(jax.random.key(seed), 7)
    return {
        "hyena_in": bell_draw(arg_keys[0], (TOKENS, 3, D), 1.0, 6.0, ((0, 32),)),
        "attn_in": draw_attn_in(jax.random.fold_in(arg_keys[6], 71), 0),
        "short_taps": bell_draw(arg_keys[2], (SHORT, 3, D), SHORT ** -0.5, 3.5, ((2, 4),), jnp.float32),
        "decay_rate": draw_decay_rate(jax.random.fold_in(arg_keys[6], 71), 0),
        "residue": bell_draw(arg_keys[4], (STATES, D), 0.25, 1.5, ((1, 4),), jnp.float32),
        "lengths": uneven(arg_keys[5], SEGS, TOKENS, MOST, 2).astype(jnp.int32),
    }


def segment_of(positions, segment_ends):
    return lax.optimization_barrier(jnp.sum((segment_ends[None, :] <= positions[:, None]).astype(jnp.int32), axis=1))

def attend_rows(query_rows, key_rows, value_rows, allowed):
    scores = jnp.dot(query_rows, key_rows.T, preferred_element_type=jnp.float32) * (1.0 / math.sqrt(DH))
    row_top = lax.optimization_barrier(jnp.max(jnp.where(allowed, scores, -jnp.inf), axis=1))
    expo = jnp.where(allowed, jnp.exp(scores - row_top[:, None]), jnp.float32(0.0))
    denom = lax.optimization_barrier(jnp.sum(expo, axis=1))
    probs = expo.astype(jnp.bfloat16)
    mixed = jnp.dot(probs, value_rows, preferred_element_type=jnp.float32)
    return (mixed / denom[:, None]).astype(jnp.bfloat16)

def reference(hyena_in, attn_in, short_taps, decay_rate, residue, lengths):
    feats = hyena_in.astype(jnp.float32)
    padded = jnp.concatenate([jnp.zeros((SHORT - 1, 3, D), jnp.float32), feats], axis=0)
    filtered = jnp.zeros((TOKENS, 3, D), jnp.float32)
    for lag in range(SHORT):
        filtered = filtered + short_taps[lag] * padded[SHORT - 1 - lag:SHORT - 1 - lag + TOKENS]
    source = filtered[:, 1] * filtered[:, 2]
    decays = jnp.exp(-decay_rate)
    weight = residue * jnp.sqrt(-jnp.expm1(-2.0 * decay_rate))

    def advance(carried, incoming):
        carried = decays * carried + incoming[None, :]
        return (carried, lax.optimization_barrier(jnp.sum(weight * carried, axis=0)))
    _, long_conv = lax.scan(advance, jnp.zeros((STATES, D), jnp.float32), source)
    hyena_out = (filtered[:, 0] * long_conv).astype(jnp.bfloat16)
    segment_ends = jnp.cumsum(lengths).astype(jnp.int32)
    positions = jnp.arange(TOKENS, dtype=jnp.int32)
    segments = segment_of(positions, segment_ends)
    stacked = attn_in.reshape(TOKENS, 3, HEADS, DH)
    rows_step = math.gcd(TOKENS, 512)
    results = []
    for first in range(0, TOKENS, rows_step):
        last = first + rows_step
        allowed = (positions[None, :last] <= positions[first:last, None]) & (segments[None, :last] == segments[first:last, None])
        query_heads = jnp.transpose(stacked[first:last, 0], (1, 0, 2))
        key_heads = jnp.transpose(stacked[:last, 1], (1, 0, 2))
        value_heads = jnp.transpose(stacked[:last, 2], (1, 0, 2))
        mixed = lax.map(lambda group: attend_rows(group[0], group[1], group[2], allowed), (query_heads, key_heads, value_heads))
        results.append(jnp.transpose(mixed, (1, 0, 2)).reshape(rows_step, HEADS * DH))
    attn_out = jnp.concatenate(results, axis=0)
    return (hyena_out, attn_out)
```

```python
import functools
import math

import jax
import jax.numpy as jnp
from jax import lax
from jax.experimental import pallas as pl
from jax.experimental.pallas import tpu as pltpu
from jax.sharding import PartitionSpec as P

DH = 128
LANES = 128
SUBS = 8
ALL = ("ctx", "tp")
VMEM_BYTES = 48 * 1024 * 1024
MASKED = -1e30


def params_of(semantics=None):
    return pltpu.CompilerParams(vmem_limit_bytes=VMEM_BYTES)


def split_heads_kernel(x_ref, o_ref):
    for h in range(o_ref.shape[0]):
        o_ref[h] = x_ref[:, :, h * DH : (h + 1) * DH]


def split_heads(x, group=4):
    kinds, rows, width = x.shape
    heads = width // DH
    return pl.pallas_call(
        split_heads_kernel,
        grid=(heads // group,),
        in_specs=[pl.BlockSpec((kinds, rows, group * DH), lambda g: (0, 0, g))],
        out_specs=pl.BlockSpec((group, kinds, rows, DH), lambda g: (g, 0, 0, 0)),
        out_shape=jax.ShapeDtypeStruct((heads, kinds, rows, DH), x.dtype),
        compiler_params=params_of(),
        name="split_heads",
    )(x)


def join_heads_kernel(x_ref, o_ref):
    for h in range(x_ref.shape[0]):
        o_ref[:, h * DH : (h + 1) * DH] = x_ref[h]


def join_heads(x, group=8):
    heads, rows, _ = x.shape
    return pl.pallas_call(
        join_heads_kernel,
        grid=(heads // group,),
        in_specs=[pl.BlockSpec((group, rows, DH), lambda g: (g, 0, 0))],
        out_specs=pl.BlockSpec((rows, group * DH), lambda g: (0, g)),
        out_shape=jax.ShapeDtypeStruct((rows, heads * DH), x.dtype),
        compiler_params=params_of(),
        name="join_heads",
    )(x)


def attend_kernel(tile_start_ref, x_ref, start_ref, o_ref, q_s, k_s, v_s, *, key_rows):
    tile = pl.program_id(0)
    blocks, _, rows, _ = x_ref.shape
    query_rows = o_ref.shape[0]
    scale = math.log2(math.e) / math.sqrt(DH)

    @pl.when(tile == 0)
    def _():
        @pl.loop(0, blocks)
        def _(b):
            place = pl.ds(pl.multiple_of(b * rows, rows), rows)
            q_s[place] = x_ref[b, 0]
            k_s[place] = x_ref[b, 1]
            v_s[place] = x_ref[b, 2]

    first_row = tile * query_rows
    q = q_s[pl.ds(pl.multiple_of(first_row, query_rows), query_rows)]
    start = start_ref[...]
    start = jnp.concatenate([start] * (key_rows // LANES), axis=1)
    shape = (query_rows, key_rows)
    row = first_row + lax.broadcasted_iota(jnp.int32, shape, 0)
    col = lax.broadcasted_iota(jnp.int32, shape, 1)
    last = (first_row + query_rows - 1) // key_rows
    first = tile_start_ref[tile] // key_rows

    def step(i, carry):
        top, denom, mixed = carry
        base = pl.multiple_of((last - i) * key_rows, key_rows)
        k = k_s[pl.ds(base, key_rows)]
        v = v_s[pl.ds(base, key_rows)]
        s = lax.dot_general(q, k, (((1,), (1,)), ((), ())), preferred_element_type=jnp.float32)
        pos = col + base
        s = jnp.where((pos >= start) & (pos <= row), s, MASKED)
        new_top = jnp.maximum(top, jnp.max(s, axis=1, keepdims=True))
        p = jnp.exp2((s - new_top) * scale)
        rescale = jnp.exp2((top - new_top) * scale)
        denom = denom * rescale + jnp.sum(p, axis=1, keepdims=True)
        mixed = mixed * rescale + jnp.dot(
            p.astype(jnp.bfloat16), v, preferred_element_type=jnp.float32
        )
        return new_top, denom, mixed

    carry = (
        jnp.full((query_rows, 1), MASKED, jnp.float32),
        jnp.zeros((query_rows, 1), jnp.float32),
        jnp.zeros((query_rows, DH), jnp.float32),
    )
    _, denom, mixed = lax.fori_loop(0, last - first + 1, step, carry)
    o_ref[...] = (mixed / denom).astype(o_ref.dtype)


def attend(x, start, query_rows=512, key_rows=512):
    blocks, _, rows, _ = x.shape
    tokens = blocks * rows
    query_rows, key_rows = math.gcd(tokens, query_rows), math.gcd(tokens, key_rows)
    wide_start = jnp.broadcast_to(start[:, None], (tokens, LANES))
    return pl.pallas_call(
        functools.partial(attend_kernel, key_rows=key_rows),
        grid_spec=pltpu.PrefetchScalarGridSpec(
            num_scalar_prefetch=1,
            grid=(tokens // query_rows,),
            in_specs=[
                pl.BlockSpec(x.shape, lambda t, s: (0, 0, 0, 0)),
                pl.BlockSpec((query_rows, LANES), lambda t, s: (t, 0)),
            ],
            out_specs=pl.BlockSpec((query_rows, DH), lambda t, s: (t, 0)),
            scratch_shapes=[pltpu.VMEM((tokens, DH), x.dtype)] * 3,
        ),
        out_shape=jax.ShapeDtypeStruct((tokens, DH), x.dtype),
        compiler_params=params_of(),
        cost_estimate=pl.CostEstimate(
            flops=2 * tokens * tokens * DH,
            bytes_accessed=x.size * 2 + tokens * (DH * 2 + LANES * 4),
            transcendentals=tokens * tokens // 2,
        ),
        name="attend",
    )(start[::query_rows], x, wide_start)


def shift_down(a, k):
    return pltpu.roll(a, k, 0)


def local_conv_kernel(x_ref, edge_ref, taps_ref, rate_ref, weight_ref, y_ref, q_ref, end_ref, xs, out_s):
    kinds, rows, width = x_ref.shape
    modes = rate_ref.shape[0]
    run = rows // SUBS
    taps_count = taps_ref.shape[0] // kinds
    rim = taps_count - 1
    head = SUBS
    sub = lax.broadcasted_iota(jnp.int32, (SUBS, LANES), 0)

    def wide(row):
        return jnp.broadcast_to(row, (SUBS, LANES))

    for c in range(width // LANES):
        lanes = slice(c * LANES, (c + 1) * LANES)
        for i in range(kinds):
            xs[i, head - rim : head] = edge_ref[i * rim : (i + 1) * rim, lanes]
            xs[i, head:] = x_ref[i, :, lanes].astype(jnp.float32)
        taps = taps_ref[:, lanes]
        rate = rate_ref[:, lanes]
        weight = weight_ref[:, lanes]
        decay = jnp.exp(-rate)
        decay_run = jnp.exp(rate * (-1.0 * run))

        def at(i, j):
            return xs[i, pl.ds(head + j, SUBS, stride=run)]

        def filtered(i):
            seen = [at(i, j - taps_count + 1) for j in range(taps_count - 1)]
            rows_of = [wide(taps[j * kinds + i : j * kinds + i + 1]) for j in range(taps_count)]
            out = []
            for j in range(run):
                seen.append(at(i, j))
                out.append(
                    sum(rows_of[lag] * seen[-1 - lag] for lag in range(1, taps_count))
                    + rows_of[0] * seen[-1]
                )
            return out

        for j, value in enumerate(filtered(0)):
            out_s[0, pl.ds(j, SUBS, stride=run)] = value
        q_ref[:, lanes] = out_s[0]
        source = [a * b for a, b in zip(filtered(1), filtered(2))]

        power = weight
        lags = []
        for j in range(run):
            lags.append(wide(jnp.sum(power, axis=0, keepdims=True)))
            power = power * decay
        conv = []
        for j in range(run):
            total = lags[0] * source[j]
            for k in range(1, j + 1):
                total = total + lags[k] * source[j - k]
            conv.append(total)

        for n in range(modes):
            d = wide(decay[n : n + 1])
            state = source[0]
            for j in range(1, run):
                state = state * d + source[j]
            span = wide(decay_run[n : n + 1])
            for k in (1, 2, 4):
                state = state + jnp.where(sub >= k, span * shift_down(state, k), 0.0)
                span = span * span
            end_ref[0, n : n + 1, lanes] = state[SUBS - 1 : SUBS]
            entering = jnp.where(sub >= 1, shift_down(state, 1), 0.0) * wide(weight[n : n + 1])
            for j in range(run):
                entering = entering * d
                conv[j] = conv[j] + entering
        for j in range(run):
            out_s[1, pl.ds(j, SUBS, stride=run)] = conv[j]
        y_ref[:, lanes] = out_s[1]


def chunk_place(ctx_size, tp_size):
    return lambda g: ((g % ctx_size) * tp_size + g // ctx_size, 0, 0)


def local_conv(x, edge, taps, rate, weight, ctx_size, tp_size):
    kinds, rows, channels = x.shape
    modes = rate.shape[0]
    width = channels // (ctx_size * tp_size)
    across = lambda g: (0, g)
    return pl.pallas_call(
        local_conv_kernel,
        grid=(channels // width,),
        in_specs=[
            pl.BlockSpec((kinds, rows, width), lambda g: (0, 0, g)),
            pl.BlockSpec((edge.shape[0], width), across),
            pl.BlockSpec((taps.shape[0], width), across),
            pl.BlockSpec((modes, width), across),
            pl.BlockSpec((modes, width), across),
        ],
        out_specs=[
            pl.BlockSpec((rows, width), across),
            pl.BlockSpec((rows, width), across),
            pl.BlockSpec((1, modes, width), chunk_place(ctx_size, tp_size)),
        ],
        out_shape=[
            jax.ShapeDtypeStruct((rows, channels), jnp.float32),
            jax.ShapeDtypeStruct((rows, channels), jnp.float32),
            jax.ShapeDtypeStruct((channels // width, modes, width), jnp.float32),
        ],
        scratch_shapes=[
            pltpu.VMEM((kinds, rows + SUBS, LANES), jnp.float32),
            pltpu.VMEM((2, rows, LANES), jnp.float32),
        ],
        compiler_params=params_of(),
        cost_estimate=pl.CostEstimate(
            flops=rows * channels * 100,
            bytes_accessed=rows * channels * 14,
            transcendentals=2 * modes * channels,
        ),
        name="local_conv",
    )(x, edge, taps, rate, weight)


def prefix_kernel(rate_ref, end_ref, o_ref, *, rows):
    blocks = end_ref.shape[0]
    span = jnp.exp(rate_ref[...] * (-1.0 * rows))
    state = jnp.zeros_like(span)
    for b in range(blocks):
        o_ref[b] = state
        state = state * span + end_ref[b]


def prefix(rate, ends, rows):
    return pl.pallas_call(
        functools.partial(prefix_kernel, rows=rows),
        out_shape=jax.ShapeDtypeStruct(ends.shape, ends.dtype),
        compiler_params=params_of(),
        name="prefix",
    )(rate, ends)


def add_entering_kernel(y_ref, q_ref, state_ref, rate_ref, weight_ref, o_ref):
    rows, width = y_ref.shape
    modes = rate_ref.shape[0]
    sub = lax.broadcasted_iota(jnp.int32, (SUBS, LANES), 0).astype(jnp.float32)
    for c in range(width // LANES):
        lanes = slice(c * LANES, (c + 1) * LANES)
        rate = rate_ref[:, lanes]
        start = state_ref[0, :, lanes] * weight_ref[:, lanes]
        step = jnp.exp(rate * (-1.0 * SUBS))
        terms, steps = [], []
        for n in range(modes):
            fall = jnp.exp((sub + 1.0) * (-rate[n : n + 1]))
            terms.append(fall * start[n : n + 1])
            steps.append(jnp.broadcast_to(step[n : n + 1], (SUBS, LANES)))
        pair = []
        for t in range(rows // SUBS):
            place = slice(t * SUBS, (t + 1) * SUBS)
            total = y_ref[place, lanes]
            parts = list(terms)
            while len(parts) > 1:
                parts = [a + b for a, b in zip(parts[::2], parts[1::2])] + (
                    [parts[-1]] if len(parts) % 2 else []
                )
            pair.append(q_ref[place, lanes] * (total + parts[0]))
            if len(pair) == 2:
                o_ref[(t - 1) * SUBS : (t + 1) * SUBS, lanes] = jnp.concatenate(
                    pair, axis=0
                ).astype(o_ref.dtype)
                pair = []
            terms = [a * b for a, b in zip(terms, steps)]


def add_entering(y, q, states, rate, weight, ctx_size, tp_size):
    rows, channels = y.shape
    modes = rate.shape[0]
    width = channels // (ctx_size * tp_size)
    across = lambda g: (0, g)
    return pl.pallas_call(
        add_entering_kernel,
        grid=(channels // width,),
        in_specs=[
            pl.BlockSpec((rows, width), across),
            pl.BlockSpec((rows, width), across),
            pl.BlockSpec((1, modes, width), chunk_place(ctx_size, tp_size)),
            pl.BlockSpec((modes, width), across),
            pl.BlockSpec((modes, width), across),
        ],
        out_specs=pl.BlockSpec((rows, width), across),
        out_shape=jax.ShapeDtypeStruct((rows, channels), jnp.bfloat16),
        compiler_params=params_of(),
        cost_estimate=pl.CostEstimate(
            flops=rows * channels * 36,
            bytes_accessed=rows * channels * 10,
            transcendentals=modes * channels * 9,
        ),
        name="add_entering",
    )(y, q, states, rate, weight)


def exchange(x, axis):
    return lax.all_to_all(x, axis, split_axis=0, concat_axis=0, tiled=True)


def gather_tp(x):
    tp_size = lax.axis_size("tp")
    spread = exchange(jnp.broadcast_to(x[None], (tp_size,) + x.shape), "tp")
    return jnp.transpose(spread, (1, 0, 2)).reshape(x.shape[0], -1)


def segment_starts(lengths, tokens):
    order = jnp.arange(lengths.shape[0], dtype=jnp.int32)
    ends = jnp.sum(jnp.where(order[:, None] <= order[None, :], lengths[:, None], 0), axis=0)
    position = jnp.arange(tokens, dtype=jnp.int32)
    passed = jnp.where(ends[None, :] <= position[:, None], ends[None, :], 0)
    return jnp.max(passed, axis=1)


def by_tokens(hyena_in, attn_in, short_taps, decay_rate, residue, lengths):
    rows, kinds, channels = hyena_in.shape
    ctx_size, tp_size = lax.axis_size("ctx"), lax.axis_size("tp")
    devices = ctx_size * tp_size
    taps_count = short_taps.shape[0]
    modes = decay_rate.shape[0]

    heads_out = split_heads(jnp.transpose(attn_in, (1, 0, 2)))
    by_head = exchange(heads_out, ALL)

    x = jnp.transpose(hyena_in, (1, 0, 2))
    edge = x[:, rows - taps_count + 1 :].reshape(kinds * (taps_count - 1), channels)
    edge = lax.ppermute(edge, ALL, [(i, i + 1) for i in range(devices - 1)]).astype(jnp.float32)
    own_weight = residue * jnp.sqrt(-jnp.expm1(-2.0 * decay_rate))
    flat_taps = short_taps.reshape(taps_count * kinds, -1)
    table = gather_tp(jnp.concatenate([decay_rate, own_weight, flat_taps], axis=0))
    rate, weight, taps = table[:modes], table[modes : 2 * modes], table[2 * modes :]
    y, q, ends = local_conv(x, edge, taps, rate, weight, ctx_size, tp_size)
    width = channels // devices
    own_rate = lax.dynamic_slice_in_dim(decay_rate, lax.axis_index("ctx") * width, width, 1)
    entering = exchange(prefix(own_rate, exchange(ends, ALL), rows), ALL)
    hyena_out = add_entering(y, q, entering, rate, weight, ctx_size, tp_size)

    mixed = attend(by_head, segment_starts(lengths, rows * devices))
    attn_out = join_heads(exchange(mixed.reshape(devices, rows, DH), ALL))
    return hyena_out, attn_out


exact_mode = lax.Precision.HIGHEST


def from_behind(block, axis, distance):
    devices = range(lax.axis_size(axis))
    route = [(i - distance, i) for i in devices if i - distance in devices]
    return lax.ppermute(block, axis, route)


def carried_in(part, axis, combine, identity):
    place = lax.axis_index(axis)
    gathered = jax.tree.map(lambda a: lax.all_gather(a, axis), part)
    state = jax.tree.map(lambda a, e: jnp.zeros_like(a) + jnp.asarray(e, a.dtype), part, identity)

    def one(lap, state):
        return combine(
            state, jax.tree.map(lambda a: lax.dynamic_index_in_dim(a, lap, 0, False), gathered)
        )

    return lax.fori_loop(0, place, one, state)


def segment_of(positions, segment_ends):
    return jnp.sum((segment_ends[None, :] <= positions[:, None]).astype(jnp.int32), axis=1)


def by_channels(hyena_in, attn_in, short_taps, decay_rate, residue, lengths):
    hyena_cols, attention_cols = (
        lax.all_to_all(hyena_in, "tp", split_axis=2, concat_axis=0, tiled=True),
        lax.all_to_all(attn_in, "tp", split_axis=2, concat_axis=0, tiled=True),
    )
    block_rows = hyena_cols.shape[0]
    rim_rows = short_taps.shape[0] - 1
    edge_rows = from_behind(hyena_cols[block_rows - rim_rows :], "ctx", 1)
    extended = jnp.concatenate([edge_rows, hyena_cols], axis=0).astype(jnp.float32)
    filtered = jnp.zeros(hyena_cols.shape, jnp.float32)
    for lag in range(rim_rows + 1):
        filtered = (
            filtered + short_taps[lag] * extended[rim_rows - lag : rim_rows - lag + block_rows]
        )
    query_side = filtered[:, 0]
    source = filtered[:, 1] * filtered[:, 2]
    channels = source.shape[1]
    weight = residue * jnp.sqrt(-jnp.expm1(-2.0 * decay_rate))
    sub_length = math.gcd(32, block_rows)
    pieces = block_rows // sub_length
    offsets = jnp.arange(sub_length, dtype=jnp.float32)
    powers = jnp.exp(-offsets[:, None, None] * decay_rate[None])
    lag_values = jnp.einsum("onc,nc->oc", powers, weight, precision=exact_mode)
    lag_index = jnp.arange(sub_length, dtype=jnp.int32)
    selector = (
        lag_index[:, None, None] - lag_index[None, :, None] == lag_index[None, None, :]
    ).astype(jnp.float32)
    toeplitz = jnp.einsum("tso,oc->tsc", selector, lag_values, precision=exact_mode)
    grouped = source.reshape(pieces, sub_length, channels)
    inner = jnp.einsum("tsc,bsc->btc", toeplitz, grouped, precision=exact_mode)
    tail_powers = jnp.exp(-(sub_length - 1.0 - offsets)[:, None, None] * decay_rate[None])
    own_states = jnp.einsum("snc,bsc->bnc", tail_powers, grouped, precision=exact_mode)
    sub_decay = jnp.exp(-sub_length * decay_rate)

    def carry_states(carried, incoming):
        return (sub_decay * carried + incoming, carried)

    local_end, entering = lax.scan(carry_states, jnp.zeros_like(sub_decay), own_states)
    block_decay = jnp.exp(-block_rows * decay_rate)

    def combine(earlier, later):
        return (earlier[0] * later[0], later[0] * earlier[1] + later[1])

    _, arriving = carried_in(
        (block_decay, local_end),
        "ctx",
        combine,
        (jnp.ones_like(block_decay), jnp.zeros_like(local_end)),
    )
    starts = jnp.arange(pieces, dtype=jnp.float32) * sub_length
    all_entering = entering + jnp.exp(-starts[:, None, None] * decay_rate[None]) * arriving[None]
    rise_powers = jnp.exp(-(offsets + 1.0)[:, None, None] * decay_rate[None]) * weight[None]
    from_state = jnp.einsum("tnc,bnc->btc", rise_powers, all_entering, precision=exact_mode)
    long_conv = (inner + from_state).reshape(block_rows, channels)
    hyena_local = (query_side * long_conv).astype(jnp.bfloat16)
    head_cols = attention_cols.shape[2]
    local_heads = head_cols // DH
    queries = attention_cols[:, 0].reshape(block_rows, local_heads, DH)
    keyvals = attention_cols[:, 1:3]
    order = jnp.arange(lengths.shape[0], dtype=jnp.int32)
    segment_ends = jnp.sum(jnp.where(order[:, None] <= order[None, :], lengths[:, None], 0), axis=0)
    block_index = lax.axis_index("ctx")
    query_pos = block_index * block_rows + jnp.arange(block_rows, dtype=jnp.int32)
    query_seg = segment_of(query_pos, segment_ends)
    score_scale = 1.0 / math.sqrt(DH)

    def attend_part(softmax_state, part, key_start):
        count = part.shape[0]
        key_pos = key_start + jnp.arange(count, dtype=jnp.int32)
        key_seg = segment_of(key_pos, segment_ends)
        allowed = (
            (key_pos[None, :] <= query_pos[:, None])
            & (key_seg[None, :] == query_seg[:, None])
            & (key_pos >= 0)[None, :]
        )

        def compute(carried):
            row_top, denom, weighted = carried
            key_rows = part[:, 0].reshape(count, local_heads, DH)
            value_rows = part[:, 1].reshape(count, local_heads, DH)
            scores = (
                jnp.einsum("qhd,khd->hqk", queries, key_rows, preferred_element_type=jnp.float32)
                * score_scale
            )
            masked = jnp.where(allowed[None], scores, jnp.float32(-1e30))
            new_top = jnp.maximum(row_top, jnp.max(masked, axis=2))
            expo = jnp.where(allowed[None], jnp.exp(scores - new_top[:, :, None]), jnp.float32(0.0))
            rescale = jnp.exp(row_top - new_top)
            denom = denom * rescale + jnp.sum(expo, axis=2)
            probs = expo.astype(jnp.bfloat16)
            added = jnp.einsum(
                "hqk,khd->qhd", probs, value_rows, preferred_element_type=jnp.float32
            )
            weighted = weighted * jnp.transpose(rescale)[:, :, None] + added
            return (new_top, denom, weighted)

        def keep(carried):
            return carried

        return lax.cond(jnp.any(allowed), compute, keep, softmax_state)

    initial = (
        jnp.full((local_heads, block_rows), -1e30, jnp.float32),
        jnp.zeros((local_heads, block_rows), jnp.float32),
        jnp.zeros((block_rows, local_heads, DH), jnp.float32),
    )
    piece = lax.all_gather(keyvals, "ctx", axis=0, tiled=True)
    rows = piece.shape[0]
    step_rows = math.gcd(rows, 512)

    def advance(count, carried):
        part = lax.dynamic_slice_in_dim(piece, count * step_rows, step_rows, 0)
        return attend_part(carried, part, count * step_rows)

    final_state = lax.fori_loop(0, rows // step_rows, advance, initial)
    _, denom, weighted = final_state
    attention_local = (
        (weighted / jnp.transpose(denom)[:, :, None])
        .reshape(block_rows, head_cols)
        .astype(jnp.bfloat16)
    )
    hyena_out, attn_out = (
        lax.all_to_all(hyena_local, "tp", split_axis=0, concat_axis=1, tiled=True),
        lax.all_to_all(attention_local, "tp", split_axis=0, concat_axis=1, tiled=True),
    )
    return (hyena_out, attn_out)


def per_device(hyena_in, attn_in, short_taps, decay_rate, residue, lengths):
    rows, _, channels = hyena_in.shape
    devices = lax.axis_size("ctx") * lax.axis_size("tp")
    one_head_each = attn_in.shape[2] == devices * DH
    whole_tiles = rows % (2 * SUBS) == 0 and channels % (devices * LANES) == 0
    plan = by_tokens if one_head_each and whole_tiles else by_channels
    return plan(hyena_in, attn_in, short_taps, decay_rate, residue, lengths)


def solution(mesh):
    placed = (
        P(("ctx", "tp"), None, None),
        P(("ctx", "tp"), None, None),
        P(None, None, "tp"),
        P(None, "tp"),
        P(None, "tp"),
        P(),
    )
    return jax.shard_map(
        per_device,
        mesh=mesh,
        in_specs=placed,
        out_specs=(P(("ctx", "tp"), None), P(("ctx", "tp"), None)),
        check_vma=False,
    )
```

```python
import functools
import math

import jax
import jax.numpy as jnp
from jax import lax
from jax.experimental import pallas as pl
from jax.experimental.pallas import tpu as pltpu
from jax.sharding import PartitionSpec as P

DH = 128
LANES = 128
SUBS = 8
ALL = ("ctx", "tp")
VMEM_BYTES = 48 * 1024 * 1024
MASKED = -1e30


def params_of(semantics=None):
    return pltpu.CompilerParams(vmem_limit_bytes=VMEM_BYTES)


def split_heads_kernel(x_ref, o_ref):
    for h in range(o_ref.shape[0]):
        o_ref[h] = x_ref[:, :, h * DH : (h + 1) * DH]


def split_heads(x, group=4):
    kinds, rows, width = x.shape
    heads = width // DH
    return pl.pallas_call(
        split_heads_kernel,
        grid=(heads // group,),
        in_specs=[pl.BlockSpec((kinds, rows, group * DH), lambda g: (0, 0, g))],
        out_specs=pl.BlockSpec((group, kinds, rows, DH), lambda g: (g, 0, 0, 0)),
        out_shape=jax.ShapeDtypeStruct((heads, kinds, rows, DH), x.dtype),
        compiler_params=params_of(),
        name="split_heads",
    )(x)


def join_heads_kernel(x_ref, o_ref):
    for h in range(x_ref.shape[0]):
        o_ref[:, h * DH : (h + 1) * DH] = x_ref[h]


def join_heads(x, group=8):
    heads, rows, _ = x.shape
    return pl.pallas_call(
        join_heads_kernel,
        grid=(heads // group,),
        in_specs=[pl.BlockSpec((group, rows, DH), lambda g: (g, 0, 0))],
        out_specs=pl.BlockSpec((rows, group * DH), lambda g: (0, g)),
        out_shape=jax.ShapeDtypeStruct((rows, heads * DH), x.dtype),
        compiler_params=params_of(),
        name="join_heads",
    )(x)


def attend_kernel(tile_start_ref, x_ref, start_ref, o_ref, q_s, k_s, v_s, *, key_rows):
    tile = pl.program_id(0)
    blocks, _, rows, _ = x_ref.shape
    query_rows = o_ref.shape[0]
    scale = math.log2(math.e) / math.sqrt(DH)

    @pl.when(tile == 0)
    def _():
        @pl.loop(0, blocks)
        def _(b):
            place = pl.ds(pl.multiple_of(b * rows, rows), rows)
            q_s[place] = x_ref[b, 0]
            k_s[place] = x_ref[b, 1]
            v_s[place] = x_ref[b, 2]

    first_row = tile * query_rows
    q = q_s[pl.ds(pl.multiple_of(first_row, query_rows), query_rows)]
    start = start_ref[...]
    start = jnp.concatenate([start] * (key_rows // LANES), axis=1)
    shape = (query_rows, key_rows)
    row = first_row + lax.broadcasted_iota(jnp.int32, shape, 0)
    col = lax.broadcasted_iota(jnp.int32, shape, 1)
    last = (first_row + query_rows - 1) // key_rows
    first = tile_start_ref[tile] // key_rows

    def step(i, carry):
        top, denom, mixed = carry
        base = pl.multiple_of((last - i) * key_rows, key_rows)
        k = k_s[pl.ds(base, key_rows)]
        v = v_s[pl.ds(base, key_rows)]
        s = lax.dot_general(q, k, (((1,), (1,)), ((), ())), preferred_element_type=jnp.float32)
        pos = col + base
        s = jnp.where((pos >= start) & (pos <= row), s, MASKED)
        new_top = jnp.maximum(top, jnp.max(s, axis=1, keepdims=True))
        p = jnp.exp2((s - new_top) * scale)
        rescale = jnp.exp2((top - new_top) * scale)
        denom = denom * rescale + jnp.sum(p, axis=1, keepdims=True)
        mixed = mixed * rescale + jnp.dot(
            p.astype(jnp.bfloat16), v, preferred_element_type=jnp.float32
        )
        return new_top, denom, mixed

    carry = (
        jnp.full((query_rows, 1), MASKED, jnp.float32),
        jnp.zeros((query_rows, 1), jnp.float32),
        jnp.zeros((query_rows, DH), jnp.float32),
    )
    _, denom, mixed = lax.fori_loop(0, last - first + 1, step, carry)
    o_ref[...] = (mixed / denom).astype(o_ref.dtype)


def attend(x, start, query_rows=512, key_rows=512):
    blocks, _, rows, _ = x.shape
    tokens = blocks * rows
    query_rows, key_rows = math.gcd(tokens, query_rows), math.gcd(tokens, key_rows)
    wide_start = jnp.broadcast_to(start[:, None], (tokens, LANES))
    return pl.pallas_call(
        functools.partial(attend_kernel, key_rows=key_rows),
        grid_spec=pltpu.PrefetchScalarGridSpec(
            num_scalar_prefetch=1,
            grid=(tokens // query_rows,),
            in_specs=[
                pl.BlockSpec(x.shape, lambda t, s: (0, 0, 0, 0)),
                pl.BlockSpec((query_rows, LANES), lambda t, s: (t, 0)),
            ],
            out_specs=pl.BlockSpec((query_rows, DH), lambda t, s: (t, 0)),
            scratch_shapes=[pltpu.VMEM((tokens, DH), x.dtype)] * 3,
        ),
        out_shape=jax.ShapeDtypeStruct((tokens, DH), x.dtype),
        compiler_params=params_of(),
        cost_estimate=pl.CostEstimate(
            flops=2 * tokens * tokens * DH,
            bytes_accessed=x.size * 2 + tokens * (DH * 2 + LANES * 4),
            transcendentals=tokens * tokens // 2,
        ),
        name="attend",
    )(start[::query_rows], x, wide_start)


def pick(k, refs, place):
    value = refs[0][place]
    for other in range(1, len(refs)):
        value = jnp.where(k == other, refs[other][place], value)
    return value


def local_conv_kernel(t_ref, x_ref, edge_ref, *refs, modes, taps_count, tp_size):
    tables, (y_ref, q_ref), ends = refs[:tp_size], refs[tp_size : tp_size + 2], refs[tp_size + 2 : -2]
    xs, out_s = refs[-2:]
    kinds, rows, width = x_ref.shape
    k, chunk = pl.program_id(0), pl.program_id(1)
    run = rows // SUBS
    rim = taps_count - 1
    head = SUBS
    sub = lax.broadcasted_iota(jnp.int32, (SUBS, LANES), 0)

    def wide(row):
        return jnp.broadcast_to(row, (SUBS, LANES))

    for c in range(width // LANES):
        lanes = slice(c * LANES, (c + 1) * LANES)
        spot = pl.ds(pl.multiple_of(chunk * width + c * LANES, LANES), LANES)
        for i in range(kinds):
            xs[i, head - rim : head] = edge_ref[i * rim : (i + 1) * rim, lanes]
            xs[i, head:] = x_ref[i, :, lanes].astype(jnp.float32)
        rate = pick(k, tables, (slice(0, modes), spot))
        weight = pick(k, tables, (slice(modes, 2 * modes), spot))
        taps = pick(k, tables, (slice(2 * modes, 2 * modes + taps_count * kinds), spot))
        decay = jnp.exp(-rate)
        decay_run = jnp.exp(rate * (-1.0 * run))

        def at(i, j):
            return xs[i, pl.ds(head + j, SUBS, stride=run)]

        def filtered(i):
            seen = [at(i, j - rim) for j in range(rim)]
            rows_of = [wide(taps[j * kinds + i : j * kinds + i + 1]) for j in range(taps_count)]
            out = []
            for j in range(run):
                seen.append(at(i, j))
                out.append(
                    sum(rows_of[lag] * seen[-1 - lag] for lag in range(1, taps_count))
                    + rows_of[0] * seen[-1]
                )
            return out

        for j, value in enumerate(filtered(0)):
            out_s[0, pl.ds(j, SUBS, stride=run)] = value
        q_ref[:, lanes] = out_s[0]
        source = [a * b for a, b in zip(filtered(1), filtered(2))]

        power = weight
        lags = []
        for j in range(run):
            lags.append(wide(jnp.sum(power, axis=0, keepdims=True)))
            power = power * decay
        conv = []
        for j in range(run):
            total = lags[0] * source[j]
            for lag in range(1, j + 1):
                total = total + lags[lag] * source[j - lag]
            conv.append(total)

        last = []
        for n in range(modes):
            d = wide(decay[n : n + 1])
            state = source[0]
            for j in range(1, run):
                state = state * d + source[j]
            span = wide(decay_run[n : n + 1])
            for hop in (1, 2, 4):
                state = state + jnp.where(sub >= hop, span * pltpu.roll(state, hop, 0), 0.0)
                span = span * span
            last.append(state[SUBS - 1 : SUBS])
            entering = jnp.where(sub >= 1, pltpu.roll(state, 1, 0), 0.0) * wide(weight[n : n + 1])
            for j in range(run):
                entering = entering * d
                conv[j] = conv[j] + entering
        last = jnp.concatenate(last, axis=0)
        for other in range(tp_size):

            @pl.when(k == other)
            def _(other=other):
                ends[other][:, spot] = last

        for j in range(run):
            out_s[1, pl.ds(j, SUBS, stride=run)] = conv[j]
        y_ref[:, lanes] = out_s[1]


def local_conv(t, x, edge, tables, modes, taps_count, width=256):
    kinds, rows, channels = x.shape
    tp_size = len(tables)
    quarter = channels // tp_size
    chunks = quarter // width
    whole = lambda k, c, t: (0, 0)
    across = lambda k, c, t: (0, (k ^ t[0]) * chunks + c)
    return pl.pallas_call(
        functools.partial(
            local_conv_kernel, modes=modes, taps_count=taps_count, tp_size=tp_size
        ),
        grid_spec=pltpu.PrefetchScalarGridSpec(
            num_scalar_prefetch=1,
            grid=(tp_size, chunks),
            in_specs=[
                pl.BlockSpec((kinds, rows, width), lambda k, c, t: (0, *across(k, c, t))),
                pl.BlockSpec((edge.shape[0], width), across),
            ]
            + [pl.BlockSpec(tables[0].shape, whole)] * tp_size,
            out_specs=[pl.BlockSpec((rows, width), across)] * 2
            + [pl.BlockSpec((modes, quarter), whole)] * tp_size,
            scratch_shapes=[
                pltpu.VMEM((kinds, rows + SUBS, LANES), jnp.float32),
                pltpu.VMEM((2, rows, LANES), jnp.float32),
            ],
        ),
        out_shape=[jax.ShapeDtypeStruct((rows, channels), jnp.float32)] * 2
        + [jax.ShapeDtypeStruct((modes, quarter), jnp.float32)] * tp_size,
        compiler_params=params_of(),
        cost_estimate=pl.CostEstimate(
            flops=rows * channels * 100,
            bytes_accessed=rows * channels * 14,
            transcendentals=2 * modes * channels,
        ),
        name="local_conv",
    )(t, x, edge, *tables)


def block_end_kernel(t_ref, rate_ref, *refs, rows):
    ends, o_ref = refs[:-1], refs[-1]
    rate = rate_ref[...]
    total = jnp.zeros_like(rate)
    for k, end in enumerate(ends):
        later = len(ends) - 1 - (k ^ t_ref[0])
        total = total + jnp.exp(rate * (later * -rows).astype(jnp.float32)) * end[...]
    o_ref[...] = total


def block_starts_kernel(t_ref, rate_ref, enter_ref, *refs, rows):
    size = len(refs) // 2
    ends, outs = refs[:size], refs[size:]
    rate = rate_ref[...]
    span = jnp.exp(rate * (-1.0 * rows))
    t = t_ref[0]
    state = enter_ref[...]
    for place in range(size):
        mine = place ^ t
        for k in range(size):

            @pl.when(mine == k)
            def _(k=k, state=state):
                outs[k][...] = state

        end = pick(mine, ends, Ellipsis)
        state = state * span + end


def small_call(kernel, t, name, outs, *arrays, **sizes):
    shape = jax.ShapeDtypeStruct(arrays[0].shape, jnp.float32)
    vmem = pl.BlockSpec(memory_space=pltpu.VMEM)
    result = pl.pallas_call(
        functools.partial(kernel, **sizes),
        in_specs=[pl.BlockSpec(memory_space=pltpu.SMEM)] + [vmem] * len(arrays),
        out_specs=[vmem] * outs,
        out_shape=[shape] * outs,
        compiler_params=params_of(),
        name=name,
    )(t, *arrays)
    return result


def scan_ctx(rate, value, block_rows):
    size = lax.axis_size("ctx")
    earlier = None
    held, distance = value, 1
    while distance < size:
        route = [(i, i + distance) for i in range(size - distance)]
        seen = lax.ppermute(held, "ctx", route)
        if earlier is None:
            earlier = seen
        else:
            earlier = earlier + jnp.exp(rate * (-1.0 * block_rows * (distance - 1))) * seen
        held = held + jnp.exp(rate * (-1.0 * block_rows * distance)) * seen
        distance *= 2
    return earlier


def add_entering_kernel(t_ref, y_ref, q_ref, *refs, modes, tp_size):
    states, tables, o_ref = refs[:tp_size], refs[tp_size:-1], refs[-1]
    rows, width = y_ref.shape
    k, chunk = pl.program_id(0), pl.program_id(1)
    sub = lax.broadcasted_iota(jnp.int32, (SUBS, LANES), 0).astype(jnp.float32)
    for c in range(width // LANES):
        lanes = slice(c * LANES, (c + 1) * LANES)
        spot = pl.ds(pl.multiple_of(chunk * width + c * LANES, LANES), LANES)
        rate = pick(k, tables, (slice(0, modes), spot))
        weight = pick(k, tables, (slice(modes, 2 * modes), spot))
        start = pick(k, states, (slice(0, modes), spot)) * weight
        step = jnp.exp(rate * (-1.0 * SUBS))
        terms, steps = [], []
        for n in range(modes):
            fall = jnp.exp((sub + 1.0) * (-rate[n : n + 1]))
            terms.append(fall * start[n : n + 1])
            steps.append(jnp.broadcast_to(step[n : n + 1], (SUBS, LANES)))
        pair = []
        for tile in range(rows // SUBS):
            place = slice(tile * SUBS, (tile + 1) * SUBS)
            total = y_ref[place, lanes]
            parts = list(terms)
            while len(parts) > 1:
                parts = [a + b for a, b in zip(parts[::2], parts[1::2])] + (
                    [parts[-1]] if len(parts) % 2 else []
                )
            pair.append(q_ref[place, lanes] * (total + parts[0]))
            if len(pair) == 2:
                o_ref[(tile - 1) * SUBS : (tile + 1) * SUBS, lanes] = jnp.concatenate(
                    pair, axis=0
                ).astype(o_ref.dtype)
                pair = []
            terms = [a * b for a, b in zip(terms, steps)]


def add_entering(t, y, q, states, tables, modes, width=256):
    rows, channels = y.shape
    tp_size = len(tables)
    quarter = channels // tp_size
    chunks = quarter // width
    whole = lambda k, c, t: (0, 0)
    across = lambda k, c, t: (0, (k ^ t[0]) * chunks + c)
    return pl.pallas_call(
        functools.partial(add_entering_kernel, modes=modes, tp_size=tp_size),
        grid_spec=pltpu.PrefetchScalarGridSpec(
            num_scalar_prefetch=1,
            grid=(tp_size, chunks),
            in_specs=[pl.BlockSpec((rows, width), across)] * 2
            + [pl.BlockSpec((modes, quarter), whole)] * tp_size
            + [pl.BlockSpec(tables[0].shape, whole)] * tp_size,
            out_specs=pl.BlockSpec((rows, width), across),
        ),
        out_shape=jax.ShapeDtypeStruct((rows, channels), jnp.bfloat16),
        compiler_params=params_of(),
        cost_estimate=pl.CostEstimate(
            flops=rows * channels * 36,
            bytes_accessed=rows * channels * 10,
            transcendentals=modes * channels * 9,
        ),
        name="add_entering",
    )(t, y, q, *states, *tables)


def exchange(x, axis):
    return lax.all_to_all(x, axis, split_axis=0, concat_axis=0, tiled=True)


def trade_tp(arrays):
    size = len(arrays)
    return [arrays[0]] + [
        lax.ppermute(arrays[k], "tp", [(i, i ^ k) for i in range(size)]) for k in range(1, size)
    ]


def segment_starts(lengths, tokens):
    order = jnp.arange(lengths.shape[0], dtype=jnp.int32)
    ends = jnp.sum(jnp.where(order[:, None] <= order[None, :], lengths[:, None], 0), axis=0)
    position = jnp.arange(tokens, dtype=jnp.int32)
    passed = jnp.where(ends[None, :] <= position[:, None], ends[None, :], 0)
    return jnp.max(passed, axis=1)


def by_tokens(hyena_in, attn_in, short_taps, decay_rate, residue, lengths):
    rows, kinds, channels = hyena_in.shape
    ctx_size, tp_size = lax.axis_size("ctx"), lax.axis_size("tp")
    devices = ctx_size * tp_size
    taps_count = short_taps.shape[0]
    modes = decay_rate.shape[0]
    t = lax.axis_index("tp").astype(jnp.int32).reshape(1)

    heads_out = split_heads(jnp.transpose(attn_in, (1, 0, 2)))
    by_head = exchange(heads_out, ALL)

    x = jnp.transpose(hyena_in, (1, 0, 2))
    edge = x[:, rows - taps_count + 1 :].reshape(kinds * (taps_count - 1), channels)
    edge = lax.ppermute(edge, ALL, [(i, i + 1) for i in range(devices - 1)]).astype(jnp.float32)
    own_weight = residue * jnp.sqrt(-jnp.expm1(-2.0 * decay_rate))
    flat_taps = short_taps.reshape(taps_count * kinds, -1)
    table = jnp.concatenate([decay_rate, own_weight, flat_taps], axis=0)
    tables = trade_tp([table] * tp_size)
    y, q, *ends = local_conv(t, x, edge, tables, modes, taps_count)
    ends = trade_tp(ends)
    [block_end] = small_call(block_end_kernel, t, "block_end", 1, decay_rate, *ends, rows=rows)
    arriving = scan_ctx(decay_rate, block_end, rows * tp_size)
    states = small_call(
        block_starts_kernel, t, "block_starts", tp_size, decay_rate, arriving, *ends, rows=rows
    )
    hyena_out = add_entering(t, y, q, trade_tp(states), tables, modes)

    mixed = attend(by_head, segment_starts(lengths, rows * devices))
    attn_out = join_heads(exchange(mixed.reshape(devices, rows, DH), ALL))
    return hyena_out, attn_out


exact_mode = lax.Precision.HIGHEST


def from_behind(block, axis, distance):
    devices = range(lax.axis_size(axis))
    route = [(i - distance, i) for i in devices if i - distance in devices]
    return lax.ppermute(block, axis, route)


def carried_in(part, axis, combine, identity):
    place = lax.axis_index(axis)
    gathered = jax.tree.map(lambda a: lax.all_gather(a, axis), part)
    state = jax.tree.map(lambda a, e: jnp.zeros_like(a) + jnp.asarray(e, a.dtype), part, identity)

    def one(lap, state):
        return combine(
            state, jax.tree.map(lambda a: lax.dynamic_index_in_dim(a, lap, 0, False), gathered)
        )

    return lax.fori_loop(0, place, one, state)


def segment_of(positions, segment_ends):
    return jnp.sum((segment_ends[None, :] <= positions[:, None]).astype(jnp.int32), axis=1)


def by_channels(hyena_in, attn_in, short_taps, decay_rate, residue, lengths):
    hyena_cols, attention_cols = (
        lax.all_to_all(hyena_in, "tp", split_axis=2, concat_axis=0, tiled=True),
        lax.all_to_all(attn_in, "tp", split_axis=2, concat_axis=0, tiled=True),
    )
    block_rows = hyena_cols.shape[0]
    rim_rows = short_taps.shape[0] - 1
    edge_rows = from_behind(hyena_cols[block_rows - rim_rows :], "ctx", 1)
    extended = jnp.concatenate([edge_rows, hyena_cols], axis=0).astype(jnp.float32)
    filtered = jnp.zeros(hyena_cols.shape, jnp.float32)
    for lag in range(rim_rows + 1):
        filtered = (
            filtered + short_taps[lag] * extended[rim_rows - lag : rim_rows - lag + block_rows]
        )
    query_side = filtered[:, 0]
    source = filtered[:, 1] * filtered[:, 2]
    channels = source.shape[1]
    weight = residue * jnp.sqrt(-jnp.expm1(-2.0 * decay_rate))
    sub_length = math.gcd(32, block_rows)
    pieces = block_rows // sub_length
    offsets = jnp.arange(sub_length, dtype=jnp.float32)
    powers = jnp.exp(-offsets[:, None, None] * decay_rate[None])
    lag_values = jnp.einsum("onc,nc->oc", powers, weight, precision=exact_mode)
    lag_index = jnp.arange(sub_length, dtype=jnp.int32)
    selector = (
        lag_index[:, None, None] - lag_index[None, :, None] == lag_index[None, None, :]
    ).astype(jnp.float32)
    toeplitz = jnp.einsum("tso,oc->tsc", selector, lag_values, precision=exact_mode)
    grouped = source.reshape(pieces, sub_length, channels)
    inner = jnp.einsum("tsc,bsc->btc", toeplitz, grouped, precision=exact_mode)
    tail_powers = jnp.exp(-(sub_length - 1.0 - offsets)[:, None, None] * decay_rate[None])
    own_states = jnp.einsum("snc,bsc->bnc", tail_powers, grouped, precision=exact_mode)
    sub_decay = jnp.exp(-sub_length * decay_rate)

    def carry_states(carried, incoming):
        return (sub_decay * carried + incoming, carried)

    local_end, entering = lax.scan(carry_states, jnp.zeros_like(sub_decay), own_states)
    block_decay = jnp.exp(-block_rows * decay_rate)

    def combine(earlier, later):
        return (earlier[0] * later[0], later[0] * earlier[1] + later[1])

    _, arriving = carried_in(
        (block_decay, local_end),
        "ctx",
        combine,
        (jnp.ones_like(block_decay), jnp.zeros_like(local_end)),
    )
    starts = jnp.arange(pieces, dtype=jnp.float32) * sub_length
    all_entering = entering + jnp.exp(-starts[:, None, None] * decay_rate[None]) * arriving[None]
    rise_powers = jnp.exp(-(offsets + 1.0)[:, None, None] * decay_rate[None]) * weight[None]
    from_state = jnp.einsum("tnc,bnc->btc", rise_powers, all_entering, precision=exact_mode)
    long_conv = (inner + from_state).reshape(block_rows, channels)
    hyena_local = (query_side * long_conv).astype(jnp.bfloat16)
    head_cols = attention_cols.shape[2]
    local_heads = head_cols // DH
    queries = attention_cols[:, 0].reshape(block_rows, local_heads, DH)
    keyvals = attention_cols[:, 1:3]
    order = jnp.arange(lengths.shape[0], dtype=jnp.int32)
    segment_ends = jnp.sum(jnp.where(order[:, None] <= order[None, :], lengths[:, None], 0), axis=0)
    block_index = lax.axis_index("ctx")
    query_pos = block_index * block_rows + jnp.arange(block_rows, dtype=jnp.int32)
    query_seg = segment_of(query_pos, segment_ends)
    score_scale = 1.0 / math.sqrt(DH)

    def attend_part(softmax_state, part, key_start):
        count = part.shape[0]
        key_pos = key_start + jnp.arange(count, dtype=jnp.int32)
        key_seg = segment_of(key_pos, segment_ends)
        allowed = (
            (key_pos[None, :] <= query_pos[:, None])
            & (key_seg[None, :] == query_seg[:, None])
            & (key_pos >= 0)[None, :]
        )

        def compute(carried):
            row_top, denom, weighted = carried
            key_rows = part[:, 0].reshape(count, local_heads, DH)
            value_rows = part[:, 1].reshape(count, local_heads, DH)
            scores = (
                jnp.einsum("qhd,khd->hqk", queries, key_rows, preferred_element_type=jnp.float32)
                * score_scale
            )
            masked = jnp.where(allowed[None], scores, jnp.float32(-1e30))
            new_top = jnp.maximum(row_top, jnp.max(masked, axis=2))
            expo = jnp.where(allowed[None], jnp.exp(scores - new_top[:, :, None]), jnp.float32(0.0))
            rescale = jnp.exp(row_top - new_top)
            denom = denom * rescale + jnp.sum(expo, axis=2)
            probs = expo.astype(jnp.bfloat16)
            added = jnp.einsum(
                "hqk,khd->qhd", probs, value_rows, preferred_element_type=jnp.float32
            )
            weighted = weighted * jnp.transpose(rescale)[:, :, None] + added
            return (new_top, denom, weighted)

        def keep(carried):
            return carried

        return lax.cond(jnp.any(allowed), compute, keep, softmax_state)

    initial = (
        jnp.full((local_heads, block_rows), -1e30, jnp.float32),
        jnp.zeros((local_heads, block_rows), jnp.float32),
        jnp.zeros((block_rows, local_heads, DH), jnp.float32),
    )
    piece = lax.all_gather(keyvals, "ctx", axis=0, tiled=True)
    rows = piece.shape[0]
    step_rows = math.gcd(rows, 512)

    def advance(count, carried):
        part = lax.dynamic_slice_in_dim(piece, count * step_rows, step_rows, 0)
        return attend_part(carried, part, count * step_rows)

    final_state = lax.fori_loop(0, rows // step_rows, advance, initial)
    _, denom, weighted = final_state
    attention_local = (
        (weighted / jnp.transpose(denom)[:, :, None])
        .reshape(block_rows, head_cols)
        .astype(jnp.bfloat16)
    )
    hyena_out, attn_out = (
        lax.all_to_all(hyena_local, "tp", split_axis=0, concat_axis=1, tiled=True),
        lax.all_to_all(attention_local, "tp", split_axis=0, concat_axis=1, tiled=True),
    )
    return (hyena_out, attn_out)


def per_device(hyena_in, attn_in, short_taps, decay_rate, residue, lengths):
    rows, _, channels = hyena_in.shape
    devices = lax.axis_size("ctx") * lax.axis_size("tp")
    one_head_each = attn_in.shape[2] == devices * DH
    tp_size = lax.axis_size("tp")
    pairs = tp_size & (tp_size - 1) == 0
    whole_tiles = pairs and rows % (2 * SUBS) == 0 and channels % (devices * 2 * LANES) == 0
    plan = by_tokens if one_head_each and whole_tiles else by_channels
    return plan(hyena_in, attn_in, short_taps, decay_rate, residue, lengths)


def solution(mesh):
    placed = (
        P(("ctx", "tp"), None, None),
        P(("ctx", "tp"), None, None),
        P(None, None, "tp"),
        P(None, "tp"),
        P(None, "tp"),
        P(),
    )
    return jax.shard_map(
        per_device,
        mesh=mesh,
        in_specs=placed,
        out_specs=(P(("ctx", "tp"), None), P(("ctx", "tp"), None)),
        check_vma=False,
    )
```

```python
import functools
import math

import jax
import jax.numpy as jnp
from jax import lax
from jax.experimental import pallas as pl
from jax.experimental.pallas import tpu as pltpu
from jax.sharding import PartitionSpec as P

DH = 128
LANES = 128
SUBS = 8
ALL = ("ctx", "tp")
VMEM_BYTES = 60 * 1024 * 1024
ATTEND_BYTES = 32 * 1024 * 1024
MASKED = -1e30


def params_of(limit=VMEM_BYTES):
    return pltpu.CompilerParams(vmem_limit_bytes=limit)


def split_heads_kernel(x_ref, o_ref):
    for h in range(o_ref.shape[0]):
        o_ref[h] = x_ref[:, :, h * DH : (h + 1) * DH]


def split_heads(x, group=4):
    kinds, rows, width = x.shape
    heads = width // DH
    return pl.pallas_call(
        split_heads_kernel,
        grid=(heads // group,),
        in_specs=[pl.BlockSpec((kinds, rows, group * DH), lambda g: (0, 0, g))],
        out_specs=pl.BlockSpec((group, kinds, rows, DH), lambda g: (g, 0, 0, 0)),
        out_shape=jax.ShapeDtypeStruct((heads, kinds, rows, DH), x.dtype),
        compiler_params=params_of(),
        name="split_heads",
    )(x)


def join_heads_kernel(x_ref, o_ref):
    for h in range(x_ref.shape[0]):
        o_ref[:, h * DH : (h + 1) * DH] = x_ref[h]


def join_heads(x, group=8):
    heads, rows, _ = x.shape
    return pl.pallas_call(
        join_heads_kernel,
        grid=(heads // group,),
        in_specs=[pl.BlockSpec((group, rows, DH), lambda g: (g, 0, 0))],
        out_specs=pl.BlockSpec((rows, group * DH), lambda g: (0, g)),
        out_shape=jax.ShapeDtypeStruct((rows, heads * DH), x.dtype),
        compiler_params=params_of(),
        name="join_heads",
    )(x)


def attend_kernel(
    tile_start_ref, x_ref, start_ref, *refs, key_rows, first_tile
):
    o_ref, q_s, k_s, v_s = refs[-4:]
    tile = pl.program_id(0) + first_tile
    blocks, _, rows, _ = x_ref.shape
    query_rows = o_ref.shape[0]
    scale = math.log2(math.e) / math.sqrt(DH)

    @pl.when(tile == first_tile)
    def _():
        @pl.loop(0, blocks)
        def _(b):
            place = pl.ds(pl.multiple_of(b * rows, rows), rows)
            q_s[place] = x_ref[b, 0]
            k_s[place] = x_ref[b, 1]
            v_s[place] = x_ref[b, 2]

    first_row = tile * query_rows
    q = q_s[pl.ds(pl.multiple_of(first_row, query_rows), query_rows)]
    start = start_ref[...]
    start = jnp.concatenate([start] * (key_rows // LANES), axis=1)
    shape = (query_rows, key_rows)
    row = first_row + lax.broadcasted_iota(jnp.int32, shape, 0)
    col = lax.broadcasted_iota(jnp.int32, shape, 1)
    last = (first_row + query_rows - 1) // key_rows
    first = tile_start_ref[tile] // key_rows

    def step(i, carry):
        top, denom, mixed = carry
        base = pl.multiple_of((last - i) * key_rows, key_rows)
        k = k_s[pl.ds(base, key_rows)]
        v = v_s[pl.ds(base, key_rows)]
        s = lax.dot_general(q, k, (((1,), (1,)), ((), ())), preferred_element_type=jnp.float32)
        pos = col + base
        s = jnp.where((pos >= start) & (pos <= row), s, MASKED)
        new_top = jnp.maximum(top, jnp.max(s, axis=1, keepdims=True))
        p = jnp.exp2((s - new_top) * scale)
        rescale = jnp.exp2((top - new_top) * scale)
        denom = denom * rescale + jnp.sum(p, axis=1, keepdims=True)
        mixed = mixed * rescale + jnp.dot(
            p.astype(jnp.bfloat16), v, preferred_element_type=jnp.float32
        )
        return new_top, denom, mixed

    carry = (
        jnp.full((query_rows, 1), MASKED, jnp.float32),
        jnp.zeros((query_rows, 1), jnp.float32),
        jnp.zeros((query_rows, DH), jnp.float32),
    )
    _, denom, mixed = lax.fori_loop(0, last - first + 1, step, carry)
    o_ref[...] = (mixed / denom).astype(o_ref.dtype)


def attend(x, start, wide_start, tiles, before, query_rows, key_rows):
    blocks, _, rows, _ = x.shape
    tokens = blocks * rows
    first_tile, end_tile = tiles
    here = lambda i, s: (i + first_tile, 0)
    old = [] if before is None else [before]
    return pl.pallas_call(
        functools.partial(attend_kernel, key_rows=key_rows, first_tile=first_tile),
        grid_spec=pltpu.PrefetchScalarGridSpec(
            num_scalar_prefetch=1,
            grid=(end_tile - first_tile,),
            in_specs=[
                pl.BlockSpec(x.shape, lambda i, s: (0, 0, 0, 0)),
                pl.BlockSpec((query_rows, LANES), here),
            ]
            + [pl.BlockSpec(memory_space=pl.ANY)] * len(old),
            out_specs=pl.BlockSpec((query_rows, DH), here),
            scratch_shapes=[pltpu.VMEM((tokens, DH), x.dtype)] * 3,
        ),
        out_shape=jax.ShapeDtypeStruct((tokens, DH), x.dtype),
        input_output_aliases={3: 0} if old else {},
        compiler_params=params_of(ATTEND_BYTES),
        cost_estimate=pl.CostEstimate(
            flops=4 * tokens * query_rows * (end_tile - first_tile) * DH,
            bytes_accessed=x.size * 2 + tokens * (DH * 2 + LANES * 4),
            transcendentals=tokens * query_rows * (end_tile - first_tile) // 2,
        ),
        name="attend",
    )(start[::query_rows], x, wide_start, *old)


def pick(k, refs, place):
    value = refs[0][place]
    for other in range(1, len(refs)):
        value = jnp.where(k == other, refs[other][place], value)
    return value


def local_conv_kernel(t_ref, x_ref, edge_ref, *refs, modes, taps_count, tp_size):
    tables, (y_ref, q_ref), ends = refs[: 2 * tp_size], refs[2 * tp_size :][:2], refs[2 * tp_size + 2 : -2]
    xs, out_s = refs[-2:]
    kinds, rows, width = x_ref.shape
    k, chunk = pl.program_id(0), pl.program_id(1)
    run = rows // SUBS
    rim = taps_count - 1
    head = SUBS
    sub = lax.broadcasted_iota(jnp.int32, (SUBS, LANES), 0)

    def wide(row):
        return jnp.broadcast_to(row, (SUBS, LANES))

    for c in range(width // LANES):
        lanes = slice(c * LANES, (c + 1) * LANES)
        spot = pl.ds(pl.multiple_of(chunk * width + c * LANES, LANES), LANES)
        for i in range(kinds):
            xs[i, head - rim : head] = edge_ref[i * rim : (i + 1) * rim, lanes]
            xs[i, head:] = x_ref[i, :, lanes].astype(jnp.float32)
        rate = from_table(k, t_ref[1], tables, 0, (slice(0, modes), spot))
        weight = from_table(k, t_ref[1], tables, 1, (slice(0, modes), spot))
        past = slice(modes, tables[0].shape[0])
        taps = [from_table(k, t_ref[1], tables, half, (past, spot)) for half in (0, 1)]
        cut = half_taps(taps_count * kinds)

        def tap(j, i):
            half, r = divmod(j * kinds + i, cut)
            return wide(taps[half][r : r + 1])

        decay = jnp.exp(-rate)
        decay_run = jnp.exp(rate * (-1.0 * run))

        def at(i, j):
            return xs[i, pl.ds(head + j, SUBS, stride=run)]

        def filtered(i):
            seen = [at(i, j - rim) for j in range(rim)]
            rows_of = [tap(j, i) for j in range(taps_count)]
            out = []
            for j in range(run):
                seen.append(at(i, j))
                out.append(
                    sum(rows_of[lag] * seen[-1 - lag] for lag in range(1, taps_count))
                    + rows_of[0] * seen[-1]
                )
            return out

        for j, value in enumerate(filtered(0)):
            out_s[0, pl.ds(j, SUBS, stride=run)] = value
        q_ref[:, lanes] = out_s[0]
        source = [a * b for a, b in zip(filtered(1), filtered(2))]

        power = weight
        lags = []
        for j in range(run):
            lags.append(wide(jnp.sum(power, axis=0, keepdims=True)))
            power = power * decay
        conv = []
        for j in range(run):
            total = lags[0] * source[j]
            for lag in range(1, j + 1):
                total = total + lags[lag] * source[j - lag]
            conv.append(total)

        last = []
        for n in range(modes):
            d = wide(decay[n : n + 1])
            state = source[0]
            for j in range(1, run):
                state = state * d + source[j]
            span = wide(decay_run[n : n + 1])
            for hop in (1, 2, 4):
                state = state + jnp.where(sub >= hop, span * pltpu.roll(state, hop, 0), 0.0)
                span = span * span
            last.append(state[SUBS - 1 : SUBS])
            entering = jnp.where(sub >= 1, pltpu.roll(state, 1, 0), 0.0) * wide(weight[n : n + 1])
            for j in range(run):
                entering = entering * d
                conv[j] = conv[j] + entering
        last = jnp.concatenate(last, axis=0)
        for other in range(tp_size):

            @pl.when(k == other)
            def _(other=other):
                ends[other][:, spot] = last

        for j in range(run):
            out_s[1, pl.ds(j, SUBS, stride=run)] = conv[j]
        y_ref[:, lanes] = out_s[1]


def local_conv(t, x, edge, tables, modes, taps_count, width=1024):
    kinds, rows, channels = x.shape
    tp_size = len(tables) // 2
    quarter = channels // tp_size
    chunks = quarter // width
    whole = lambda k, c, t: (0, 0)
    across = lambda k, c, t: (0, (k ^ t[0]) * chunks + c)
    return pl.pallas_call(
        functools.partial(
            local_conv_kernel, modes=modes, taps_count=taps_count, tp_size=tp_size
        ),
        grid_spec=pltpu.PrefetchScalarGridSpec(
            num_scalar_prefetch=1,
            grid=(tp_size, chunks),
            in_specs=[
                pl.BlockSpec((kinds, rows, width), lambda k, c, t: (0, *across(k, c, t))),
                pl.BlockSpec((edge.shape[0], width), across),
            ]
            + [pl.BlockSpec(tables[0].shape, whole)] * len(tables),
            out_specs=[pl.BlockSpec((rows, width), across)] * 2
            + [pl.BlockSpec((modes, quarter), whole)] * tp_size,
            scratch_shapes=[
                pltpu.VMEM((kinds, rows + SUBS, LANES), jnp.float32),
                pltpu.VMEM((2, rows, LANES), jnp.float32),
            ],
        ),
        out_shape=[jax.ShapeDtypeStruct((rows, channels), jnp.float32)] * 2
        + [jax.ShapeDtypeStruct((modes, quarter), jnp.float32)] * tp_size,
        compiler_params=params_of(),
        cost_estimate=pl.CostEstimate(
            flops=rows * channels * 100,
            bytes_accessed=rows * channels * 14,
            transcendentals=2 * modes * channels,
        ),
        name="local_conv",
    )(t, x, edge, *tables)


def half_taps(taps_rows):
    return (taps_rows + 1) // 2


def half_rows(modes, taps_rows):
    return -(-(modes + half_taps(taps_rows)) // SUBS) * SUBS


def table_kernel(parity_ref, taps_ref, rate_ref, residue_ref, mine_ref, other_ref):
    lags, kinds, _ = taps_ref.shape
    modes = rate_ref.shape[0]
    rate = rate_ref[...]
    x = 2.0 * rate
    series = jnp.ones_like(x)
    for term in range(10, 1, -1):
        series = 1.0 - series * x * (1.0 / term)
    lost = jnp.where(x < 0.5, x * series, 1.0 - jnp.exp(-x))
    weight = residue_ref[...] * jnp.sqrt(lost)
    rows = [taps_ref[r // kinds, r % kinds : r % kinds + 1] for r in range(lags * kinds)]
    cut = half_taps(len(rows))

    def fill(lower_ref, upper_ref):
        lower_ref[0:modes] = rate
        upper_ref[0:modes] = weight
        for r, row in enumerate(rows):
            ref, place = (lower_ref, r) if r < cut else (upper_ref, r - cut)
            ref[modes + place : modes + place + 1] = row
        for ref, used in ((lower_ref, modes + cut), (upper_ref, modes + len(rows) - cut)):
            ref[used:] = jnp.zeros((ref.shape[0] - used, ref.shape[1]), jnp.float32)

    @pl.when(parity_ref[0] == 0)
    def _():
        fill(mine_ref, other_ref)

    @pl.when(parity_ref[0] == 1)
    def _():
        fill(other_ref, mine_ref)


def make_table(parity, taps, rate, residue):
    height = half_rows(rate.shape[0], taps.shape[0] * taps.shape[1])
    vmem = pl.BlockSpec(memory_space=pltpu.VMEM)
    return pl.pallas_call(
        table_kernel,
        in_specs=[pl.BlockSpec(memory_space=pltpu.SMEM)] + [vmem] * 3,
        out_specs=[vmem] * 2,
        out_shape=[jax.ShapeDtypeStruct((height, rate.shape[1]), jnp.float32)] * 2,
        compiler_params=params_of(),
        name="make_table",
    )(parity, taps, rate, residue)


def from_table(k, parity, tables, half, place):
    size = len(tables) // 2
    ordered = [
        jnp.where(parity == half, tables[i][place], tables[size + i][place]) for i in range(size)
    ]
    value = ordered[0]
    for other in range(1, size):
        value = jnp.where(k == other, ordered[other], value)
    return value


def block_end_kernel(t_ref, rate_ref, *refs, rows):
    ends, o_ref = refs[:-1], refs[-1]
    rate = rate_ref[...]
    total = jnp.zeros_like(rate)
    for k, end in enumerate(ends):
        later = len(ends) - 1 - (k ^ t_ref[0])
        total = total + jnp.exp(rate * (later * -rows).astype(jnp.float32)) * end[...]
    o_ref[...] = total


def block_starts_kernel(t_ref, rate_ref, enter_ref, *refs, rows):
    size = len(refs) // 2
    ends, outs = refs[:size], refs[size:]
    rate = rate_ref[...]
    span = jnp.exp(rate * (-1.0 * rows))
    t = t_ref[0]
    state = enter_ref[...]
    for place in range(size):
        mine = place ^ t
        for k in range(size):

            @pl.when(mine == k)
            def _(k=k, state=state):
                outs[k][...] = state

        end = pick(mine, ends, Ellipsis)
        state = state * span + end


def small_call(kernel, t, name, outs, *arrays, **sizes):
    shape = jax.ShapeDtypeStruct(arrays[0].shape, jnp.float32)
    vmem = pl.BlockSpec(memory_space=pltpu.VMEM)
    result = pl.pallas_call(
        functools.partial(kernel, **sizes),
        in_specs=[pl.BlockSpec(memory_space=pltpu.SMEM)] + [vmem] * len(arrays),
        out_specs=[vmem] * outs,
        out_shape=[shape] * outs,
        compiler_params=params_of(),
        name=name,
    )(t, *arrays)
    return result


def pair_kernel(parity_ref, rate_ref, own_ref, mate_ref, total_ref, *, rows):
    odd = parity_ref[0] == 1
    own, mate = own_ref[...], mate_ref[...]
    first, second = jnp.where(odd, mate, own), jnp.where(odd, own, mate)
    total_ref[...] = first * jnp.exp(rate_ref[...] * (-1.0 * rows)) + second


def add_entering_kernel(t_ref, y_ref, q_ref, *refs, modes, tp_size):
    states, tables, o_ref = refs[:tp_size], refs[tp_size:-1], refs[-1]
    rows, width = y_ref.shape
    k, chunk = pl.program_id(0), pl.program_id(1)
    sub = lax.broadcasted_iota(jnp.int32, (SUBS, LANES), 0).astype(jnp.float32)
    for c in range(width // LANES):
        lanes = slice(c * LANES, (c + 1) * LANES)
        spot = pl.ds(pl.multiple_of(chunk * width + c * LANES, LANES), LANES)
        rate = from_table(k, t_ref[1], tables, 0, (slice(0, modes), spot))
        weight = from_table(k, t_ref[1], tables, 1, (slice(0, modes), spot))
        start = pick(k, states, (slice(0, modes), spot)) * weight
        step = jnp.exp(rate * (-1.0 * SUBS))
        terms, steps = [], []
        for n in range(modes):
            fall = jnp.exp((sub + 1.0) * (-rate[n : n + 1]))
            terms.append(fall * start[n : n + 1])
            steps.append(jnp.broadcast_to(step[n : n + 1], (SUBS, LANES)))
        pair = []
        for tile in range(rows // SUBS):
            place = slice(tile * SUBS, (tile + 1) * SUBS)
            total = y_ref[place, lanes]
            parts = list(terms)
            while len(parts) > 1:
                parts = [a + b for a, b in zip(parts[::2], parts[1::2])] + (
                    [parts[-1]] if len(parts) % 2 else []
                )
            pair.append(q_ref[place, lanes] * (total + parts[0]))
            if len(pair) == 2:
                o_ref[(tile - 1) * SUBS : (tile + 1) * SUBS, lanes] = jnp.concatenate(
                    pair, axis=0
                ).astype(o_ref.dtype)
                pair = []
            terms = [a * b for a, b in zip(terms, steps)]


def add_entering(t, y, q, states, tables, modes, width=1024):
    rows, channels = y.shape
    tp_size = len(tables) // 2
    quarter = channels // tp_size
    chunks = quarter // width
    whole = lambda k, c, t: (0, 0)
    across = lambda k, c, t: (0, (k ^ t[0]) * chunks + c)
    return pl.pallas_call(
        functools.partial(add_entering_kernel, modes=modes, tp_size=tp_size),
        grid_spec=pltpu.PrefetchScalarGridSpec(
            num_scalar_prefetch=1,
            grid=(tp_size, chunks),
            in_specs=[pl.BlockSpec((rows, width), across)] * 2
            + [pl.BlockSpec((modes, quarter), whole)] * tp_size
            + [pl.BlockSpec(tables[0].shape, whole)] * len(tables),
            out_specs=pl.BlockSpec((rows, width), across),
        ),
        out_shape=jax.ShapeDtypeStruct((rows, channels), jnp.bfloat16),
        compiler_params=params_of(),
        cost_estimate=pl.CostEstimate(
            flops=rows * channels * 36,
            bytes_accessed=rows * channels * 10,
            transcendentals=modes * channels * 9,
        ),
        name="add_entering",
    )(t, y, q, *states, *tables)


def exchange(x, axis):
    return lax.all_to_all(x, axis, split_axis=0, concat_axis=0, tiled=True)


def trade_tp(arrays):
    size = len(arrays)
    return [arrays[0]] + [
        lax.ppermute(arrays[k], "tp", [(i, i ^ k) for i in range(size)]) for k in range(1, size)
    ]


def segment_starts(lengths, tokens):
    order = jnp.arange(lengths.shape[0], dtype=jnp.int32)
    ends = jnp.sum(jnp.where(order[:, None] <= order[None, :], lengths[:, None], 0), axis=0)
    position = jnp.arange(tokens, dtype=jnp.int32)
    passed = jnp.where(ends[None, :] <= position[:, None], ends[None, :], 0)
    return jnp.max(passed, axis=1)


def by_tokens(hyena_in, attn_in, short_taps, decay_rate, residue, lengths):
    rows, kinds, channels = hyena_in.shape
    ctx_size, tp_size = lax.axis_size("ctx"), lax.axis_size("tp")
    devices = ctx_size * tp_size
    taps_count = short_taps.shape[0]
    modes = decay_rate.shape[0]
    parity = (lax.axis_index("ctx") % 2).astype(jnp.int32)
    t = jnp.stack([lax.axis_index("tp").astype(jnp.int32), parity])
    swap = [(i, i ^ 1) for i in range(ctx_size)]

    x = jnp.transpose(hyena_in, (1, 0, 2))
    edge = x[:, rows - taps_count + 1 :].reshape(kinds * (taps_count - 1), channels)
    edge, decay_rate = lax.optimization_barrier((edge, decay_rate))
    edge = lax.ppermute(edge, ALL, [(i, i + 1) for i in range(devices - 1)])
    mine, other = make_table(parity.reshape(1), short_taps, decay_rate, residue)
    mine = trade_tp([mine] * tp_size)
    heads_out = split_heads(jnp.transpose(attn_in, (1, 0, 2)))
    heads_out, edge, *mine = lax.optimization_barrier((heads_out, edge, *mine))
    by_head = exchange(heads_out, ALL)
    edge = edge.astype(jnp.float32)
    tables = mine + [other] + [lax.ppermute(half, "ctx", swap) for half in mine[1:]]
    y, q, *ends = local_conv(t, x, edge, tables, modes, taps_count)
    ends = trade_tp(ends)
    [block_end] = small_call(block_end_kernel, t, "block_end", 1, decay_rate, *ends, rows=rows)

    block_rows = rows * tp_size
    mate = lax.ppermute(block_end, "ctx", swap)
    [held] = small_call(
        pair_kernel, parity.reshape(1), "pair", 1, decay_rate, block_end, mate, rows=block_rows
    )
    distances = []
    while 2 << len(distances) < ctx_size:
        distances.append(2 << len(distances))

    start = segment_starts(lengths, rows * devices)
    wide_start = jnp.broadcast_to(start[:, None], (rows * devices, LANES))
    query_rows = math.gcd(rows * devices, 512)
    count = rows * devices // query_rows
    cut = count * 2 // 3
    earlier, mixed = None, None
    for distance in distances:
        if distance == distances[-1]:
            by_head, held = lax.optimization_barrier((by_head, held))
            mixed = attend(by_head, start, wide_start, (0, cut), None, query_rows, query_rows)
        seen = lax.ppermute(held, "ctx", [(i, i + distance) for i in range(ctx_size - distance)])
        if earlier is None:
            earlier = seen
        else:
            earlier = earlier + jnp.exp(decay_rate * (-1.0 * block_rows * (distance - 2))) * seen
        held = held + jnp.exp(decay_rate * (-1.0 * block_rows * distance)) * seen
    arriving = jnp.where(
        parity == 1, earlier * jnp.exp(decay_rate * (-1.0 * block_rows)) + mate, earlier
    )
    states = small_call(
        block_starts_kernel, t, "block_starts", tp_size, decay_rate, arriving, *ends, rows=rows
    )
    mixed, *states = lax.optimization_barrier((mixed, *states))
    mixed = attend(by_head, start, wide_start, (cut, count), mixed, query_rows, query_rows)
    mixed, *states = lax.optimization_barrier((mixed, *trade_tp(states)))
    attn_out = join_heads(exchange(mixed.reshape(devices, rows, DH), ALL))
    hyena_out = add_entering(t, y, q, states, tables, modes)
    return hyena_out, attn_out


exact_mode = lax.Precision.HIGHEST


def from_behind(block, axis, distance):
    devices = range(lax.axis_size(axis))
    route = [(i - distance, i) for i in devices if i - distance in devices]
    return lax.ppermute(block, axis, route)


def carried_in(part, axis, combine, identity):
    place = lax.axis_index(axis)
    gathered = jax.tree.map(lambda a: lax.all_gather(a, axis), part)
    state = jax.tree.map(lambda a, e: jnp.zeros_like(a) + jnp.asarray(e, a.dtype), part, identity)

    def one(lap, state):
        return combine(
            state, jax.tree.map(lambda a: lax.dynamic_index_in_dim(a, lap, 0, False), gathered)
        )

    return lax.fori_loop(0, place, one, state)


def segment_of(positions, segment_ends):
    return jnp.sum((segment_ends[None, :] <= positions[:, None]).astype(jnp.int32), axis=1)


def by_channels(hyena_in, attn_in, short_taps, decay_rate, residue, lengths):
    hyena_cols, attention_cols = (
        lax.all_to_all(hyena_in, "tp", split_axis=2, concat_axis=0, tiled=True),
        lax.all_to_all(attn_in, "tp", split_axis=2, concat_axis=0, tiled=True),
    )
    block_rows = hyena_cols.shape[0]
    rim_rows = short_taps.shape[0] - 1
    edge_rows = from_behind(hyena_cols[block_rows - rim_rows :], "ctx", 1)
    extended = jnp.concatenate([edge_rows, hyena_cols], axis=0).astype(jnp.float32)
    filtered = jnp.zeros(hyena_cols.shape, jnp.float32)
    for lag in range(rim_rows + 1):
        filtered = (
            filtered + short_taps[lag] * extended[rim_rows - lag : rim_rows - lag + block_rows]
        )
    query_side = filtered[:, 0]
    source = filtered[:, 1] * filtered[:, 2]
    channels = source.shape[1]
    weight = residue * jnp.sqrt(-jnp.expm1(-2.0 * decay_rate))
    sub_length = math.gcd(32, block_rows)
    pieces = block_rows // sub_length
    offsets = jnp.arange(sub_length, dtype=jnp.float32)
    powers = jnp.exp(-offsets[:, None, None] * decay_rate[None])
    lag_values = jnp.einsum("onc,nc->oc", powers, weight, precision=exact_mode)
    lag_index = jnp.arange(sub_length, dtype=jnp.int32)
    selector = (
        lag_index[:, None, None] - lag_index[None, :, None] == lag_index[None, None, :]
    ).astype(jnp.float32)
    toeplitz = jnp.einsum("tso,oc->tsc", selector, lag_values, precision=exact_mode)
    grouped = source.reshape(pieces, sub_length, channels)
    inner = jnp.einsum("tsc,bsc->btc", toeplitz, grouped, precision=exact_mode)
    tail_powers = jnp.exp(-(sub_length - 1.0 - offsets)[:, None, None] * decay_rate[None])
    own_states = jnp.einsum("snc,bsc->bnc", tail_powers, grouped, precision=exact_mode)
    sub_decay = jnp.exp(-sub_length * decay_rate)

    def carry_states(carried, incoming):
        return (sub_decay * carried + incoming, carried)

    local_end, entering = lax.scan(carry_states, jnp.zeros_like(sub_decay), own_states)
    block_decay = jnp.exp(-block_rows * decay_rate)

    def combine(earlier, later):
        return (earlier[0] * later[0], later[0] * earlier[1] + later[1])

    _, arriving = carried_in(
        (block_decay, local_end),
        "ctx",
        combine,
        (jnp.ones_like(block_decay), jnp.zeros_like(local_end)),
    )
    starts = jnp.arange(pieces, dtype=jnp.float32) * sub_length
    all_entering = entering + jnp.exp(-starts[:, None, None] * decay_rate[None]) * arriving[None]
    rise_powers = jnp.exp(-(offsets + 1.0)[:, None, None] * decay_rate[None]) * weight[None]
    from_state = jnp.einsum("tnc,bnc->btc", rise_powers, all_entering, precision=exact_mode)
    long_conv = (inner + from_state).reshape(block_rows, channels)
    hyena_local = (query_side * long_conv).astype(jnp.bfloat16)
    head_cols = attention_cols.shape[2]
    local_heads = head_cols // DH
    queries = attention_cols[:, 0].reshape(block_rows, local_heads, DH)
    keyvals = attention_cols[:, 1:3]
    order = jnp.arange(lengths.shape[0], dtype=jnp.int32)
    segment_ends = jnp.sum(jnp.where(order[:, None] <= order[None, :], lengths[:, None], 0), axis=0)
    block_index = lax.axis_index("ctx")
    query_pos = block_index * block_rows + jnp.arange(block_rows, dtype=jnp.int32)
    query_seg = segment_of(query_pos, segment_ends)
    score_scale = 1.0 / math.sqrt(DH)

    def attend_part(softmax_state, part, key_start):
        count = part.shape[0]
        key_pos = key_start + jnp.arange(count, dtype=jnp.int32)
        key_seg = segment_of(key_pos, segment_ends)
        allowed = (
            (key_pos[None, :] <= query_pos[:, None])
            & (key_seg[None, :] == query_seg[:, None])
            & (key_pos >= 0)[None, :]
        )

        def compute(carried):
            row_top, denom, weighted = carried
            key_rows = part[:, 0].reshape(count, local_heads, DH)
            value_rows = part[:, 1].reshape(count, local_heads, DH)
            scores = (
                jnp.einsum("qhd,khd->hqk", queries, key_rows, preferred_element_type=jnp.float32)
                * score_scale
            )
            masked = jnp.where(allowed[None], scores, jnp.float32(-1e30))
            new_top = jnp.maximum(row_top, jnp.max(masked, axis=2))
            expo = jnp.where(allowed[None], jnp.exp(scores - new_top[:, :, None]), jnp.float32(0.0))
            rescale = jnp.exp(row_top - new_top)
            denom = denom * rescale + jnp.sum(expo, axis=2)
            probs = expo.astype(jnp.bfloat16)
            added = jnp.einsum(
                "hqk,khd->qhd", probs, value_rows, preferred_element_type=jnp.float32
            )
            weighted = weighted * jnp.transpose(rescale)[:, :, None] + added
            return (new_top, denom, weighted)

        def keep(carried):
            return carried

        return lax.cond(jnp.any(allowed), compute, keep, softmax_state)

    initial = (
        jnp.full((local_heads, block_rows), -1e30, jnp.float32),
        jnp.zeros((local_heads, block_rows), jnp.float32),
        jnp.zeros((block_rows, local_heads, DH), jnp.float32),
    )
    piece = lax.all_gather(keyvals, "ctx", axis=0, tiled=True)
    rows = piece.shape[0]
    step_rows = math.gcd(rows, 512)

    def advance(count, carried):
        part = lax.dynamic_slice_in_dim(piece, count * step_rows, step_rows, 0)
        return attend_part(carried, part, count * step_rows)

    final_state = lax.fori_loop(0, rows // step_rows, advance, initial)
    _, denom, weighted = final_state
    attention_local = (
        (weighted / jnp.transpose(denom)[:, :, None])
        .reshape(block_rows, head_cols)
        .astype(jnp.bfloat16)
    )
    hyena_out, attn_out = (
        lax.all_to_all(hyena_local, "tp", split_axis=0, concat_axis=1, tiled=True),
        lax.all_to_all(attention_local, "tp", split_axis=0, concat_axis=1, tiled=True),
    )
    return (hyena_out, attn_out)


def per_device(hyena_in, attn_in, short_taps, decay_rate, residue, lengths):
    rows, _, channels = hyena_in.shape
    devices = lax.axis_size("ctx") * lax.axis_size("tp")
    one_head_each = attn_in.shape[2] == devices * DH
    tp_size = lax.axis_size("tp")
    pairs = tp_size & (tp_size - 1) == 0
    pairs = pairs and lax.axis_size("ctx") >= 4 and lax.axis_size("ctx") % 2 == 0
    whole_tiles = pairs and rows % (2 * SUBS) == 0 and channels % (tp_size * 1024) == 0
    plan = by_tokens if one_head_each and whole_tiles else by_channels
    return plan(hyena_in, attn_in, short_taps, decay_rate, residue, lengths)


def solution(mesh):
    placed = (
        P(("ctx", "tp"), None, None),
        P(("ctx", "tp"), None, None),
        P(None, None, "tp"),
        P(None, "tp"),
        P(None, "tp"),
        P(),
    )
    return jax.shard_map(
        per_device,
        mesh=mesh,
        in_specs=placed,
        out_specs=(P(("ctx", "tp"), None), P(("ctx", "tp"), None)),
        check_vma=False,
    )
```

```python
import functools
import math

import jax
import jax.numpy as jnp
from jax import lax
from jax.experimental import pallas as pl
from jax.experimental.pallas import tpu as pltpu
from jax.sharding import PartitionSpec as P

DH = 128
LANES = 128
SUBS = 8
ALL = ("ctx", "tp")
VMEM_BYTES = 60 * 1024 * 1024
ATTEND_BYTES = 32 * 1024 * 1024
MASKED = -1e30


def params_of(limit=VMEM_BYTES):
    return pltpu.CompilerParams(vmem_limit_bytes=limit)


def split_heads_kernel(x_ref, o_ref):
    for h in range(o_ref.shape[0]):
        o_ref[h] = x_ref[:, :, h * DH : (h + 1) * DH]


def split_heads(x, group=8):
    kinds, rows, width = x.shape
    heads = width // DH
    return pl.pallas_call(
        split_heads_kernel,
        grid=(heads // group,),
        in_specs=[pl.BlockSpec((kinds, rows, group * DH), lambda g: (0, 0, g))],
        out_specs=pl.BlockSpec((group, kinds, rows, DH), lambda g: (g, 0, 0, 0)),
        out_shape=jax.ShapeDtypeStruct((heads, kinds, rows, DH), x.dtype),
        compiler_params=params_of(),
        name="split_heads",
    )(x)


def join_heads_kernel(x_ref, o_ref):
    for h in range(x_ref.shape[0]):
        o_ref[:, h * DH : (h + 1) * DH] = x_ref[h]


def join_heads(x, group=8):
    heads, rows, _ = x.shape
    return pl.pallas_call(
        join_heads_kernel,
        grid=(heads // group,),
        in_specs=[pl.BlockSpec((group, rows, DH), lambda g: (g, 0, 0))],
        out_specs=pl.BlockSpec((rows, group * DH), lambda g: (0, g)),
        out_shape=jax.ShapeDtypeStruct((rows, heads * DH), x.dtype),
        compiler_params=params_of(ATTEND_BYTES),
        name="join_heads",
    )(x)


def attend_kernel(tile_start_ref, x_ref, start_ref, o_ref, q_s, k_s, v_s, *, key_rows):
    tile = pl.program_id(0)
    blocks, _, rows, _ = x_ref.shape
    query_rows = o_ref.shape[0]
    scale = math.log2(math.e) / math.sqrt(DH)

    @pl.when(tile == 0)
    def _():
        @pl.loop(0, blocks)
        def _(b):
            place = pl.ds(pl.multiple_of(b * rows, rows), rows)
            q_s[place] = x_ref[b, 0]
            k_s[place] = x_ref[b, 1]
            v_s[place] = x_ref[b, 2]

    first_row = tile * query_rows
    q = q_s[pl.ds(pl.multiple_of(first_row, query_rows), query_rows)]
    start = start_ref[...]
    start = jnp.concatenate([start] * (key_rows // LANES), axis=1)
    shape = (query_rows, key_rows)
    row = first_row + lax.broadcasted_iota(jnp.int32, shape, 0)
    col = lax.broadcasted_iota(jnp.int32, shape, 1)
    last = (first_row + query_rows - 1) // key_rows
    first = tile_start_ref[tile] // key_rows

    def step(i, carry):
        top, denom, mixed = carry
        base = pl.multiple_of((last - i) * key_rows, key_rows)
        k = k_s[pl.ds(base, key_rows)]
        v = v_s[pl.ds(base, key_rows)]
        s = lax.dot_general(q, k, (((1,), (1,)), ((), ())), preferred_element_type=jnp.float32)
        pos = col + base
        s = jnp.where((pos >= start) & (pos <= row), s, MASKED)
        new_top = jnp.maximum(top, jnp.max(s, axis=1, keepdims=True))
        p = jnp.exp2((s - new_top) * scale)
        rescale = jnp.exp2((top - new_top) * scale)
        denom = denom * rescale + jnp.sum(p, axis=1, keepdims=True)
        mixed = mixed * rescale + jnp.dot(
            p.astype(jnp.bfloat16), v, preferred_element_type=jnp.float32
        )
        return new_top, denom, mixed

    carry = (
        jnp.full((query_rows, 1), MASKED, jnp.float32),
        jnp.zeros((query_rows, 1), jnp.float32),
        jnp.zeros((query_rows, DH), jnp.float32),
    )
    _, denom, mixed = lax.fori_loop(0, last - first + 1, step, carry)
    o_ref[...] = (mixed / denom).astype(o_ref.dtype)


def attend(x, start, query_rows=512, key_rows=512):
    blocks, _, rows, _ = x.shape
    tokens = blocks * rows
    query_rows, key_rows = math.gcd(tokens, query_rows), math.gcd(tokens, key_rows)
    wide_start = jnp.broadcast_to(start[:, None], (tokens, LANES))
    return pl.pallas_call(
        functools.partial(attend_kernel, key_rows=key_rows),
        grid_spec=pltpu.PrefetchScalarGridSpec(
            num_scalar_prefetch=1,
            grid=(tokens // query_rows,),
            in_specs=[
                pl.BlockSpec(x.shape, lambda t, s: (0, 0, 0, 0)),
                pl.BlockSpec((query_rows, LANES), lambda t, s: (t, 0)),
            ],
            out_specs=pl.BlockSpec((query_rows, DH), lambda t, s: (t, 0)),
            scratch_shapes=[pltpu.VMEM((tokens, DH), x.dtype)] * 3,
        ),
        out_shape=jax.ShapeDtypeStruct((tokens, DH), x.dtype),
        compiler_params=params_of(ATTEND_BYTES),
        cost_estimate=pl.CostEstimate(
            flops=2 * tokens * tokens * DH,
            bytes_accessed=x.size * 2 + tokens * (DH * 2 + LANES * 4),
            transcendentals=tokens * tokens // 2,
        ),
        name="attend",
    )(start[::query_rows], x, wide_start)


def pick(k, refs, place):
    value = refs[0][place]
    for other in range(1, len(refs)):
        value = jnp.where(k == other, refs[other][place], value)
    return value


def wide(row):
    return jnp.broadcast_to(row, (SUBS, LANES))


def added(parts):
    while len(parts) > 1:
        parts = [a + b for a, b in zip(parts[::2], parts[1::2])] + (
            [parts[-1]] if len(parts) % 2 else []
        )
    return parts[0]


def filtered_runs(xs, i, taps, run):
    rim = len(taps) - 1
    seen = [xs[i, pl.ds(SUBS + j - rim, SUBS, stride=run)] for j in range(rim)]
    out = []
    for j in range(run):
        seen.append(xs[i, pl.ds(SUBS + j, SUBS, stride=run)])
        out.append(sum(taps[lag] * seen[-1 - lag] for lag in range(1, rim + 1)) + taps[0] * seen[-1])
    return out


def taps_of(k, parity, tables, modes, taps_count, kinds, spot):
    past = slice(modes, tables[0].shape[0])
    halves = [from_table(k, parity, tables, half, (past, spot)) for half in (0, 1)]
    cut = half_taps(taps_count * kinds)

    def tap(lag, i):
        half, r = divmod(lag * kinds + i, cut)
        return wide(halves[half][r : r + 1])

    return lambda i: [tap(lag, i) for lag in range(taps_count)]


def block_states_kernel(t_ref, x_ref, edge_ref, *refs, modes, taps_count, tp_size):
    tables, (source_ref, enter_ref) = refs[: 2 * tp_size], refs[2 * tp_size :][:2]
    ends, xs = refs[2 * tp_size + 2 : -1], refs[-1]
    kinds, rows, width = x_ref.shape
    k, chunk = pl.program_id(0), pl.program_id(1)
    run = rows // SUBS
    rim = taps_count - 1
    sub = lax.broadcasted_iota(jnp.int32, (SUBS, LANES), 0)
    for c in range(width // LANES):
        lanes = slice(c * LANES, (c + 1) * LANES)
        spot = pl.ds(pl.multiple_of(chunk * width + c * LANES, LANES), LANES)
        for i in (1, 2):
            xs[i, SUBS - rim : SUBS] = edge_ref[i * rim : (i + 1) * rim, lanes]
            xs[i, SUBS:] = x_ref[i, :, lanes].astype(jnp.float32)
        rate = from_table(k, t_ref[1], tables, 0, (slice(0, modes), spot))
        taps = taps_of(k, t_ref[1], tables, modes, taps_count, kinds, spot)
        decay = jnp.exp(-rate)
        decay_run = jnp.exp(rate * (-1.0 * run))
        source = [
            a * b
            for a, b in zip(filtered_runs(xs, 1, taps(1), run), filtered_runs(xs, 2, taps(2), run))
        ]
        for j in range(run):
            source_ref[j * SUBS : (j + 1) * SUBS, lanes] = source[j]

        last = []
        for n in range(modes):
            d = wide(decay[n : n + 1])
            state = source[0]
            for j in range(1, run):
                state = state * d + source[j]
            span = wide(decay_run[n : n + 1])
            for hop in (1, 2, 4):
                state = state + jnp.where(sub >= hop, span * pltpu.roll(state, hop, 0), 0.0)
                span = span * span
            last.append(state[SUBS - 1 : SUBS])
            enter_ref[n * SUBS : (n + 1) * SUBS, lanes] = jnp.where(
                sub >= 1, pltpu.roll(state, 1, 0), 0.0
            )
        last = jnp.concatenate(last, axis=0)
        for other in range(tp_size):

            @pl.when(k == other)
            def _(other=other):
                ends[other][:, spot] = last


def inside_runs_kernel(t_ref, x_ref, edge_ref, source_ref, enter_ref, *refs, modes, taps_count, tp_size):
    tables, y_ref, q_ref, xs = refs[: 2 * tp_size], refs[-3], refs[-2], refs[-1]
    _, rows, width = x_ref.shape
    kinds = edge_ref.shape[0] // (taps_count - 1)
    k, chunk = pl.program_id(0), pl.program_id(1)
    run = rows // SUBS
    rim = taps_count - 1
    for c in range(width // LANES):
        lanes = slice(c * LANES, (c + 1) * LANES)
        spot = pl.ds(pl.multiple_of(chunk * width + c * LANES, LANES), LANES)
        xs[0, SUBS - rim : SUBS] = edge_ref[0:rim, lanes]
        xs[0, SUBS:] = x_ref[0, :, lanes].astype(jnp.float32)
        rate = from_table(k, t_ref[1], tables, 0, (slice(0, modes), spot))
        weight = from_table(k, t_ref[1], tables, 1, (slice(0, modes), spot))
        taps = taps_of(k, t_ref[1], tables, modes, taps_count, kinds, spot)
        for j, value in enumerate(filtered_runs(xs, 0, taps(0), run)):
            q_ref[j * SUBS : (j + 1) * SUBS, lanes] = value
        decay = jnp.exp(-rate)
        power = weight
        lags = []
        for j in range(run):
            lags.append(wide(jnp.sum(power, axis=0, keepdims=True)))
            power = power * decay
        source = [source_ref[j * SUBS : (j + 1) * SUBS, lanes] for j in range(run)]
        weight = weight * decay
        terms = [
            enter_ref[n * SUBS : (n + 1) * SUBS, lanes] * wide(weight[n : n + 1])
            for n in range(modes)
        ]
        steps = [wide(decay[n : n + 1]) for n in range(modes)]
        for j in range(run):
            total = added(terms)
            for lag in range(j + 1):
                total = total + lags[lag] * source[j - lag]
            y_ref[j * SUBS : (j + 1) * SUBS, lanes] = total
            terms = [a * b for a, b in zip(terms, steps)]


def quarter_grid(tables, channels, width):
    tp_size = len(tables) // 2
    quarter = channels // tp_size
    chunks = quarter // width
    whole = lambda k, c, t: (0, 0)
    across = lambda k, c, t: (0, (k ^ t[0]) * chunks + c)
    return tp_size, quarter, (tp_size, chunks), whole, across


def block_states(t, x, edge, tables, modes, taps_count, width=1024):
    kinds, rows, channels = x.shape
    tp_size, quarter, grid, whole, across = quarter_grid(tables, channels, width)
    return pl.pallas_call(
        functools.partial(
            block_states_kernel, modes=modes, taps_count=taps_count, tp_size=tp_size
        ),
        grid_spec=pltpu.PrefetchScalarGridSpec(
            num_scalar_prefetch=1,
            grid=grid,
            in_specs=[
                pl.BlockSpec((kinds, rows, width), lambda k, c, t: (0, *across(k, c, t))),
                pl.BlockSpec((edge.shape[0], width), across),
            ]
            + [pl.BlockSpec(tables[0].shape, whole)] * len(tables),
            out_specs=[pl.BlockSpec((rows, width), across), pl.BlockSpec((modes * SUBS, width), across)]
            + [pl.BlockSpec((modes, quarter), whole)] * tp_size,
            scratch_shapes=[pltpu.VMEM((kinds, rows + SUBS, LANES), jnp.float32)],
        ),
        out_shape=[
            jax.ShapeDtypeStruct((rows, channels), jnp.float32),
            jax.ShapeDtypeStruct((modes * SUBS, channels), jnp.float32),
        ]
        + [jax.ShapeDtypeStruct((modes, quarter), jnp.float32)] * tp_size,
        compiler_params=params_of(),
        cost_estimate=pl.CostEstimate(
            flops=rows * channels * 50,
            bytes_accessed=rows * channels * 14,
            transcendentals=2 * modes * channels,
        ),
        name="block_states",
    )(t, x, edge, *tables)


def inside_runs(t, x, edge, source, enter, tables, modes, taps_count, width=1024):
    _, rows, channels = x.shape
    tp_size, _, grid, whole, across = quarter_grid(tables, channels, width)
    return pl.pallas_call(
        functools.partial(inside_runs_kernel, modes=modes, taps_count=taps_count, tp_size=tp_size),
        grid_spec=pltpu.PrefetchScalarGridSpec(
            num_scalar_prefetch=1,
            grid=grid,
            in_specs=[
                pl.BlockSpec((1, rows, width), lambda k, c, t: (0, *across(k, c, t))),
                pl.BlockSpec((edge.shape[0], width), across),
                pl.BlockSpec((rows, width), across),
                pl.BlockSpec((enter.shape[0], width), across),
            ]
            + [pl.BlockSpec(tables[0].shape, whole)] * len(tables),
            out_specs=[pl.BlockSpec((rows, width), across)] * 2,
            scratch_shapes=[pltpu.VMEM((1, rows + SUBS, LANES), jnp.float32)],
        ),
        out_shape=[jax.ShapeDtypeStruct((rows, channels), jnp.float32)] * 2,
        compiler_params=params_of(),
        cost_estimate=pl.CostEstimate(
            flops=rows * channels * 25,
            bytes_accessed=rows * channels * 14,
            transcendentals=modes * channels,
        ),
        name="inside_runs",
    )(t, x, edge, source, enter, *tables)


def half_taps(taps_rows):
    return (taps_rows + 1) // 2


def half_rows(modes, taps_rows):
    return -(-(modes + half_taps(taps_rows)) // SUBS) * SUBS


def table_kernel(parity_ref, taps_ref, rate_ref, residue_ref, mine_ref, other_ref):
    lags, kinds, _ = taps_ref.shape
    modes = rate_ref.shape[0]
    rate = rate_ref[...]
    x = 2.0 * rate
    series = jnp.ones_like(x)
    for term in range(10, 1, -1):
        series = 1.0 - series * x * (1.0 / term)
    lost = jnp.where(x < 0.5, x * series, 1.0 - jnp.exp(-x))
    weight = residue_ref[...] * jnp.sqrt(lost)
    rows = [taps_ref[r // kinds, r % kinds : r % kinds + 1] for r in range(lags * kinds)]
    cut = half_taps(len(rows))

    def fill(lower_ref, upper_ref):
        lower_ref[0:modes] = rate
        upper_ref[0:modes] = weight
        for r, row in enumerate(rows):
            ref, place = (lower_ref, r) if r < cut else (upper_ref, r - cut)
            ref[modes + place : modes + place + 1] = row
        for ref, used in ((lower_ref, modes + cut), (upper_ref, modes + len(rows) - cut)):
            ref[used:] = jnp.zeros((ref.shape[0] - used, ref.shape[1]), jnp.float32)

    @pl.when(parity_ref[0] == 0)
    def _():
        fill(mine_ref, other_ref)

    @pl.when(parity_ref[0] == 1)
    def _():
        fill(other_ref, mine_ref)


def make_table(parity, taps, rate, residue):
    height = half_rows(rate.shape[0], taps.shape[0] * taps.shape[1])
    vmem = pl.BlockSpec(memory_space=pltpu.VMEM)
    return pl.pallas_call(
        table_kernel,
        in_specs=[pl.BlockSpec(memory_space=pltpu.SMEM)] + [vmem] * 3,
        out_specs=[vmem] * 2,
        out_shape=[jax.ShapeDtypeStruct((height, rate.shape[1]), jnp.float32)] * 2,
        compiler_params=params_of(),
        name="make_table",
    )(parity, taps, rate, residue)


def from_table(k, parity, tables, half, place):
    size = len(tables) // 2
    ordered = [
        jnp.where(parity == half, tables[i][place], tables[size + i][place]) for i in range(size)
    ]
    value = ordered[0]
    for other in range(1, size):
        value = jnp.where(k == other, ordered[other], value)
    return value


def block_end_kernel(t_ref, rate_ref, *refs, rows):
    ends, o_ref = refs[:-1], refs[-1]
    rate = rate_ref[...]
    total = jnp.zeros_like(rate)
    for k, end in enumerate(ends):
        later = len(ends) - 1 - (k ^ t_ref[0])
        total = total + jnp.exp(rate * (later * -rows).astype(jnp.float32)) * end[...]
    o_ref[...] = total


def pair_kernel(t_ref, rate_ref, own_ref, mate_ref, o_ref, *, rows):
    odd = t_ref[1] == 1
    own, mate = own_ref[...], mate_ref[...]
    first, second = jnp.where(odd, mate, own), jnp.where(odd, own, mate)
    total = first * jnp.exp(rate_ref[...] * (-1.0 * rows)) + second
    half = o_ref.shape[0]
    o_ref[...] = jnp.where(odd, total[half:], total[:half])


def block_starts_kernel(t_ref, rate_ref, mate_ref, *refs, rows, size):
    seen, ends, outs = refs[: -2 * size], refs[-2 * size : -size], refs[-size:]
    hops = len(seen) // 2
    rate = rate_ref[...]
    t, odd = t_ref[0], t_ref[1] == 1
    pair_span = jnp.exp(rate * (-2.0 * rows * size))
    state = jnp.zeros_like(rate)
    for hop in reversed(range(hops)):
        mine, other = seen[hop][...], seen[hops + hop][...]
        state = state * pair_span + jnp.concatenate(
            [jnp.where(odd, other, mine), jnp.where(odd, mine, other)], axis=0
        )
    state = jnp.where(odd, state * jnp.exp(rate * (-1.0 * rows * size)) + mate_ref[...], state)
    span = jnp.exp(rate * (-1.0 * rows))
    for place in range(size):
        mine = place ^ t
        for k in range(size):

            @pl.when(mine == k)
            def _(k=k, state=state):
                outs[k][...] = state

        end = pick(mine, ends, Ellipsis)
        state = state * span + end


def small_call(kernel, t, name, outs, height, *arrays, **sizes):
    shape = jax.ShapeDtypeStruct((height, arrays[0].shape[1]), jnp.float32)
    vmem = pl.BlockSpec(memory_space=pltpu.VMEM)
    return pl.pallas_call(
        functools.partial(kernel, **sizes),
        in_specs=[pl.BlockSpec(memory_space=pltpu.SMEM)] + [vmem] * len(arrays),
        out_specs=[vmem] * outs,
        out_shape=[shape] * outs,
        compiler_params=params_of(),
        name=name,
    )(t, *arrays)


def add_entering_kernel(t_ref, y_ref, q_ref, *refs, modes, size):
    o_ref, out_s = refs[-2:]
    states, mines, others = refs[:size], refs[size : 2 * size], refs[2 * size : 3 * size]
    k = pl.program_id(0)
    rows, width = y_ref.shape
    run = rows // SUBS
    even = t_ref[1] == 0
    before = lax.broadcasted_iota(jnp.int32, (SUBS, LANES), 0).astype(jnp.float32) * (-1.0 * run)
    for c in range(width // LANES):
        lanes = slice(c * LANES, (c + 1) * LANES)
        mine, other = (pick(k, half, (slice(0, modes), lanes)) for half in (mines, others))
        rate, weight = jnp.where(even, mine, other), jnp.where(even, other, mine)
        decay = jnp.exp(-rate)
        state = pick(k, states, (slice(0, modes), lanes)) * weight * decay
        terms, steps = [], []
        for n in range(modes):
            terms.append(jnp.exp(before * rate[n : n + 1]) * state[n : n + 1])
            steps.append(wide(decay[n : n + 1]))
        for j in range(run):
            place = slice(j * SUBS, (j + 1) * SUBS)
            out_s[pl.ds(j, SUBS, stride=run)] = q_ref[place, lanes] * (y_ref[place, lanes] + added(terms))
            terms = [a * b for a, b in zip(terms, steps)]
        o_ref[:, lanes] = out_s[...].astype(o_ref.dtype)


def add_entering(t, first, y, q, states, mines, others, before, modes, width=1024):
    rows, channels = y.shape
    size = len(states)
    chunks = states[0].shape[1] // width
    there = lambda k, c, t: (0, ((k + first) ^ t[0]) * chunks + c)
    across = lambda k, c, t: (0, c)
    old = [] if before is None else [before]
    return pl.pallas_call(
        functools.partial(add_entering_kernel, modes=modes, size=size),
        grid_spec=pltpu.PrefetchScalarGridSpec(
            num_scalar_prefetch=1,
            grid=(size, chunks),
            in_specs=[pl.BlockSpec((rows, width), there)] * 2
            + [pl.BlockSpec((modes, width), across)] * size
            + [pl.BlockSpec((mines[0].shape[0], width), across)] * (2 * size)
            + [pl.BlockSpec(memory_space=pl.ANY)] * len(old),
            out_specs=pl.BlockSpec((rows, width), there),
            scratch_shapes=[pltpu.VMEM((rows, LANES), jnp.float32)],
        ),
        out_shape=jax.ShapeDtypeStruct((rows, channels), jnp.bfloat16),
        input_output_aliases={3 + 3 * size: 0} if old else {},
        compiler_params=params_of(),
        cost_estimate=pl.CostEstimate(
            flops=size * rows * states[0].shape[1] * 36,
            bytes_accessed=size * rows * states[0].shape[1] * 10,
            transcendentals=size * modes * states[0].shape[1] * 9,
        ),
        name="add_entering",
    )(t, y, q, *states, *mines, *others, *old)


def exchange(x, axis):
    return lax.all_to_all(x, axis, split_axis=0, concat_axis=0, tiled=True)


def trade_tp(arrays):
    size = len(arrays)
    return [arrays[0]] + [
        lax.ppermute(arrays[k], "tp", [(i, i ^ k) for i in range(size)]) for k in range(1, size)
    ]


def segment_starts(lengths, tokens):
    order = jnp.arange(lengths.shape[0], dtype=jnp.int32)
    ends = jnp.sum(jnp.where(order[:, None] <= order[None, :], lengths[:, None], 0), axis=0)
    position = jnp.arange(tokens, dtype=jnp.int32)
    passed = jnp.where(ends[None, :] <= position[:, None], ends[None, :], 0)
    return jnp.max(passed, axis=1)


def by_tokens(hyena_in, attn_in, short_taps, decay_rate, residue, lengths):
    rows, kinds, channels = hyena_in.shape
    ctx_size, tp_size = lax.axis_size("ctx"), lax.axis_size("tp")
    devices = ctx_size * tp_size
    taps_count = short_taps.shape[0]
    modes = decay_rate.shape[0]
    parity = (lax.axis_index("ctx") % 2).astype(jnp.int32)
    t = jnp.stack([lax.axis_index("tp").astype(jnp.int32), parity])
    swap = [(i, i ^ 1) for i in range(ctx_size)]

    x = jnp.transpose(hyena_in, (1, 0, 2))
    edge = x[:, rows - taps_count + 1 :].reshape(kinds * (taps_count - 1), channels)
    edge, decay_rate = lax.optimization_barrier((edge, decay_rate))
    edge = lax.ppermute(edge, ALL, [(i, i + 1) for i in range(devices - 1)])
    mine, other = make_table(parity.reshape(1), short_taps, decay_rate, residue)
    mine = trade_tp([mine] * tp_size)
    heads_out = split_heads(jnp.transpose(attn_in, (1, 0, 2)))
    heads_out, edge, *mine = lax.optimization_barrier((heads_out, edge, *mine))
    by_head = exchange(heads_out, ALL)
    edge = edge.astype(jnp.float32)
    tables = mine + [other] + [lax.ppermute(half, "ctx", swap) for half in mine[1:]]
    source, enter, *ends = block_states(t, x, edge, tables, modes, taps_count)
    y, q = inside_runs(t, x, edge, source, enter, tables, modes, taps_count)
    y, *ends = lax.optimization_barrier((y, *trade_tp(ends)))
    [block_end] = small_call(
        block_end_kernel, t, "block_end", 1, modes, decay_rate, *ends, rows=rows
    )

    block_rows = rows * tp_size
    mate = lax.ppermute(block_end, "ctx", swap)
    [total] = small_call(
        pair_kernel, t, "pair", 1, modes // 2, decay_rate, block_end, mate, rows=block_rows
    )
    seen = [
        lax.ppermute(total, "ctx", [(i, i + hop) for i in range(ctx_size - hop)])
        for hop in range(2, ctx_size, 2)
    ]

    by_head, _ = lax.optimization_barrier((by_head, total))
    mixed = attend(by_head, segment_starts(lengths, rows * devices))
    mixed, *seen = lax.optimization_barrier((mixed, *seen))
    seen += [lax.ppermute(half, "ctx", swap) for half in seen]
    states = small_call(
        block_starts_kernel, t, "block_starts", tp_size, modes,
        decay_rate, mate, *seen, *ends, rows=rows, size=tp_size,
    )
    states = trade_tp(states)
    attn_out = join_heads(exchange(mixed.reshape(devices, rows, DH), ALL))
    mines, others = tables[:tp_size], tables[tp_size:]
    hyena_out = None
    for part in (slice(0, 1), slice(1, tp_size)):
        hyena_out = add_entering(
            t, part.start, y, q, states[part], mines[part], others[part], hyena_out, modes
        )
    return hyena_out, attn_out


exact_mode = lax.Precision.HIGHEST


def from_behind(block, axis, distance):
    devices = range(lax.axis_size(axis))
    route = [(i - distance, i) for i in devices if i - distance in devices]
    return lax.ppermute(block, axis, route)


def carried_in(part, axis, combine, identity):
    place = lax.axis_index(axis)
    gathered = jax.tree.map(lambda a: lax.all_gather(a, axis), part)
    state = jax.tree.map(lambda a, e: jnp.zeros_like(a) + jnp.asarray(e, a.dtype), part, identity)

    def one(lap, state):
        return combine(
            state, jax.tree.map(lambda a: lax.dynamic_index_in_dim(a, lap, 0, False), gathered)
        )

    return lax.fori_loop(0, place, one, state)


def segment_of(positions, segment_ends):
    return jnp.sum((segment_ends[None, :] <= positions[:, None]).astype(jnp.int32), axis=1)


def by_channels(hyena_in, attn_in, short_taps, decay_rate, residue, lengths):
    hyena_cols, attention_cols = (
        lax.all_to_all(hyena_in, "tp", split_axis=2, concat_axis=0, tiled=True),
        lax.all_to_all(attn_in, "tp", split_axis=2, concat_axis=0, tiled=True),
    )
    block_rows = hyena_cols.shape[0]
    rim_rows = short_taps.shape[0] - 1
    edge_rows = from_behind(hyena_cols[block_rows - rim_rows :], "ctx", 1)
    extended = jnp.concatenate([edge_rows, hyena_cols], axis=0).astype(jnp.float32)
    filtered = jnp.zeros(hyena_cols.shape, jnp.float32)
    for lag in range(rim_rows + 1):
        filtered = (
            filtered + short_taps[lag] * extended[rim_rows - lag : rim_rows - lag + block_rows]
        )
    query_side = filtered[:, 0]
    source = filtered[:, 1] * filtered[:, 2]
    channels = source.shape[1]
    weight = residue * jnp.sqrt(-jnp.expm1(-2.0 * decay_rate))
    sub_length = math.gcd(32, block_rows)
    pieces = block_rows // sub_length
    offsets = jnp.arange(sub_length, dtype=jnp.float32)
    powers = jnp.exp(-offsets[:, None, None] * decay_rate[None])
    lag_values = jnp.einsum("onc,nc->oc", powers, weight, precision=exact_mode)
    lag_index = jnp.arange(sub_length, dtype=jnp.int32)
    selector = (
        lag_index[:, None, None] - lag_index[None, :, None] == lag_index[None, None, :]
    ).astype(jnp.float32)
    toeplitz = jnp.einsum("tso,oc->tsc", selector, lag_values, precision=exact_mode)
    grouped = source.reshape(pieces, sub_length, channels)
    inner = jnp.einsum("tsc,bsc->btc", toeplitz, grouped, precision=exact_mode)
    tail_powers = jnp.exp(-(sub_length - 1.0 - offsets)[:, None, None] * decay_rate[None])
    own_states = jnp.einsum("snc,bsc->bnc", tail_powers, grouped, precision=exact_mode)
    sub_decay = jnp.exp(-sub_length * decay_rate)

    def carry_states(carried, incoming):
        return (sub_decay * carried + incoming, carried)

    local_end, entering = lax.scan(carry_states, jnp.zeros_like(sub_decay), own_states)
    block_decay = jnp.exp(-block_rows * decay_rate)

    def combine(earlier, later):
        return (earlier[0] * later[0], later[0] * earlier[1] + later[1])

    _, arriving = carried_in(
        (block_decay, local_end),
        "ctx",
        combine,
        (jnp.ones_like(block_decay), jnp.zeros_like(local_end)),
    )
    starts = jnp.arange(pieces, dtype=jnp.float32) * sub_length
    all_entering = entering + jnp.exp(-starts[:, None, None] * decay_rate[None]) * arriving[None]
    rise_powers = jnp.exp(-(offsets + 1.0)[:, None, None] * decay_rate[None]) * weight[None]
    from_state = jnp.einsum("tnc,bnc->btc", rise_powers, all_entering, precision=exact_mode)
    long_conv = (inner + from_state).reshape(block_rows, channels)
    hyena_local = (query_side * long_conv).astype(jnp.bfloat16)
    head_cols = attention_cols.shape[2]
    local_heads = head_cols // DH
    queries = attention_cols[:, 0].reshape(block_rows, local_heads, DH)
    keyvals = attention_cols[:, 1:3]
    order = jnp.arange(lengths.shape[0], dtype=jnp.int32)
    segment_ends = jnp.sum(jnp.where(order[:, None] <= order[None, :], lengths[:, None], 0), axis=0)
    block_index = lax.axis_index("ctx")
    query_pos = block_index * block_rows + jnp.arange(block_rows, dtype=jnp.int32)
    query_seg = segment_of(query_pos, segment_ends)
    score_scale = 1.0 / math.sqrt(DH)

    def attend_part(softmax_state, part, key_start):
        count = part.shape[0]
        key_pos = key_start + jnp.arange(count, dtype=jnp.int32)
        key_seg = segment_of(key_pos, segment_ends)
        allowed = (
            (key_pos[None, :] <= query_pos[:, None])
            & (key_seg[None, :] == query_seg[:, None])
            & (key_pos >= 0)[None, :]
        )

        def compute(carried):
            row_top, denom, weighted = carried
            key_rows = part[:, 0].reshape(count, local_heads, DH)
            value_rows = part[:, 1].reshape(count, local_heads, DH)
            scores = (
                jnp.einsum("qhd,khd->hqk", queries, key_rows, preferred_element_type=jnp.float32)
                * score_scale
            )
            masked = jnp.where(allowed[None], scores, jnp.float32(-1e30))
            new_top = jnp.maximum(row_top, jnp.max(masked, axis=2))
            expo = jnp.where(allowed[None], jnp.exp(scores - new_top[:, :, None]), jnp.float32(0.0))
            rescale = jnp.exp(row_top - new_top)
            denom = denom * rescale + jnp.sum(expo, axis=2)
            probs = expo.astype(jnp.bfloat16)
            added = jnp.einsum(
                "hqk,khd->qhd", probs, value_rows, preferred_element_type=jnp.float32
            )
            weighted = weighted * jnp.transpose(rescale)[:, :, None] + added
            return (new_top, denom, weighted)

        def keep(carried):
            return carried

        return lax.cond(jnp.any(allowed), compute, keep, softmax_state)

    initial = (
        jnp.full((local_heads, block_rows), -1e30, jnp.float32),
        jnp.zeros((local_heads, block_rows), jnp.float32),
        jnp.zeros((block_rows, local_heads, DH), jnp.float32),
    )
    piece = lax.all_gather(keyvals, "ctx", axis=0, tiled=True)
    rows = piece.shape[0]
    step_rows = math.gcd(rows, 512)

    def advance(count, carried):
        part = lax.dynamic_slice_in_dim(piece, count * step_rows, step_rows, 0)
        return attend_part(carried, part, count * step_rows)

    final_state = lax.fori_loop(0, rows // step_rows, advance, initial)
    _, denom, weighted = final_state
    attention_local = (
        (weighted / jnp.transpose(denom)[:, :, None])
        .reshape(block_rows, head_cols)
        .astype(jnp.bfloat16)
    )
    hyena_out, attn_out = (
        lax.all_to_all(hyena_local, "tp", split_axis=0, concat_axis=1, tiled=True),
        lax.all_to_all(attention_local, "tp", split_axis=0, concat_axis=1, tiled=True),
    )
    return (hyena_out, attn_out)


def per_device(hyena_in, attn_in, short_taps, decay_rate, residue, lengths):
    rows, _, channels = hyena_in.shape
    devices = lax.axis_size("ctx") * lax.axis_size("tp")
    one_head_each = attn_in.shape[2] == devices * DH
    tp_size = lax.axis_size("tp")
    pairs = tp_size & (tp_size - 1) == 0
    pairs = pairs and lax.axis_size("ctx") >= 4 and lax.axis_size("ctx") % 2 == 0
    whole_tiles = pairs and rows % (2 * SUBS) == 0 and channels % (tp_size * 1024) == 0
    whole_tiles = whole_tiles and decay_rate.shape[0] % (2 * SUBS) == 0
    plan = by_tokens if one_head_each and whole_tiles else by_channels
    return plan(hyena_in, attn_in, short_taps, decay_rate, residue, lengths)


def solution(mesh):
    placed = (
        P(("ctx", "tp"), None, None),
        P(("ctx", "tp"), None, None),
        P(None, None, "tp"),
        P(None, "tp"),
        P(None, "tp"),
        P(),
    )
    return jax.shard_map(
        per_device,
        mesh=mesh,
        in_specs=placed,
        out_specs=(P(("ctx", "tp"), None), P(("ctx", "tp"), None)),
        check_vma=False,
    )
```

```python
import functools
import math

import jax
import jax.numpy as jnp
from jax import lax
from jax.experimental import pallas as pl
from jax.experimental.pallas import tpu as pltpu
from jax.sharding import PartitionSpec as P

DH = 128
LANES = 128
SUBS = 8
ALL = ("ctx", "tp")
VMEM_BYTES = 60 * 1024 * 1024
ATTEND_BYTES = 32 * 1024 * 1024
MASKED = -1e30


def params_of(limit=VMEM_BYTES):
    return pltpu.CompilerParams(vmem_limit_bytes=limit)


def split_heads_kernel(x_ref, o_ref):
    for h in range(o_ref.shape[0]):
        o_ref[h] = x_ref[:, :, h * DH : (h + 1) * DH]


def split_heads(x, group=8):
    kinds, rows, width = x.shape
    heads = width // DH
    return pl.pallas_call(
        split_heads_kernel,
        grid=(heads // group,),
        in_specs=[pl.BlockSpec((kinds, rows, group * DH), lambda g: (0, 0, g))],
        out_specs=pl.BlockSpec((group, kinds, rows, DH), lambda g: (g, 0, 0, 0)),
        out_shape=jax.ShapeDtypeStruct((heads, kinds, rows, DH), x.dtype),
        compiler_params=params_of(),
        name="split_heads",
    )(x)


def join_heads_kernel(x_ref, o_ref):
    for h in range(x_ref.shape[0]):
        o_ref[:, h * DH : (h + 1) * DH] = x_ref[h]


def join_heads(x, group=8):
    heads, rows, _ = x.shape
    return pl.pallas_call(
        join_heads_kernel,
        grid=(heads // group,),
        in_specs=[pl.BlockSpec((group, rows, DH), lambda g: (g, 0, 0))],
        out_specs=pl.BlockSpec((rows, group * DH), lambda g: (0, g)),
        out_shape=jax.ShapeDtypeStruct((rows, heads * DH), x.dtype),
        compiler_params=params_of(ATTEND_BYTES),
        name="join_heads",
    )(x)


def attend_kernel(tile_start_ref, x_ref, start_ref, o_ref, q_s, k_s, v_s, *, key_rows):
    tile = pl.program_id(0)
    blocks, _, rows, _ = x_ref.shape
    query_rows = o_ref.shape[0]
    scale = math.log2(math.e) / math.sqrt(DH)

    @pl.when(tile == 0)
    def _():
        @pl.loop(0, blocks)
        def _(b):
            place = pl.ds(pl.multiple_of(b * rows, rows), rows)
            q_s[place] = x_ref[b, 0]
            k_s[place] = x_ref[b, 1]
            v_s[place] = x_ref[b, 2]

    first_row = tile * query_rows
    q = q_s[pl.ds(pl.multiple_of(first_row, query_rows), query_rows)]
    start = start_ref[...]
    start = jnp.concatenate([start] * (key_rows // LANES), axis=1)
    shape = (query_rows, key_rows)
    row = first_row + lax.broadcasted_iota(jnp.int32, shape, 0)
    col = lax.broadcasted_iota(jnp.int32, shape, 1)
    last = (first_row + query_rows - 1) // key_rows
    first = tile_start_ref[tile] // key_rows

    def step(i, carry):
        top, denom, mixed = carry
        base = pl.multiple_of((last - i) * key_rows, key_rows)
        k = k_s[pl.ds(base, key_rows)]
        v = v_s[pl.ds(base, key_rows)]
        s = lax.dot_general(q, k, (((1,), (1,)), ((), ())), preferred_element_type=jnp.float32)
        pos = col + base
        s = jnp.where((pos >= start) & (pos <= row), s, MASKED)
        new_top = jnp.maximum(top, jnp.max(s, axis=1, keepdims=True))
        p = jnp.exp2((s - new_top) * scale)
        rescale = jnp.exp2((top - new_top) * scale)
        denom = denom * rescale + jnp.sum(p, axis=1, keepdims=True)
        mixed = mixed * rescale + jnp.dot(
            p.astype(jnp.bfloat16), v, preferred_element_type=jnp.float32
        )
        return new_top, denom, mixed

    carry = (
        jnp.full((query_rows, 1), MASKED, jnp.float32),
        jnp.zeros((query_rows, 1), jnp.float32),
        jnp.zeros((query_rows, DH), jnp.float32),
    )
    _, denom, mixed = lax.fori_loop(0, last - first + 1, step, carry)
    o_ref[...] = (mixed / denom).astype(o_ref.dtype)


def attend(x, start, query_rows=512, key_rows=512):
    blocks, _, rows, _ = x.shape
    tokens = blocks * rows
    query_rows, key_rows = math.gcd(tokens, query_rows), math.gcd(tokens, key_rows)
    wide_start = jnp.broadcast_to(start[:, None], (tokens, LANES))
    return pl.pallas_call(
        functools.partial(attend_kernel, key_rows=key_rows),
        grid_spec=pltpu.PrefetchScalarGridSpec(
            num_scalar_prefetch=1,
            grid=(tokens // query_rows,),
            in_specs=[
                pl.BlockSpec(x.shape, lambda t, s: (0, 0, 0, 0)),
                pl.BlockSpec((query_rows, LANES), lambda t, s: (t, 0)),
            ],
            out_specs=pl.BlockSpec((query_rows, DH), lambda t, s: (t, 0)),
            scratch_shapes=[pltpu.VMEM((tokens, DH), x.dtype)] * 3,
        ),
        out_shape=jax.ShapeDtypeStruct((tokens, DH), x.dtype),
        compiler_params=params_of(ATTEND_BYTES),
        cost_estimate=pl.CostEstimate(
            flops=2 * tokens * tokens * DH,
            bytes_accessed=x.size * 2 + tokens * (DH * 2 + LANES * 4),
            transcendentals=tokens * tokens // 2,
        ),
        name="attend",
    )(start[::query_rows], x, wide_start)


def pick(k, refs, place):
    value = refs[0][place]
    for other in range(1, len(refs)):
        value = jnp.where(k == other, refs[other][place], value)
    return value


def wide(row):
    return jnp.broadcast_to(row, (SUBS, LANES))


def added(parts):
    while len(parts) > 1:
        parts = [a + b for a, b in zip(parts[::2], parts[1::2])] + (
            [parts[-1]] if len(parts) % 2 else []
        )
    return parts[0]


def filtered_runs(xs, i, taps, run):
    rim = len(taps) - 1
    seen = [xs[i, pl.ds(SUBS + j - rim, SUBS, stride=run)] for j in range(rim)]
    out = []
    for j in range(run):
        seen.append(xs[i, pl.ds(SUBS + j, SUBS, stride=run)])
        out.append(sum(taps[lag] * seen[-1 - lag] for lag in range(1, rim + 1)) + taps[0] * seen[-1])
    return out


def taps_of(k, parity, tables, modes, taps_count, kinds, spot):
    past = slice(modes, tables[0].shape[0])
    halves = [from_table(k, parity, tables, half, (past, spot)) for half in (0, 1)]
    cut = half_taps(taps_count * kinds)

    def tap(lag, i):
        half, r = divmod(lag * kinds + i, cut)
        return wide(halves[half][r : r + 1])

    return lambda i: [tap(lag, i) for lag in range(taps_count)]


def block_states_kernel(t_ref, x_ref, edge_ref, *refs, modes, taps_count, tp_size):
    tables, (source_ref, enter_ref) = refs[: 2 * tp_size], refs[2 * tp_size :][:2]
    ends, xs = refs[2 * tp_size + 2 : -1], refs[-1]
    kinds, rows, width = x_ref.shape
    k, chunk = pl.program_id(0), pl.program_id(1)
    run = rows // SUBS
    rim = taps_count - 1
    sub = lax.broadcasted_iota(jnp.int32, (SUBS, LANES), 0)
    for c in range(width // LANES):
        lanes = slice(c * LANES, (c + 1) * LANES)
        spot = pl.ds(pl.multiple_of(chunk * width + c * LANES, LANES), LANES)
        for i in (1, 2):
            xs[i, SUBS - rim : SUBS] = edge_ref[i * rim : (i + 1) * rim, lanes]
            xs[i, SUBS:] = x_ref[i, :, lanes].astype(jnp.float32)
        rate = from_table(k, t_ref[1], tables, 0, (slice(0, modes), spot))
        taps = taps_of(k, t_ref[1], tables, modes, taps_count, kinds, spot)
        decay = jnp.exp(-rate)
        decay_run = jnp.exp(rate * (-1.0 * run))
        source = [
            a * b
            for a, b in zip(filtered_runs(xs, 1, taps(1), run), filtered_runs(xs, 2, taps(2), run))
        ]
        for j in range(run):
            source_ref[j * SUBS : (j + 1) * SUBS, lanes] = source[j]

        decays = [wide(decay[n : n + 1]) for n in range(modes)]
        states = [source[0]] * modes
        for j in range(1, run):
            states = [state * d + source[j] for state, d in zip(states, decays)]
        spans = [wide(decay_run[n : n + 1]) for n in range(modes)]
        for hop in (1, 2, 4):
            states = [
                state + jnp.where(sub >= hop, span * pltpu.roll(state, hop, 0), 0.0)
                for state, span in zip(states, spans)
            ]
            spans = [span * span for span in spans]
        last = [state[SUBS - 1 : SUBS] for state in states]
        for n, state in enumerate(states):
            enter_ref[n * SUBS : (n + 1) * SUBS, lanes] = jnp.where(
                sub >= 1, pltpu.roll(state, 1, 0), 0.0
            )
        last = jnp.concatenate(last, axis=0)
        for other in range(tp_size):

            @pl.when(k == other)
            def _(other=other):
                ends[other][:, spot] = last


def inside_runs_kernel(t_ref, x_ref, edge_ref, source_ref, enter_ref, *refs, modes, taps_count, tp_size):
    tables, y_ref, q_ref, xs = refs[: 2 * tp_size], refs[-3], refs[-2], refs[-1]
    _, rows, width = x_ref.shape
    kinds = edge_ref.shape[0] // (taps_count - 1)
    k, chunk = pl.program_id(0), pl.program_id(1)
    run = rows // SUBS
    rim = taps_count - 1
    for c in range(width // LANES):
        lanes = slice(c * LANES, (c + 1) * LANES)
        spot = pl.ds(pl.multiple_of(chunk * width + c * LANES, LANES), LANES)
        xs[0, SUBS - rim : SUBS] = edge_ref[0:rim, lanes]
        xs[0, SUBS:] = x_ref[0, :, lanes].astype(jnp.float32)
        rate = from_table(k, t_ref[1], tables, 0, (slice(0, modes), spot))
        weight = from_table(k, t_ref[1], tables, 1, (slice(0, modes), spot))
        taps = taps_of(k, t_ref[1], tables, modes, taps_count, kinds, spot)
        for j, value in enumerate(filtered_runs(xs, 0, taps(0), run)):
            q_ref[j * SUBS : (j + 1) * SUBS, lanes] = value
        decay = jnp.exp(-rate)
        power = weight
        lags = []
        for j in range(run):
            lags.append(wide(jnp.sum(power, axis=0, keepdims=True)))
            power = power * decay
        source = [source_ref[j * SUBS : (j + 1) * SUBS, lanes] for j in range(run)]
        weight = weight * decay
        terms = [
            enter_ref[n * SUBS : (n + 1) * SUBS, lanes] * wide(weight[n : n + 1])
            for n in range(modes)
        ]
        steps = [wide(decay[n : n + 1]) for n in range(modes)]
        for j in range(run):
            total = added(terms)
            for lag in range(j + 1):
                total = total + lags[lag] * source[j - lag]
            y_ref[j * SUBS : (j + 1) * SUBS, lanes] = total
            terms = [a * b for a, b in zip(terms, steps)]


def quarter_grid(tables, channels, width):
    tp_size = len(tables) // 2
    quarter = channels // tp_size
    chunks = quarter // width
    whole = lambda k, c, t: (0, 0)
    across = lambda k, c, t: (0, (k ^ t[0]) * chunks + c)
    return tp_size, quarter, (tp_size, chunks), whole, across


def block_states(t, x, edge, tables, modes, taps_count, width=1024):
    kinds, rows, channels = x.shape
    tp_size, quarter, grid, whole, across = quarter_grid(tables, channels, width)
    return pl.pallas_call(
        functools.partial(
            block_states_kernel, modes=modes, taps_count=taps_count, tp_size=tp_size
        ),
        grid_spec=pltpu.PrefetchScalarGridSpec(
            num_scalar_prefetch=1,
            grid=grid,
            in_specs=[
                pl.BlockSpec((kinds, rows, width), lambda k, c, t: (0, *across(k, c, t))),
                pl.BlockSpec((edge.shape[0], width), across),
            ]
            + [pl.BlockSpec(tables[0].shape, whole)] * len(tables),
            out_specs=[pl.BlockSpec((rows, width), across), pl.BlockSpec((modes * SUBS, width), across)]
            + [pl.BlockSpec((modes, quarter), whole)] * tp_size,
            scratch_shapes=[pltpu.VMEM((kinds, rows + SUBS, LANES), jnp.float32)],
        ),
        out_shape=[
            jax.ShapeDtypeStruct((rows, channels), jnp.float32),
            jax.ShapeDtypeStruct((modes * SUBS, channels), jnp.float32),
        ]
        + [jax.ShapeDtypeStruct((modes, quarter), jnp.float32)] * tp_size,
        compiler_params=params_of(),
        cost_estimate=pl.CostEstimate(
            flops=rows * channels * 50,
            bytes_accessed=rows * channels * 14,
            transcendentals=2 * modes * channels,
        ),
        name="block_states",
    )(t, x, edge, *tables)


def inside_runs(t, x, edge, source, enter, tables, modes, taps_count, width=1024):
    _, rows, channels = x.shape
    tp_size, _, grid, whole, across = quarter_grid(tables, channels, width)
    return pl.pallas_call(
        functools.partial(inside_runs_kernel, modes=modes, taps_count=taps_count, tp_size=tp_size),
        grid_spec=pltpu.PrefetchScalarGridSpec(
            num_scalar_prefetch=1,
            grid=grid,
            in_specs=[
                pl.BlockSpec((1, rows, width), lambda k, c, t: (0, *across(k, c, t))),
                pl.BlockSpec((edge.shape[0], width), across),
                pl.BlockSpec((rows, width), across),
                pl.BlockSpec((enter.shape[0], width), across),
            ]
            + [pl.BlockSpec(tables[0].shape, whole)] * len(tables),
            out_specs=[pl.BlockSpec((rows, width), across)] * 2,
            scratch_shapes=[pltpu.VMEM((1, rows + SUBS, LANES), jnp.float32)],
        ),
        out_shape=[jax.ShapeDtypeStruct((rows, channels), jnp.float32)] * 2,
        compiler_params=params_of(),
        cost_estimate=pl.CostEstimate(
            flops=rows * channels * 25,
            bytes_accessed=rows * channels * 14,
            transcendentals=modes * channels,
        ),
        name="inside_runs",
    )(t, x, edge, source, enter, *tables)


def half_taps(taps_rows):
    return (taps_rows + 1) // 2


def half_rows(modes, taps_rows):
    return -(-(modes + half_taps(taps_rows)) // SUBS) * SUBS


def table_kernel(parity_ref, taps_ref, rate_ref, residue_ref, mine_ref, other_ref):
    lags, kinds, _ = taps_ref.shape
    modes = rate_ref.shape[0]
    rate = rate_ref[...]
    x = 2.0 * rate
    series = jnp.ones_like(x)
    for term in range(10, 1, -1):
        series = 1.0 - series * x * (1.0 / term)
    lost = jnp.where(x < 0.5, x * series, 1.0 - jnp.exp(-x))
    weight = residue_ref[...] * jnp.sqrt(lost)
    rows = [taps_ref[r // kinds, r % kinds : r % kinds + 1] for r in range(lags * kinds)]
    cut = half_taps(len(rows))

    def fill(lower_ref, upper_ref):
        lower_ref[0:modes] = rate
        upper_ref[0:modes] = weight
        for r, row in enumerate(rows):
            ref, place = (lower_ref, r) if r < cut else (upper_ref, r - cut)
            ref[modes + place : modes + place + 1] = row
        for ref, used in ((lower_ref, modes + cut), (upper_ref, modes + len(rows) - cut)):
            ref[used:] = jnp.zeros((ref.shape[0] - used, ref.shape[1]), jnp.float32)

    @pl.when(parity_ref[0] == 0)
    def _():
        fill(mine_ref, other_ref)

    @pl.when(parity_ref[0] == 1)
    def _():
        fill(other_ref, mine_ref)


def make_table(parity, taps, rate, residue):
    height = half_rows(rate.shape[0], taps.shape[0] * taps.shape[1])
    vmem = pl.BlockSpec(memory_space=pltpu.VMEM)
    return pl.pallas_call(
        table_kernel,
        in_specs=[pl.BlockSpec(memory_space=pltpu.SMEM)] + [vmem] * 3,
        out_specs=[vmem] * 2,
        out_shape=[jax.ShapeDtypeStruct((height, rate.shape[1]), jnp.float32)] * 2,
        compiler_params=params_of(),
        name="make_table",
    )(parity, taps, rate, residue)


def from_table(k, parity, tables, half, place):
    size = len(tables) // 2
    ordered = [
        jnp.where(parity == half, tables[i][place], tables[size + i][place]) for i in range(size)
    ]
    value = ordered[0]
    for other in range(1, size):
        value = jnp.where(k == other, ordered[other], value)
    return value


def block_end_kernel(t_ref, rate_ref, *refs, rows):
    ends, o_ref = refs[:-1], refs[-1]
    rate = rate_ref[...]
    total = jnp.zeros_like(rate)
    for k, end in enumerate(ends):
        later = len(ends) - 1 - (k ^ t_ref[0])
        total = total + jnp.exp(rate * (later * -rows).astype(jnp.float32)) * end[...]
    o_ref[...] = total


def pair_enters_kernel(t_ref, rate_ref, *refs, rows):
    seen, o_ref = refs[:-1], refs[-1]
    half = o_ref.shape[0]
    rate = jnp.where(t_ref[1] == 1, rate_ref[half:], rate_ref[:half])
    span = jnp.exp(rate * (-2.0 * rows))
    total = seen[-1][...]
    for one in seen[-2::-1]:
        total = total * span + one[...]
    o_ref[...] = total


def pair_kernel(t_ref, rate_ref, own_ref, mate_ref, *refs, rows):
    size = len(refs) // 2
    ends, total_ref, outs = refs[:size], refs[size], refs[size + 1 :]
    t, odd = t_ref[0], t_ref[1] == 1
    rate, own, mate = rate_ref[...], own_ref[...], mate_ref[...]
    first, second = jnp.where(odd, mate, own), jnp.where(odd, own, mate)
    total = first * jnp.exp(rate * (-1.0 * rows * size)) + second
    half = total_ref.shape[0]
    total_ref[...] = jnp.where(odd, total[half:], total[:half])
    span = jnp.exp(rate * (-1.0 * rows))
    state = jnp.where(odd, mate, 0.0)
    for place in range(size):
        mine = place ^ t
        for k in range(size):

            @pl.when(mine == k)
            def _(k=k, state=state):
                outs[k][...] = state

        end = pick(mine, ends, Ellipsis)
        state = state * span + end


def small_call(kernel, t, name, heights, *arrays, **sizes):
    vmem = pl.BlockSpec(memory_space=pltpu.VMEM)
    return pl.pallas_call(
        functools.partial(kernel, **sizes),
        in_specs=[pl.BlockSpec(memory_space=pltpu.SMEM)] + [vmem] * len(arrays),
        out_specs=[vmem] * len(heights),
        out_shape=[jax.ShapeDtypeStruct((h, arrays[0].shape[1]), jnp.float32) for h in heights],
        compiler_params=params_of(),
        name=name,
    )(t, *arrays)


def add_entering_kernel(t_ref, y_ref, q_ref, *refs, modes, size, tp_size):
    o_ref, out_s = refs[-2:]
    inside, mine_enters, other_enters, mines, others = (
        refs[i * size : (i + 1) * size] for i in range(5)
    )
    k = pl.program_id(0)
    blocks_before = t_ref[1] * tp_size + t_ref[0]
    rows, width = y_ref.shape
    run = rows // SUBS
    even = t_ref[1] == 0
    before = lax.broadcasted_iota(jnp.int32, (SUBS, LANES), 0).astype(jnp.float32) * (-1.0 * run)
    for c in range(width // LANES):
        lanes = slice(c * LANES, (c + 1) * LANES)
        mine, other = (pick(k, half, (slice(0, modes), lanes)) for half in (mines, others))
        rate, weight = jnp.where(even, mine, other), jnp.where(even, other, mine)
        decay = jnp.exp(-rate)
        one = (slice(0, modes // 2), lanes)
        mine, other = pick(k, mine_enters, one), pick(k, other_enters, one)
        enters = jnp.concatenate(
            [jnp.where(even, mine, other), jnp.where(even, other, mine)], axis=0
        )
        state = enters * jnp.exp(rate * (blocks_before * -rows).astype(jnp.float32))
        state = (state + pick(k, inside, (slice(0, modes), lanes))) * weight * decay
        terms, steps = [], []
        for n in range(modes):
            terms.append(jnp.exp(before * rate[n : n + 1]) * state[n : n + 1])
            steps.append(wide(decay[n : n + 1]))
        for j in range(run):
            place = slice(j * SUBS, (j + 1) * SUBS)
            out_s[pl.ds(j, SUBS, stride=run)] = q_ref[place, lanes] * (y_ref[place, lanes] + added(terms))
            terms = [a * b for a, b in zip(terms, steps)]
        o_ref[:, lanes] = out_s[...].astype(o_ref.dtype)


def add_entering(t, first, y, q, families, before, modes, width=1024):
    rows, channels = y.shape
    size, quarter = len(families[0]), families[0][0].shape[1]
    chunks = quarter // width
    arrays = [a for family in families for a in family]
    there = lambda k, c, t: (0, ((k + first) ^ t[0]) * chunks + c)
    across = lambda k, c, t: (0, c)
    old = [] if before is None else [before]
    return pl.pallas_call(
        functools.partial(
            add_entering_kernel, modes=modes, size=size, tp_size=channels // quarter
        ),
        grid_spec=pltpu.PrefetchScalarGridSpec(
            num_scalar_prefetch=1,
            grid=(size, chunks),
            in_specs=[pl.BlockSpec((rows, width), there)] * 2
            + [pl.BlockSpec((a.shape[0], width), across) for a in arrays]
            + [pl.BlockSpec(memory_space=pl.ANY)] * len(old),
            out_specs=pl.BlockSpec((rows, width), there),
            scratch_shapes=[pltpu.VMEM((rows, LANES), jnp.float32)],
        ),
        out_shape=jax.ShapeDtypeStruct((rows, channels), jnp.bfloat16),
        input_output_aliases={3 + len(arrays): 0} if old else {},
        compiler_params=params_of(),
        cost_estimate=pl.CostEstimate(
            flops=size * rows * quarter * 36,
            bytes_accessed=size * rows * quarter * 10,
            transcendentals=size * modes * quarter * 9,
        ),
        name="add_entering",
    )(t, y, q, *arrays, *old)


def exchange(x, axis):
    return lax.all_to_all(x, axis, split_axis=0, concat_axis=0, tiled=True)


def trade_tp(arrays):
    size = len(arrays)
    return [arrays[0]] + [
        lax.ppermute(arrays[k], "tp", [(i, i ^ k) for i in range(size)]) for k in range(1, size)
    ]


def segment_starts(lengths, tokens):
    order = jnp.arange(lengths.shape[0], dtype=jnp.int32)
    ends = jnp.sum(jnp.where(order[:, None] <= order[None, :], lengths[:, None], 0), axis=0)
    position = jnp.arange(tokens, dtype=jnp.int32)
    passed = jnp.where(ends[None, :] <= position[:, None], ends[None, :], 0)
    return jnp.max(passed, axis=1)


def by_tokens(hyena_in, attn_in, short_taps, decay_rate, residue, lengths):
    rows, kinds, channels = hyena_in.shape
    ctx_size, tp_size = lax.axis_size("ctx"), lax.axis_size("tp")
    devices = ctx_size * tp_size
    taps_count = short_taps.shape[0]
    modes = decay_rate.shape[0]
    parity = (lax.axis_index("ctx") % 2).astype(jnp.int32)
    t = jnp.stack([lax.axis_index("tp").astype(jnp.int32), parity])
    swap = [(i, i ^ 1) for i in range(ctx_size)]

    x = jnp.transpose(hyena_in, (1, 0, 2))
    edge = x[:, rows - taps_count + 1 :].reshape(kinds * (taps_count - 1), channels)
    edge, decay_rate = lax.optimization_barrier((edge, decay_rate))
    edge = lax.ppermute(edge, ALL, [(i, i + 1) for i in range(devices - 1)])
    mine, other = make_table(parity.reshape(1), short_taps, decay_rate, residue)
    mine = trade_tp([mine] * tp_size)
    heads_out = split_heads(jnp.transpose(attn_in, (1, 0, 2)))
    heads_out, edge, *mine = lax.optimization_barrier((heads_out, edge, *mine))
    by_head = exchange(heads_out, ALL)
    edge = edge.astype(jnp.float32)
    tables = mine + [other] + [lax.ppermute(half, "ctx", swap) for half in mine[1:]]
    source, enter, *ends = block_states(t, x, edge, tables, modes, taps_count)
    y, q = inside_runs(t, x, edge, source, enter, tables, modes, taps_count)
    y, *ends = lax.optimization_barrier((y, *trade_tp(ends)))
    [block_end] = small_call(
        block_end_kernel, t, "block_end", [modes], decay_rate, *ends, rows=rows
    )

    mate = lax.ppermute(block_end, "ctx", swap)
    total, *inside = small_call(
        pair_kernel, t, "pair", [modes // 2] + [modes] * tp_size,
        decay_rate, block_end, mate, *ends, rows=rows,
    )
    seen = [
        lax.ppermute(total, "ctx", [(i, i + hop) for i in range(ctx_size - hop)])
        for hop in range(2, ctx_size, 2)
    ]

    by_head, *_ = lax.optimization_barrier((by_head, *inside, total))
    inside = trade_tp(inside)
    mixed = attend(by_head, segment_starts(lengths, rows * devices))
    mixed, seen, inside = lax.optimization_barrier((mixed, seen, inside))
    [enters] = small_call(
        pair_enters_kernel, t, "pair_enters", [modes // 2], decay_rate, *seen, rows=rows * tp_size
    )
    mate_enters = lax.ppermute(enters, "ctx", swap)
    enters = trade_tp([enters] * tp_size)
    attn_out = join_heads(exchange(mixed.reshape(devices, rows, DH), ALL))
    mines, others = tables[:tp_size], tables[tp_size:]
    own = inside[:1], enters[:1], [mate_enters], mines[:1], others[:1]
    hyena_out = add_entering(t, 0, y, q, own, None, modes)
    hyena_out, *enters = lax.optimization_barrier((hyena_out, *enters[1:]))
    mate_enters = [lax.ppermute(half, "ctx", swap) for half in enters]
    rest = inside[1:], enters, mate_enters, mines[1:], others[1:]
    hyena_out = add_entering(t, 1, y, q, rest, hyena_out, modes)
    return hyena_out, attn_out


exact_mode = lax.Precision.HIGHEST


def from_behind(block, axis, distance):
    devices = range(lax.axis_size(axis))
    route = [(i - distance, i) for i in devices if i - distance in devices]
    return lax.ppermute(block, axis, route)


def carried_in(part, axis, combine, identity):
    place = lax.axis_index(axis)
    gathered = jax.tree.map(lambda a: lax.all_gather(a, axis), part)
    state = jax.tree.map(lambda a, e: jnp.zeros_like(a) + jnp.asarray(e, a.dtype), part, identity)

    def one(lap, state):
        return combine(
            state, jax.tree.map(lambda a: lax.dynamic_index_in_dim(a, lap, 0, False), gathered)
        )

    return lax.fori_loop(0, place, one, state)


def segment_of(positions, segment_ends):
    return jnp.sum((segment_ends[None, :] <= positions[:, None]).astype(jnp.int32), axis=1)


def by_channels(hyena_in, attn_in, short_taps, decay_rate, residue, lengths):
    hyena_cols, attention_cols = (
        lax.all_to_all(hyena_in, "tp", split_axis=2, concat_axis=0, tiled=True),
        lax.all_to_all(attn_in, "tp", split_axis=2, concat_axis=0, tiled=True),
    )
    block_rows = hyena_cols.shape[0]
    rim_rows = short_taps.shape[0] - 1
    edge_rows = from_behind(hyena_cols[block_rows - rim_rows :], "ctx", 1)
    extended = jnp.concatenate([edge_rows, hyena_cols], axis=0).astype(jnp.float32)
    filtered = jnp.zeros(hyena_cols.shape, jnp.float32)
    for lag in range(rim_rows + 1):
        filtered = (
            filtered + short_taps[lag] * extended[rim_rows - lag : rim_rows - lag + block_rows]
        )
    query_side = filtered[:, 0]
    source = filtered[:, 1] * filtered[:, 2]
    channels = source.shape[1]
    weight = residue * jnp.sqrt(-jnp.expm1(-2.0 * decay_rate))
    sub_length = math.gcd(32, block_rows)
    pieces = block_rows // sub_length
    offsets = jnp.arange(sub_length, dtype=jnp.float32)
    powers = jnp.exp(-offsets[:, None, None] * decay_rate[None])
    lag_values = jnp.einsum("onc,nc->oc", powers, weight, precision=exact_mode)
    lag_index = jnp.arange(sub_length, dtype=jnp.int32)
    selector = (
        lag_index[:, None, None] - lag_index[None, :, None] == lag_index[None, None, :]
    ).astype(jnp.float32)
    toeplitz = jnp.einsum("tso,oc->tsc", selector, lag_values, precision=exact_mode)
    grouped = source.reshape(pieces, sub_length, channels)
    inner = jnp.einsum("tsc,bsc->btc", toeplitz, grouped, precision=exact_mode)
    tail_powers = jnp.exp(-(sub_length - 1.0 - offsets)[:, None, None] * decay_rate[None])
    own_states = jnp.einsum("snc,bsc->bnc", tail_powers, grouped, precision=exact_mode)
    sub_decay = jnp.exp(-sub_length * decay_rate)

    def carry_states(carried, incoming):
        return (sub_decay * carried + incoming, carried)

    local_end, entering = lax.scan(carry_states, jnp.zeros_like(sub_decay), own_states)
    block_decay = jnp.exp(-block_rows * decay_rate)

    def combine(earlier, later):
        return (earlier[0] * later[0], later[0] * earlier[1] + later[1])

    _, arriving = carried_in(
        (block_decay, local_end),
        "ctx",
        combine,
        (jnp.ones_like(block_decay), jnp.zeros_like(local_end)),
    )
    starts = jnp.arange(pieces, dtype=jnp.float32) * sub_length
    all_entering = entering + jnp.exp(-starts[:, None, None] * decay_rate[None]) * arriving[None]
    rise_powers = jnp.exp(-(offsets + 1.0)[:, None, None] * decay_rate[None]) * weight[None]
    from_state = jnp.einsum("tnc,bnc->btc", rise_powers, all_entering, precision=exact_mode)
    long_conv = (inner + from_state).reshape(block_rows, channels)
    hyena_local = (query_side * long_conv).astype(jnp.bfloat16)
    head_cols = attention_cols.shape[2]
    local_heads = head_cols // DH
    queries = attention_cols[:, 0].reshape(block_rows, local_heads, DH)
    keyvals = attention_cols[:, 1:3]
    order = jnp.arange(lengths.shape[0], dtype=jnp.int32)
    segment_ends = jnp.sum(jnp.where(order[:, None] <= order[None, :], lengths[:, None], 0), axis=0)
    block_index = lax.axis_index("ctx")
    query_pos = block_index * block_rows + jnp.arange(block_rows, dtype=jnp.int32)
    query_seg = segment_of(query_pos, segment_ends)
    score_scale = 1.0 / math.sqrt(DH)

    def attend_part(softmax_state, part, key_start):
        count = part.shape[0]
        key_pos = key_start + jnp.arange(count, dtype=jnp.int32)
        key_seg = segment_of(key_pos, segment_ends)
        allowed = (
            (key_pos[None, :] <= query_pos[:, None])
            & (key_seg[None, :] == query_seg[:, None])
            & (key_pos >= 0)[None, :]
        )

        def compute(carried):
            row_top, denom, weighted = carried
            key_rows = part[:, 0].reshape(count, local_heads, DH)
            value_rows = part[:, 1].reshape(count, local_heads, DH)
            scores = (
                jnp.einsum("qhd,khd->hqk", queries, key_rows, preferred_element_type=jnp.float32)
                * score_scale
            )
            masked = jnp.where(allowed[None], scores, jnp.float32(-1e30))
            new_top = jnp.maximum(row_top, jnp.max(masked, axis=2))
            expo = jnp.where(allowed[None], jnp.exp(scores - new_top[:, :, None]), jnp.float32(0.0))
            rescale = jnp.exp(row_top - new_top)
            denom = denom * rescale + jnp.sum(expo, axis=2)
            probs = expo.astype(jnp.bfloat16)
            added = jnp.einsum(
                "hqk,khd->qhd", probs, value_rows, preferred_element_type=jnp.float32
            )
            weighted = weighted * jnp.transpose(rescale)[:, :, None] + added
            return (new_top, denom, weighted)

        def keep(carried):
            return carried

        return lax.cond(jnp.any(allowed), compute, keep, softmax_state)

    initial = (
        jnp.full((local_heads, block_rows), -1e30, jnp.float32),
        jnp.zeros((local_heads, block_rows), jnp.float32),
        jnp.zeros((block_rows, local_heads, DH), jnp.float32),
    )
    piece = lax.all_gather(keyvals, "ctx", axis=0, tiled=True)
    rows = piece.shape[0]
    step_rows = math.gcd(rows, 512)

    def advance(count, carried):
        part = lax.dynamic_slice_in_dim(piece, count * step_rows, step_rows, 0)
        return attend_part(carried, part, count * step_rows)

    final_state = lax.fori_loop(0, rows // step_rows, advance, initial)
    _, denom, weighted = final_state
    attention_local = (
        (weighted / jnp.transpose(denom)[:, :, None])
        .reshape(block_rows, head_cols)
        .astype(jnp.bfloat16)
    )
    hyena_out, attn_out = (
        lax.all_to_all(hyena_local, "tp", split_axis=0, concat_axis=1, tiled=True),
        lax.all_to_all(attention_local, "tp", split_axis=0, concat_axis=1, tiled=True),
    )
    return (hyena_out, attn_out)


def per_device(hyena_in, attn_in, short_taps, decay_rate, residue, lengths):
    rows, _, channels = hyena_in.shape
    devices = lax.axis_size("ctx") * lax.axis_size("tp")
    one_head_each = attn_in.shape[2] == devices * DH
    tp_size = lax.axis_size("tp")
    pairs = tp_size & (tp_size - 1) == 0
    pairs = pairs and lax.axis_size("ctx") >= 4 and lax.axis_size("ctx") % 2 == 0
    whole_tiles = pairs and rows % (2 * SUBS) == 0 and channels % (tp_size * 1024) == 0
    whole_tiles = whole_tiles and decay_rate.shape[0] % (2 * SUBS) == 0
    plan = by_tokens if one_head_each and whole_tiles else by_channels
    return plan(hyena_in, attn_in, short_taps, decay_rate, residue, lengths)


def solution(mesh):
    placed = (
        P(("ctx", "tp"), None, None),
        P(("ctx", "tp"), None, None),
        P(None, None, "tp"),
        P(None, "tp"),
        P(None, "tp"),
        P(),
    )
    return jax.shard_map(
        per_device,
        mesh=mesh,
        in_specs=placed,
        out_specs=(P(("ctx", "tp"), None), P(("ctx", "tp"), None)),
        check_vma=False,
    )
```

```python
import functools
import math

import jax
import jax.numpy as jnp
from jax import lax
from jax.experimental import pallas as pl
from jax.experimental.pallas import tpu as pltpu
from jax.sharding import PartitionSpec as P

DH = 128
LANES = 128
SUBS = 8
ALL = ("ctx", "tp")
VMEM_BYTES = 60 * 1024 * 1024
ATTEND_BYTES = 32 * 1024 * 1024
MASKED = -1e30


def params_of(limit=VMEM_BYTES):
    return pltpu.CompilerParams(vmem_limit_bytes=limit)


def split_heads_kernel(x_ref, o_ref):
    for h in range(o_ref.shape[0]):
        o_ref[h] = x_ref[:, :, h * DH : (h + 1) * DH]


def split_heads(x, group=8):
    kinds, rows, width = x.shape
    heads = width // DH
    return pl.pallas_call(
        split_heads_kernel,
        grid=(heads // group,),
        in_specs=[pl.BlockSpec((kinds, rows, group * DH), lambda g: (0, 0, g))],
        out_specs=pl.BlockSpec((group, kinds, rows, DH), lambda g: (g, 0, 0, 0)),
        out_shape=jax.ShapeDtypeStruct((heads, kinds, rows, DH), x.dtype),
        compiler_params=params_of(),
        name="split_heads",
    )(x)


def join_heads_kernel(x_ref, o_ref):
    for h in range(x_ref.shape[0]):
        o_ref[:, h * DH : (h + 1) * DH] = x_ref[h]


def join_heads(x, group=8):
    heads, rows, _ = x.shape
    return pl.pallas_call(
        join_heads_kernel,
        grid=(heads // group,),
        in_specs=[pl.BlockSpec((group, rows, DH), lambda g: (g, 0, 0))],
        out_specs=pl.BlockSpec((rows, group * DH), lambda g: (0, g)),
        out_shape=jax.ShapeDtypeStruct((rows, heads * DH), x.dtype),
        compiler_params=params_of(ATTEND_BYTES),
        name="join_heads",
    )(x)


def attend_kernel(tile_start_ref, x_ref, start_ref, o_ref, q_s, k_s, v_s, *, key_rows):
    tile = pl.program_id(0)
    blocks, _, rows, _ = x_ref.shape
    query_rows = o_ref.shape[0]
    scale = math.log2(math.e) / math.sqrt(DH)

    @pl.when(tile == 0)
    def _():
        @pl.loop(0, blocks)
        def _(b):
            place = pl.ds(pl.multiple_of(b * rows, rows), rows)
            q_s[place] = x_ref[b, 0]
            k_s[place] = x_ref[b, 1]
            v_s[place] = x_ref[b, 2]

    first_row = tile * query_rows
    q = q_s[pl.ds(pl.multiple_of(first_row, query_rows), query_rows)]
    start = start_ref[...]
    start = jnp.concatenate([start] * (key_rows // LANES), axis=1)
    shape = (query_rows, key_rows)
    row = first_row + lax.broadcasted_iota(jnp.int32, shape, 0)
    col = lax.broadcasted_iota(jnp.int32, shape, 1)
    last = (first_row + query_rows - 1) // key_rows
    first = tile_start_ref[tile] // key_rows

    def step(i, carry):
        top, denom, mixed = carry
        base = pl.multiple_of((last - i) * key_rows, key_rows)
        k = k_s[pl.ds(base, key_rows)]
        v = v_s[pl.ds(base, key_rows)]
        s = lax.dot_general(q, k, (((1,), (1,)), ((), ())), preferred_element_type=jnp.float32)
        pos = col + base
        s = jnp.where((pos >= start) & (pos <= row), s, MASKED)
        new_top = jnp.maximum(top, jnp.max(s, axis=1, keepdims=True))
        p = jnp.exp2((s - new_top) * scale)
        rescale = jnp.exp2((top - new_top) * scale)
        denom = denom * rescale + jnp.sum(p, axis=1, keepdims=True)
        mixed = mixed * rescale + jnp.dot(
            p.astype(jnp.bfloat16), v, preferred_element_type=jnp.float32
        )
        return new_top, denom, mixed

    carry = (
        jnp.full((query_rows, 1), MASKED, jnp.float32),
        jnp.zeros((query_rows, 1), jnp.float32),
        jnp.zeros((query_rows, DH), jnp.float32),
    )
    _, denom, mixed = lax.fori_loop(0, last - first + 1, step, carry)
    o_ref[...] = (mixed / denom).astype(o_ref.dtype)


def attend(x, start, query_rows=512, key_rows=512):
    blocks, _, rows, _ = x.shape
    tokens = blocks * rows
    query_rows, key_rows = math.gcd(tokens, query_rows), math.gcd(tokens, key_rows)
    wide_start = jnp.broadcast_to(start[:, None], (tokens, LANES))
    return pl.pallas_call(
        functools.partial(attend_kernel, key_rows=key_rows),
        grid_spec=pltpu.PrefetchScalarGridSpec(
            num_scalar_prefetch=1,
            grid=(tokens // query_rows,),
            in_specs=[
                pl.BlockSpec(x.shape, lambda t, s: (0, 0, 0, 0)),
                pl.BlockSpec((query_rows, LANES), lambda t, s: (t, 0)),
            ],
            out_specs=pl.BlockSpec((query_rows, DH), lambda t, s: (t, 0)),
            scratch_shapes=[pltpu.VMEM((tokens, DH), x.dtype)] * 3,
        ),
        out_shape=jax.ShapeDtypeStruct((tokens, DH), x.dtype),
        compiler_params=params_of(ATTEND_BYTES),
        cost_estimate=pl.CostEstimate(
            flops=2 * tokens * tokens * DH,
            bytes_accessed=x.size * 2 + tokens * (DH * 2 + LANES * 4),
            transcendentals=tokens * tokens // 2,
        ),
        name="attend",
    )(start[::query_rows], x, wide_start)


def pick(k, refs, place):
    value = refs[0][place]
    for other in range(1, len(refs)):
        value = jnp.where(k == other, refs[other][place], value)
    return value


def wide(row):
    return jnp.broadcast_to(row, (SUBS, LANES))


def added(parts):
    while len(parts) > 1:
        parts = [a + b for a, b in zip(parts[::2], parts[1::2])] + (
            [parts[-1]] if len(parts) % 2 else []
        )
    return parts[0]


def filtered_runs(xs, i, taps, run):
    rim = len(taps) - 1
    seen = [xs[i, pl.ds(SUBS + j - rim, SUBS, stride=run)] for j in range(rim)]
    out = []
    for j in range(run):
        seen.append(xs[i, pl.ds(SUBS + j, SUBS, stride=run)])
        out.append(sum(taps[lag] * seen[-1 - lag] for lag in range(1, rim + 1)) + taps[0] * seen[-1])
    return out


def taps_of(k, parity, tables, modes, taps_count, kinds, spot):
    past = slice(modes, tables[0].shape[0])
    halves = [from_table(k, parity, tables, half, (past, spot)) for half in (0, 1)]
    cut = half_taps(taps_count * kinds)

    def tap(lag, i):
        half, r = divmod(lag * kinds + i, cut)
        return wide(halves[half][r : r + 1])

    return lambda i: [tap(lag, i) for lag in range(taps_count)]


def block_states_kernel(t_ref, x_ref, edge_ref, *refs, modes, taps_count, tp_size):
    tables, (source_ref, enter_ref) = refs[: 2 * tp_size], refs[2 * tp_size :][:2]
    ends, xs = refs[2 * tp_size + 2 : -1], refs[-1]
    kinds, rows, width = x_ref.shape
    k, chunk = pl.program_id(0), pl.program_id(1)
    run = rows // SUBS
    rim = taps_count - 1
    sub = lax.broadcasted_iota(jnp.int32, (SUBS, LANES), 0)
    for c in range(width // LANES):
        lanes = slice(c * LANES, (c + 1) * LANES)
        spot = pl.ds(pl.multiple_of(chunk * width + c * LANES, LANES), LANES)
        edge = edge_ref[:, lanes].astype(jnp.float32)
        for i in (1, 2):
            xs[i, SUBS - rim : SUBS] = edge[i * rim : (i + 1) * rim]
            xs[i, SUBS:] = x_ref[i, :, lanes].astype(jnp.float32)
        rate = from_table(k, t_ref[1], tables, 0, (slice(0, modes), spot))
        taps = taps_of(k, t_ref[1], tables, modes, taps_count, kinds, spot)
        decay = jnp.exp(-rate)
        decay_run = jnp.exp(rate * (-1.0 * run))
        source = [
            a * b
            for a, b in zip(filtered_runs(xs, 1, taps(1), run), filtered_runs(xs, 2, taps(2), run))
        ]
        for j in range(run):
            source_ref[j * SUBS : (j + 1) * SUBS, lanes] = source[j]

        decays = [wide(decay[n : n + 1]) for n in range(modes)]
        states = [source[0]] * modes
        for j in range(1, run):
            states = [state * d + source[j] for state, d in zip(states, decays)]
        spans = [wide(decay_run[n : n + 1]) for n in range(modes)]
        for hop in (1, 2, 4):
            states = [
                state + jnp.where(sub >= hop, span * pltpu.roll(state, hop, 0), 0.0)
                for state, span in zip(states, spans)
            ]
            spans = [span * span for span in spans]
        last = [state[SUBS - 1 : SUBS] for state in states]
        for n, state in enumerate(states):
            enter_ref[n * SUBS : (n + 1) * SUBS, lanes] = jnp.where(
                sub >= 1, pltpu.roll(state, 1, 0), 0.0
            )
        last = jnp.concatenate(last, axis=0)
        for other in range(tp_size):

            @pl.when(k == other)
            def _(other=other):
                ends[other][:, spot] = last


def inside_runs_kernel(t_ref, x_ref, edge_ref, source_ref, enter_ref, *refs, modes, taps_count, tp_size):
    tables, y_ref, q_ref, xs = refs[: 2 * tp_size], refs[-3], refs[-2], refs[-1]
    _, rows, width = x_ref.shape
    kinds = edge_ref.shape[0] // (taps_count - 1)
    k, chunk = pl.program_id(0), pl.program_id(1)
    run = rows // SUBS
    rim = taps_count - 1
    for c in range(width // LANES):
        lanes = slice(c * LANES, (c + 1) * LANES)
        spot = pl.ds(pl.multiple_of(chunk * width + c * LANES, LANES), LANES)
        xs[0, SUBS - rim : SUBS] = edge_ref[:, lanes].astype(jnp.float32)[0:rim]
        xs[0, SUBS:] = x_ref[0, :, lanes].astype(jnp.float32)
        rate = from_table(k, t_ref[1], tables, 0, (slice(0, modes), spot))
        weight = from_table(k, t_ref[1], tables, 1, (slice(0, modes), spot))
        taps = taps_of(k, t_ref[1], tables, modes, taps_count, kinds, spot)
        for j, value in enumerate(filtered_runs(xs, 0, taps(0), run)):
            q_ref[j * SUBS : (j + 1) * SUBS, lanes] = value
        decay = jnp.exp(-rate)
        power = weight
        lags = []
        for j in range(run):
            lags.append(wide(jnp.sum(power, axis=0, keepdims=True)))
            power = power * decay
        source = [source_ref[j * SUBS : (j + 1) * SUBS, lanes] for j in range(run)]
        weight = weight * decay
        terms = [
            enter_ref[n * SUBS : (n + 1) * SUBS, lanes] * wide(weight[n : n + 1])
            for n in range(modes)
        ]
        steps = [wide(decay[n : n + 1]) for n in range(modes)]
        for j in range(run):
            total = added(terms)
            for lag in range(j + 1):
                total = total + lags[lag] * source[j - lag]
            y_ref[j * SUBS : (j + 1) * SUBS, lanes] = total
            terms = [a * b for a, b in zip(terms, steps)]


def quarter_grid(tables, channels, width):
    tp_size = len(tables) // 2
    quarter = channels // tp_size
    chunks = quarter // width
    whole = lambda k, c, t: (0, 0)
    across = lambda k, c, t: (0, (k ^ t[0]) * chunks + c)
    return tp_size, quarter, (tp_size, chunks), whole, across


def block_states(t, x, edge, tables, modes, taps_count, width=2048):
    kinds, rows, channels = x.shape
    tp_size, quarter, grid, whole, across = quarter_grid(tables, channels, width)
    return pl.pallas_call(
        functools.partial(
            block_states_kernel, modes=modes, taps_count=taps_count, tp_size=tp_size
        ),
        grid_spec=pltpu.PrefetchScalarGridSpec(
            num_scalar_prefetch=1,
            grid=grid,
            in_specs=[
                pl.BlockSpec((kinds, rows, width), lambda k, c, t: (0, *across(k, c, t))),
                pl.BlockSpec((edge.shape[0], width), across),
            ]
            + [pl.BlockSpec(tables[0].shape, whole)] * len(tables),
            out_specs=[pl.BlockSpec((rows, width), across), pl.BlockSpec((modes * SUBS, width), across)]
            + [pl.BlockSpec((modes, quarter), whole)] * tp_size,
            scratch_shapes=[pltpu.VMEM((kinds, rows + SUBS, LANES), jnp.float32)],
        ),
        out_shape=[
            jax.ShapeDtypeStruct((rows, channels), jnp.float32),
            jax.ShapeDtypeStruct((modes * SUBS, channels), jnp.float32),
        ]
        + [jax.ShapeDtypeStruct((modes, quarter), jnp.float32)] * tp_size,
        compiler_params=params_of(),
        cost_estimate=pl.CostEstimate(
            flops=rows * channels * 50,
            bytes_accessed=rows * channels * 14,
            transcendentals=2 * modes * channels,
        ),
        name="block_states",
    )(t, x, edge, *tables)


def inside_runs(t, x, edge, source, enter, tables, modes, taps_count, width=2048):
    _, rows, channels = x.shape
    tp_size, _, grid, whole, across = quarter_grid(tables, channels, width)
    return pl.pallas_call(
        functools.partial(inside_runs_kernel, modes=modes, taps_count=taps_count, tp_size=tp_size),
        grid_spec=pltpu.PrefetchScalarGridSpec(
            num_scalar_prefetch=1,
            grid=grid,
            in_specs=[
                pl.BlockSpec((1, rows, width), lambda k, c, t: (0, *across(k, c, t))),
                pl.BlockSpec((edge.shape[0], width), across),
                pl.BlockSpec((rows, width), across),
                pl.BlockSpec((enter.shape[0], width), across),
            ]
            + [pl.BlockSpec(tables[0].shape, whole)] * len(tables),
            out_specs=[pl.BlockSpec((rows, width), across)] * 2,
            scratch_shapes=[pltpu.VMEM((1, rows + SUBS, LANES), jnp.float32)],
        ),
        out_shape=[jax.ShapeDtypeStruct((rows, channels), jnp.float32)] * 2,
        compiler_params=params_of(),
        cost_estimate=pl.CostEstimate(
            flops=rows * channels * 25,
            bytes_accessed=rows * channels * 14,
            transcendentals=modes * channels,
        ),
        name="inside_runs",
    )(t, x, edge, source, enter, *tables)


def half_taps(taps_rows):
    return (taps_rows + 1) // 2


def half_rows(modes, taps_rows):
    return -(-(modes + half_taps(taps_rows)) // SUBS) * SUBS


def table_kernel(parity_ref, taps_ref, rate_ref, residue_ref, mine_ref, other_ref):
    lags, kinds, _ = taps_ref.shape
    modes = rate_ref.shape[0]
    rate = rate_ref[...]
    x = 2.0 * rate
    series = jnp.ones_like(x)
    for term in range(10, 1, -1):
        series = 1.0 - series * x * (1.0 / term)
    lost = jnp.where(x < 0.5, x * series, 1.0 - jnp.exp(-x))
    weight = residue_ref[...] * jnp.sqrt(lost)
    rows = [taps_ref[r // kinds, r % kinds : r % kinds + 1] for r in range(lags * kinds)]
    cut = half_taps(len(rows))

    def fill(lower_ref, upper_ref):
        lower_ref[0:modes] = rate
        upper_ref[0:modes] = weight
        for r, row in enumerate(rows):
            ref, place = (lower_ref, r) if r < cut else (upper_ref, r - cut)
            ref[modes + place : modes + place + 1] = row
        for ref, used in ((lower_ref, modes + cut), (upper_ref, modes + len(rows) - cut)):
            ref[used:] = jnp.zeros((ref.shape[0] - used, ref.shape[1]), jnp.float32)

    @pl.when(parity_ref[0] == 0)
    def _():
        fill(mine_ref, other_ref)

    @pl.when(parity_ref[0] == 1)
    def _():
        fill(other_ref, mine_ref)


def make_table(parity, taps, rate, residue):
    height = half_rows(rate.shape[0], taps.shape[0] * taps.shape[1])
    vmem = pl.BlockSpec(memory_space=pltpu.VMEM)
    return pl.pallas_call(
        table_kernel,
        in_specs=[pl.BlockSpec(memory_space=pltpu.SMEM)] + [vmem] * 3,
        out_specs=[vmem] * 2,
        out_shape=[jax.ShapeDtypeStruct((height, rate.shape[1]), jnp.float32)] * 2,
        compiler_params=params_of(),
        name="make_table",
    )(parity, taps, rate, residue)


def from_table(k, parity, tables, half, place):
    size = len(tables) // 2
    ordered = [
        jnp.where(parity == half, tables[i][place], tables[size + i][place]) for i in range(size)
    ]
    value = ordered[0]
    for other in range(1, size):
        value = jnp.where(k == other, ordered[other], value)
    return value


def block_end_kernel(t_ref, rate_ref, *refs, rows):
    ends, o_ref = refs[:-1], refs[-1]
    rate = rate_ref[...]
    total = jnp.zeros_like(rate)
    for k, end in enumerate(ends):
        later = len(ends) - 1 - (k ^ t_ref[0])
        total = total + jnp.exp(rate * (later * -rows).astype(jnp.float32)) * end[...]
    o_ref[...] = total


def pair_enters_kernel(t_ref, rate_ref, *refs, rows):
    seen, o_ref = refs[:-1], refs[-1]
    half = o_ref.shape[0]
    rate = jnp.where(t_ref[1] == 1, rate_ref[half:], rate_ref[:half])
    span = jnp.exp(rate * (-2.0 * rows))
    total = seen[-1][...]
    for one in seen[-2::-1]:
        total = total * span + one[...]
    o_ref[...] = total


def pair_kernel(t_ref, rate_ref, own_ref, mate_ref, *refs, rows):
    size = len(refs) // 2
    ends, total_ref, outs = refs[:size], refs[size], refs[size + 1 :]
    t, odd = t_ref[0], t_ref[1] == 1
    rate, own, mate = rate_ref[...], own_ref[...], mate_ref[...]
    first, second = jnp.where(odd, mate, own), jnp.where(odd, own, mate)
    total = first * jnp.exp(rate * (-1.0 * rows * size)) + second
    half = total_ref.shape[0]
    total_ref[...] = jnp.where(odd, total[half:], total[:half])
    span = jnp.exp(rate * (-1.0 * rows))
    state = jnp.where(odd, mate, 0.0)
    for place in range(size):
        mine = place ^ t
        for k in range(size):

            @pl.when(mine == k)
            def _(k=k, state=state):
                outs[k][...] = state

        end = pick(mine, ends, Ellipsis)
        state = state * span + end


def small_call(kernel, t, name, heights, *arrays, **sizes):
    vmem = pl.BlockSpec(memory_space=pltpu.VMEM)
    return pl.pallas_call(
        functools.partial(kernel, **sizes),
        in_specs=[pl.BlockSpec(memory_space=pltpu.SMEM)] + [vmem] * len(arrays),
        out_specs=[vmem] * len(heights),
        out_shape=[jax.ShapeDtypeStruct((h, arrays[0].shape[1]), jnp.float32) for h in heights],
        compiler_params=params_of(),
        name=name,
    )(t, *arrays)


def add_entering_kernel(t_ref, y_ref, q_ref, *refs, modes, size, tp_size):
    o_ref, out_s = refs[-2:]
    inside, mine_enters, other_enters, mines, others = (
        refs[i * size : (i + 1) * size] for i in range(5)
    )
    k = pl.program_id(0)
    blocks_before = t_ref[1] * tp_size + t_ref[0]
    rows, width = y_ref.shape
    run = rows // SUBS
    even = t_ref[1] == 0
    before = lax.broadcasted_iota(jnp.int32, (SUBS, LANES), 0).astype(jnp.float32) * (-1.0 * run)
    for c in range(width // LANES):
        lanes = slice(c * LANES, (c + 1) * LANES)
        mine, other = (pick(k, half, (slice(0, modes), lanes)) for half in (mines, others))
        rate, weight = jnp.where(even, mine, other), jnp.where(even, other, mine)
        decay = jnp.exp(-rate)
        one = (slice(0, modes // 2), lanes)
        mine, other = pick(k, mine_enters, one), pick(k, other_enters, one)
        enters = jnp.concatenate(
            [jnp.where(even, mine, other), jnp.where(even, other, mine)], axis=0
        )
        state = enters * jnp.exp(rate * (blocks_before * -rows).astype(jnp.float32))
        state = (state + pick(k, inside, (slice(0, modes), lanes))) * weight * decay
        terms, steps = [], []
        for n in range(modes):
            terms.append(jnp.exp(before * rate[n : n + 1]) * state[n : n + 1])
            steps.append(wide(decay[n : n + 1]))
        for j in range(run):
            place = slice(j * SUBS, (j + 1) * SUBS)
            out_s[pl.ds(j, SUBS, stride=run)] = q_ref[place, lanes] * (y_ref[place, lanes] + added(terms))
            terms = [a * b for a, b in zip(terms, steps)]
        o_ref[:, lanes] = out_s[...].astype(o_ref.dtype)


def add_entering(t, first, y, q, families, before, modes, width=2048):
    rows, channels = y.shape
    size, quarter = len(families[0]), families[0][0].shape[1]
    chunks = quarter // width
    arrays = [a for family in families for a in family]
    there = lambda k, c, t: (0, ((k + first) ^ t[0]) * chunks + c)
    across = lambda k, c, t: (0, c)
    old = [] if before is None else [before]
    return pl.pallas_call(
        functools.partial(
            add_entering_kernel, modes=modes, size=size, tp_size=channels // quarter
        ),
        grid_spec=pltpu.PrefetchScalarGridSpec(
            num_scalar_prefetch=1,
            grid=(size, chunks),
            in_specs=[pl.BlockSpec((rows, width), there)] * 2
            + [pl.BlockSpec((a.shape[0], width), across) for a in arrays]
            + [pl.BlockSpec(memory_space=pl.ANY)] * len(old),
            out_specs=pl.BlockSpec((rows, width), there),
            scratch_shapes=[pltpu.VMEM((rows, LANES), jnp.float32)],
        ),
        out_shape=jax.ShapeDtypeStruct((rows, channels), jnp.bfloat16),
        input_output_aliases={3 + len(arrays): 0} if old else {},
        compiler_params=params_of(),
        cost_estimate=pl.CostEstimate(
            flops=size * rows * quarter * 36,
            bytes_accessed=size * rows * quarter * 10,
            transcendentals=size * modes * quarter * 9,
        ),
        name="add_entering",
    )(t, y, q, *arrays, *old)


def exchange(x, axis):
    return lax.all_to_all(x, axis, split_axis=0, concat_axis=0, tiled=True)


def trade_tp(arrays):
    size = len(arrays)
    return [arrays[0]] + [
        lax.ppermute(arrays[k], "tp", [(i, i ^ k) for i in range(size)]) for k in range(1, size)
    ]


def segment_starts(lengths, tokens):
    order = jnp.arange(lengths.shape[0], dtype=jnp.int32)
    ends = jnp.sum(jnp.where(order[:, None] <= order[None, :], lengths[:, None], 0), axis=0)
    position = jnp.arange(tokens, dtype=jnp.int32)
    passed = jnp.where(ends[None, :] <= position[:, None], ends[None, :], 0)
    return jnp.max(passed, axis=1)


def by_tokens(hyena_in, attn_in, short_taps, decay_rate, residue, lengths):
    rows, kinds, channels = hyena_in.shape
    ctx_size, tp_size = lax.axis_size("ctx"), lax.axis_size("tp")
    devices = ctx_size * tp_size
    taps_count = short_taps.shape[0]
    modes = decay_rate.shape[0]
    parity = (lax.axis_index("ctx") % 2).astype(jnp.int32)
    t = jnp.stack([lax.axis_index("tp").astype(jnp.int32), parity])
    swap = [(i, i ^ 1) for i in range(ctx_size)]

    x = jnp.transpose(hyena_in, (1, 0, 2))
    edge = x[:, rows - taps_count + 1 :].reshape(kinds * (taps_count - 1), channels)
    edge, decay_rate = lax.optimization_barrier((edge, decay_rate))
    edge = lax.ppermute(edge, ALL, [(i, i + 1) for i in range(devices - 1)])
    mine, other = make_table(parity.reshape(1), short_taps, decay_rate, residue)
    mine = trade_tp([mine] * tp_size)
    heads_out = split_heads(jnp.transpose(attn_in, (1, 0, 2)))
    heads_out, edge, *mine = lax.optimization_barrier((heads_out, edge, *mine))
    by_head = exchange(heads_out, ALL)
    tables = mine + [other] + [lax.ppermute(half, "ctx", swap) for half in mine[1:]]
    source, enter, *ends = block_states(t, x, edge, tables, modes, taps_count)
    y, q = inside_runs(t, x, edge, source, enter, tables, modes, taps_count)
    y, *ends = lax.optimization_barrier((y, *trade_tp(ends)))
    [block_end] = small_call(
        block_end_kernel, t, "block_end", [modes], decay_rate, *ends, rows=rows
    )

    mate = lax.ppermute(block_end, "ctx", swap)
    total, *inside = small_call(
        pair_kernel, t, "pair", [modes // 2] + [modes] * tp_size,
        decay_rate, block_end, mate, *ends, rows=rows,
    )
    by_head, *_ = lax.optimization_barrier((by_head, *inside, total))
    inside = trade_tp(inside)
    total, inside[1] = lax.optimization_barrier((total, inside[1]))
    seen = [
        lax.ppermute(total, "ctx", [(i, i + hop) for i in range(ctx_size - hop)])
        for hop in range(2, ctx_size, 2)
    ]

    mixed = attend(by_head, segment_starts(lengths, rows * devices))
    mixed, seen, inside = lax.optimization_barrier((mixed, seen, inside))
    [enters] = small_call(
        pair_enters_kernel, t, "pair_enters", [modes // 2], decay_rate, *seen, rows=rows * tp_size
    )
    mate_enters = lax.ppermute(enters, "ctx", swap)
    enters = trade_tp([enters] * tp_size)
    attn_out = join_heads(exchange(mixed.reshape(devices, rows, DH), ALL))
    mines, others = tables[:tp_size], tables[tp_size:]
    own = inside[:1], enters[:1], [mate_enters], mines[:1], others[:1]
    hyena_out = add_entering(t, 0, y, q, own, None, modes)
    hyena_out, *enters = lax.optimization_barrier((hyena_out, *enters[1:]))
    mate_enters = [lax.ppermute(half, "ctx", swap) for half in enters]
    rest = inside[1:], enters, mate_enters, mines[1:], others[1:]
    hyena_out = add_entering(t, 1, y, q, rest, hyena_out, modes)
    return hyena_out, attn_out


exact_mode = lax.Precision.HIGHEST


def from_behind(block, axis, distance):
    devices = range(lax.axis_size(axis))
    route = [(i - distance, i) for i in devices if i - distance in devices]
    return lax.ppermute(block, axis, route)


def carried_in(part, axis, combine, identity):
    place = lax.axis_index(axis)
    gathered = jax.tree.map(lambda a: lax.all_gather(a, axis), part)
    state = jax.tree.map(lambda a, e: jnp.zeros_like(a) + jnp.asarray(e, a.dtype), part, identity)

    def one(lap, state):
        return combine(
            state, jax.tree.map(lambda a: lax.dynamic_index_in_dim(a, lap, 0, False), gathered)
        )

    return lax.fori_loop(0, place, one, state)


def segment_of(positions, segment_ends):
    return jnp.sum((segment_ends[None, :] <= positions[:, None]).astype(jnp.int32), axis=1)


def by_channels(hyena_in, attn_in, short_taps, decay_rate, residue, lengths):
    hyena_cols, attention_cols = (
        lax.all_to_all(hyena_in, "tp", split_axis=2, concat_axis=0, tiled=True),
        lax.all_to_all(attn_in, "tp", split_axis=2, concat_axis=0, tiled=True),
    )
    block_rows = hyena_cols.shape[0]
    rim_rows = short_taps.shape[0] - 1
    edge_rows = from_behind(hyena_cols[block_rows - rim_rows :], "ctx", 1)
    extended = jnp.concatenate([edge_rows, hyena_cols], axis=0).astype(jnp.float32)
    filtered = jnp.zeros(hyena_cols.shape, jnp.float32)
    for lag in range(rim_rows + 1):
        filtered = (
            filtered + short_taps[lag] * extended[rim_rows - lag : rim_rows - lag + block_rows]
        )
    query_side = filtered[:, 0]
    source = filtered[:, 1] * filtered[:, 2]
    channels = source.shape[1]
    weight = residue * jnp.sqrt(-jnp.expm1(-2.0 * decay_rate))
    sub_length = math.gcd(32, block_rows)
    pieces = block_rows // sub_length
    offsets = jnp.arange(sub_length, dtype=jnp.float32)
    powers = jnp.exp(-offsets[:, None, None] * decay_rate[None])
    lag_values = jnp.einsum("onc,nc->oc", powers, weight, precision=exact_mode)
    lag_index = jnp.arange(sub_length, dtype=jnp.int32)
    selector = (
        lag_index[:, None, None] - lag_index[None, :, None] == lag_index[None, None, :]
    ).astype(jnp.float32)
    toeplitz = jnp.einsum("tso,oc->tsc", selector, lag_values, precision=exact_mode)
    grouped = source.reshape(pieces, sub_length, channels)
    inner = jnp.einsum("tsc,bsc->btc", toeplitz, grouped, precision=exact_mode)
    tail_powers = jnp.exp(-(sub_length - 1.0 - offsets)[:, None, None] * decay_rate[None])
    own_states = jnp.einsum("snc,bsc->bnc", tail_powers, grouped, precision=exact_mode)
    sub_decay = jnp.exp(-sub_length * decay_rate)

    def carry_states(carried, incoming):
        return (sub_decay * carried + incoming, carried)

    local_end, entering = lax.scan(carry_states, jnp.zeros_like(sub_decay), own_states)
    block_decay = jnp.exp(-block_rows * decay_rate)

    def combine(earlier, later):
        return (earlier[0] * later[0], later[0] * earlier[1] + later[1])

    _, arriving = carried_in(
        (block_decay, local_end),
        "ctx",
        combine,
        (jnp.ones_like(block_decay), jnp.zeros_like(local_end)),
    )
    starts = jnp.arange(pieces, dtype=jnp.float32) * sub_length
    all_entering = entering + jnp.exp(-starts[:, None, None] * decay_rate[None]) * arriving[None]
    rise_powers = jnp.exp(-(offsets + 1.0)[:, None, None] * decay_rate[None]) * weight[None]
    from_state = jnp.einsum("tnc,bnc->btc", rise_powers, all_entering, precision=exact_mode)
    long_conv = (inner + from_state).reshape(block_rows, channels)
    hyena_local = (query_side * long_conv).astype(jnp.bfloat16)
    head_cols = attention_cols.shape[2]
    local_heads = head_cols // DH
    queries = attention_cols[:, 0].reshape(block_rows, local_heads, DH)
    keyvals = attention_cols[:, 1:3]
    order = jnp.arange(lengths.shape[0], dtype=jnp.int32)
    segment_ends = jnp.sum(jnp.where(order[:, None] <= order[None, :], lengths[:, None], 0), axis=0)
    block_index = lax.axis_index("ctx")
    query_pos = block_index * block_rows + jnp.arange(block_rows, dtype=jnp.int32)
    query_seg = segment_of(query_pos, segment_ends)
    score_scale = 1.0 / math.sqrt(DH)

    def attend_part(softmax_state, part, key_start):
        count = part.shape[0]
        key_pos = key_start + jnp.arange(count, dtype=jnp.int32)
        key_seg = segment_of(key_pos, segment_ends)
        allowed = (
            (key_pos[None, :] <= query_pos[:, None])
            & (key_seg[None, :] == query_seg[:, None])
            & (key_pos >= 0)[None, :]
        )

        def compute(carried):
            row_top, denom, weighted = carried
            key_rows = part[:, 0].reshape(count, local_heads, DH)
            value_rows = part[:, 1].reshape(count, local_heads, DH)
            scores = (
                jnp.einsum("qhd,khd->hqk", queries, key_rows, preferred_element_type=jnp.float32)
                * score_scale
            )
            masked = jnp.where(allowed[None], scores, jnp.float32(-1e30))
            new_top = jnp.maximum(row_top, jnp.max(masked, axis=2))
            expo = jnp.where(allowed[None], jnp.exp(scores - new_top[:, :, None]), jnp.float32(0.0))
            rescale = jnp.exp(row_top - new_top)
            denom = denom * rescale + jnp.sum(expo, axis=2)
            probs = expo.astype(jnp.bfloat16)
            added = jnp.einsum(
                "hqk,khd->qhd", probs, value_rows, preferred_element_type=jnp.float32
            )
            weighted = weighted * jnp.transpose(rescale)[:, :, None] + added
            return (new_top, denom, weighted)

        def keep(carried):
            return carried

        return lax.cond(jnp.any(allowed), compute, keep, softmax_state)

    initial = (
        jnp.full((local_heads, block_rows), -1e30, jnp.float32),
        jnp.zeros((local_heads, block_rows), jnp.float32),
        jnp.zeros((block_rows, local_heads, DH), jnp.float32),
    )
    piece = lax.all_gather(keyvals, "ctx", axis=0, tiled=True)
    rows = piece.shape[0]
    step_rows = math.gcd(rows, 512)

    def advance(count, carried):
        part = lax.dynamic_slice_in_dim(piece, count * step_rows, step_rows, 0)
        return attend_part(carried, part, count * step_rows)

    final_state = lax.fori_loop(0, rows // step_rows, advance, initial)
    _, denom, weighted = final_state
    attention_local = (
        (weighted / jnp.transpose(denom)[:, :, None])
        .reshape(block_rows, head_cols)
        .astype(jnp.bfloat16)
    )
    hyena_out, attn_out = (
        lax.all_to_all(hyena_local, "tp", split_axis=0, concat_axis=1, tiled=True),
        lax.all_to_all(attention_local, "tp", split_axis=0, concat_axis=1, tiled=True),
    )
    return (hyena_out, attn_out)


def per_device(hyena_in, attn_in, short_taps, decay_rate, residue, lengths):
    rows, _, channels = hyena_in.shape
    devices = lax.axis_size("ctx") * lax.axis_size("tp")
    one_head_each = attn_in.shape[2] == devices * DH
    tp_size = lax.axis_size("tp")
    pairs = tp_size & (tp_size - 1) == 0
    pairs = pairs and lax.axis_size("ctx") >= 4 and lax.axis_size("ctx") % 2 == 0
    whole_tiles = pairs and rows % (2 * SUBS) == 0 and channels % (tp_size * 2048) == 0
    whole_tiles = whole_tiles and decay_rate.shape[0] % (2 * SUBS) == 0
    plan = by_tokens if one_head_each and whole_tiles else by_channels
    return plan(hyena_in, attn_in, short_taps, decay_rate, residue, lengths)


def solution(mesh):
    placed = (
        P(("ctx", "tp"), None, None),
        P(("ctx", "tp"), None, None),
        P(None, None, "tp"),
        P(None, "tp"),
        P(None, "tp"),
        P(),
    )
    return jax.shard_map(
        per_device,
        mesh=mesh,
        in_specs=placed,
        out_specs=(P(("ctx", "tp"), None), P(("ctx", "tp"), None)),
        check_vma=False,
    )
```

```python
import functools
import math

import jax
import jax.numpy as jnp
from jax import lax
from jax.experimental import pallas as pl
from jax.experimental.pallas import tpu as pltpu
from jax.sharding import PartitionSpec as P

DH = 128
LANES = 128
SUBS = 8
ALL = ("ctx", "tp")
VMEM_BYTES = 60 * 1024 * 1024
ATTEND_BYTES = 32 * 1024 * 1024
MASKED = -1e30


def params_of(limit=VMEM_BYTES):
    return pltpu.CompilerParams(vmem_limit_bytes=limit)


def split_heads_kernel(x_ref, o_ref):
    for h in range(o_ref.shape[0]):
        o_ref[h] = x_ref[:, :, h * DH : (h + 1) * DH]


def split_heads(x, group=8):
    kinds, rows, width = x.shape
    heads = width // DH
    return pl.pallas_call(
        split_heads_kernel,
        grid=(heads // group,),
        in_specs=[pl.BlockSpec((kinds, rows, group * DH), lambda g: (0, 0, g))],
        out_specs=pl.BlockSpec((group, kinds, rows, DH), lambda g: (g, 0, 0, 0)),
        out_shape=jax.ShapeDtypeStruct((heads, kinds, rows, DH), x.dtype),
        compiler_params=params_of(),
        name="split_heads",
    )(x)


def join_heads_kernel(x_ref, o_ref):
    for h in range(x_ref.shape[0]):
        o_ref[:, h * DH : (h + 1) * DH] = x_ref[h]


def join_heads(x, group=8):
    heads, rows, _ = x.shape
    return pl.pallas_call(
        join_heads_kernel,
        grid=(heads // group,),
        in_specs=[pl.BlockSpec((group, rows, DH), lambda g: (g, 0, 0))],
        out_specs=pl.BlockSpec((rows, group * DH), lambda g: (0, g)),
        out_shape=jax.ShapeDtypeStruct((rows, heads * DH), x.dtype),
        compiler_params=params_of(ATTEND_BYTES),
        name="join_heads",
    )(x)


def attend_kernel(tile_start_ref, x_ref, start_ref, o_ref, q_s, k_s, v_s):
    tile = pl.program_id(0)
    blocks, _, rows, _ = x_ref.shape
    query_rows = o_ref.shape[0]
    scale = math.log2(math.e) / math.sqrt(DH)

    @pl.when(tile == 0)
    def _():
        @pl.loop(0, blocks)
        def _(b):
            place = pl.ds(pl.multiple_of(b * rows, rows), rows)
            q_s[place] = x_ref[b, 0]
            k_s[place] = x_ref[b, 1]
            v_s[place] = x_ref[b, 2]

    first_row = tile * query_rows
    q = q_s[pl.ds(pl.multiple_of(first_row, query_rows), query_rows)]
    start = jnp.concatenate([start_ref[...]] * (query_rows // LANES), axis=1)
    shape = (query_rows, query_rows)
    row = lax.broadcasted_iota(jnp.int32, shape, 0)
    col = lax.broadcasted_iota(jnp.int32, shape, 1)

    def step(i, carry, diagonal=False):
        top, denom, mixed = carry
        base = pl.multiple_of(i * query_rows, query_rows)
        k = k_s[pl.ds(base, query_rows)]
        v = v_s[pl.ds(base, query_rows)]
        s = lax.dot_general(q, k, (((1,), (1,)), ((), ())), preferred_element_type=jnp.float32)
        allowed = col >= start - base
        if diagonal:
            allowed = allowed & (col <= row)
        s = jnp.where(allowed, s, MASKED)
        new_top = jnp.maximum(top, jnp.max(s, axis=1, keepdims=True))
        p = jnp.exp2((s - new_top) * scale)
        rescale = jnp.exp2((top - new_top) * scale)
        denom = denom * rescale
        for c in range(query_rows // LANES):
            denom = denom + p[:, c * LANES : (c + 1) * LANES]
        mixed = mixed * rescale + jnp.dot(
            p.astype(jnp.bfloat16), v, preferred_element_type=jnp.float32
        )
        return new_top, denom, mixed

    carry = (
        jnp.full((query_rows, 1), MASKED, jnp.float32),
        jnp.zeros((query_rows, LANES), jnp.float32),
        jnp.zeros((query_rows, DH), jnp.float32),
    )
    carry = step(tile, carry, diagonal=True)
    _, denom, mixed = lax.fori_loop(tile_start_ref[tile] // query_rows, tile, step, carry)
    o_ref[...] = (mixed / jnp.sum(denom, axis=1, keepdims=True)).astype(o_ref.dtype)


def attend(x, start, query_rows=512):
    blocks, _, rows, _ = x.shape
    tokens = blocks * rows
    query_rows = math.gcd(tokens, query_rows)
    wide_start = jnp.broadcast_to(start[:, None], (tokens, LANES))
    return pl.pallas_call(
        attend_kernel,
        grid_spec=pltpu.PrefetchScalarGridSpec(
            num_scalar_prefetch=1,
            grid=(tokens // query_rows,),
            in_specs=[
                pl.BlockSpec(x.shape, lambda t, s: (0, 0, 0, 0)),
                pl.BlockSpec((query_rows, LANES), lambda t, s: (t, 0)),
            ],
            out_specs=pl.BlockSpec((query_rows, DH), lambda t, s: (t, 0)),
            scratch_shapes=[pltpu.VMEM((tokens, DH), x.dtype)] * 3,
        ),
        out_shape=jax.ShapeDtypeStruct((tokens, DH), x.dtype),
        compiler_params=params_of(ATTEND_BYTES),
        cost_estimate=pl.CostEstimate(
            flops=2 * tokens * tokens * DH,
            bytes_accessed=x.size * 2 + tokens * (DH * 2 + LANES * 4),
            transcendentals=tokens * tokens // 2,
        ),
        name="attend",
    )(start[::query_rows], x, wide_start)


def pick(k, refs, place):
    value = refs[0][place]
    for other in range(1, len(refs)):
        value = jnp.where(k == other, refs[other][place], value)
    return value


def wide(row):
    return jnp.broadcast_to(row, (SUBS, LANES))


def added(parts):
    while len(parts) > 1:
        parts = [a + b for a, b in zip(parts[::2], parts[1::2])] + (
            [parts[-1]] if len(parts) % 2 else []
        )
    return parts[0]


def filtered_runs(xs, i, taps, run):
    rim = len(taps) - 1
    seen = [xs[i, pl.ds(SUBS + j - rim, SUBS, stride=run)] for j in range(rim)]
    out = []
    for j in range(run):
        seen.append(xs[i, pl.ds(SUBS + j, SUBS, stride=run)])
        out.append(sum(taps[lag] * seen[-1 - lag] for lag in range(1, rim + 1)) + taps[0] * seen[-1])
    return out


def taps_of(k, parity, tables, modes, taps_count, kinds, spot):
    past = slice(modes, tables[0].shape[0])
    halves = [from_table(k, parity, tables, half, (past, spot)) for half in (0, 1)]
    cut = half_taps(taps_count * kinds)

    def tap(lag, i):
        half, r = divmod(lag * kinds + i, cut)
        return wide(halves[half][r : r + 1])

    return lambda i: [tap(lag, i) for lag in range(taps_count)]


def block_states_kernel(t_ref, x_ref, edge_ref, *refs, modes, taps_count, tp_size):
    tables, (source_ref, enter_ref) = refs[: 2 * tp_size], refs[2 * tp_size :][:2]
    ends, xs = refs[2 * tp_size + 2 : -1], refs[-1]
    kinds, rows, width = x_ref.shape
    k, chunk = pl.program_id(0), pl.program_id(1)
    run = rows // SUBS
    rim = taps_count - 1
    sub = lax.broadcasted_iota(jnp.int32, (SUBS, LANES), 0)
    for c in range(width // LANES):
        lanes = slice(c * LANES, (c + 1) * LANES)
        spot = pl.ds(pl.multiple_of(chunk * width + c * LANES, LANES), LANES)
        edge = edge_ref[:, lanes].astype(jnp.float32)
        for i in (1, 2):
            xs[i, SUBS - rim : SUBS] = edge[i * rim : (i + 1) * rim]
            xs[i, SUBS:] = x_ref[i, :, lanes].astype(jnp.float32)
        rate = from_table(k, t_ref[1], tables, 0, (slice(0, modes), spot))
        taps = taps_of(k, t_ref[1], tables, modes, taps_count, kinds, spot)
        decay = jnp.exp(-rate)
        decay_run = jnp.exp(rate * (-1.0 * run))
        source = [
            a * b
            for a, b in zip(filtered_runs(xs, 1, taps(1), run), filtered_runs(xs, 2, taps(2), run))
        ]
        for j in range(run):
            source_ref[j * SUBS : (j + 1) * SUBS, lanes] = source[j]

        decays = [wide(decay[n : n + 1]) for n in range(modes)]
        states = [source[0]] * modes
        for j in range(1, run):
            states = [state * d + source[j] for state, d in zip(states, decays)]
        spans = [wide(decay_run[n : n + 1]) for n in range(modes)]
        for hop in (1, 2, 4):
            states = [
                state + jnp.where(sub >= hop, span * pltpu.roll(state, hop, 0), 0.0)
                for state, span in zip(states, spans)
            ]
            spans = [span * span for span in spans]
        last = [state[SUBS - 1 : SUBS] for state in states]
        for n, state in enumerate(states):
            enter_ref[n * SUBS : (n + 1) * SUBS, lanes] = jnp.where(
                sub >= 1, pltpu.roll(state, 1, 0), 0.0
            )
        last = jnp.concatenate(last, axis=0)
        for other in range(tp_size):

            @pl.when(k == other)
            def _(other=other):
                ends[other][:, spot] = last


def inside_runs_kernel(t_ref, x_ref, edge_ref, source_ref, enter_ref, *refs, modes, taps_count, tp_size):
    tables, y_ref, q_ref, xs = refs[: 2 * tp_size], refs[-3], refs[-2], refs[-1]
    _, rows, width = x_ref.shape
    kinds = edge_ref.shape[0] // (taps_count - 1)
    k, chunk = pl.program_id(0), pl.program_id(1)
    run = rows // SUBS
    rim = taps_count - 1
    for c in range(width // LANES):
        lanes = slice(c * LANES, (c + 1) * LANES)
        spot = pl.ds(pl.multiple_of(chunk * width + c * LANES, LANES), LANES)
        xs[0, SUBS - rim : SUBS] = edge_ref[:, lanes].astype(jnp.float32)[0:rim]
        xs[0, SUBS:] = x_ref[0, :, lanes].astype(jnp.float32)
        rate = from_table(k, t_ref[1], tables, 0, (slice(0, modes), spot))
        weight = from_table(k, t_ref[1], tables, 1, (slice(0, modes), spot))
        taps = taps_of(k, t_ref[1], tables, modes, taps_count, kinds, spot)
        for j, value in enumerate(filtered_runs(xs, 0, taps(0), run)):
            q_ref[j * SUBS : (j + 1) * SUBS, lanes] = value
        decay = jnp.exp(-rate)
        power = weight
        lags = []
        for j in range(run):
            lags.append(wide(jnp.sum(power, axis=0, keepdims=True)))
            power = power * decay
        source = [source_ref[j * SUBS : (j + 1) * SUBS, lanes] for j in range(run)]
        weight = weight * decay
        terms = [
            enter_ref[n * SUBS : (n + 1) * SUBS, lanes] * wide(weight[n : n + 1])
            for n in range(modes)
        ]
        steps = [wide(decay[n : n + 1]) for n in range(modes)]
        for j in range(run):
            total = added(terms)
            for lag in range(j + 1):
                total = total + lags[lag] * source[j - lag]
            y_ref[j * SUBS : (j + 1) * SUBS, lanes] = total
            terms = [a * b for a, b in zip(terms, steps)]


def quarter_grid(tables, channels, width):
    tp_size = len(tables) // 2
    quarter = channels // tp_size
    chunks = quarter // width
    whole = lambda k, c, t: (0, 0)
    across = lambda k, c, t: (0, (k ^ t[0]) * chunks + c)
    return tp_size, quarter, (tp_size, chunks), whole, across


def block_states(t, x, edge, tables, modes, taps_count, width=2048):
    kinds, rows, channels = x.shape
    tp_size, quarter, grid, whole, across = quarter_grid(tables, channels, width)
    return pl.pallas_call(
        functools.partial(
            block_states_kernel, modes=modes, taps_count=taps_count, tp_size=tp_size
        ),
        grid_spec=pltpu.PrefetchScalarGridSpec(
            num_scalar_prefetch=1,
            grid=grid,
            in_specs=[
                pl.BlockSpec((kinds, rows, width), lambda k, c, t: (0, *across(k, c, t))),
                pl.BlockSpec((edge.shape[0], width), across),
            ]
            + [pl.BlockSpec(tables[0].shape, whole)] * len(tables),
            out_specs=[pl.BlockSpec((rows, width), across), pl.BlockSpec((modes * SUBS, width), across)]
            + [pl.BlockSpec((modes, quarter), whole)] * tp_size,
            scratch_shapes=[pltpu.VMEM((kinds, rows + SUBS, LANES), jnp.float32)],
        ),
        out_shape=[
            jax.ShapeDtypeStruct((rows, channels), jnp.float32),
            jax.ShapeDtypeStruct((modes * SUBS, channels), jnp.float32),
        ]
        + [jax.ShapeDtypeStruct((modes, quarter), jnp.float32)] * tp_size,
        compiler_params=params_of(),
        cost_estimate=pl.CostEstimate(
            flops=rows * channels * 50,
            bytes_accessed=rows * channels * 14,
            transcendentals=2 * modes * channels,
        ),
        name="block_states",
    )(t, x, edge, *tables)


def inside_runs(t, x, edge, source, enter, tables, modes, taps_count, width=2048):
    _, rows, channels = x.shape
    tp_size, _, grid, whole, across = quarter_grid(tables, channels, width)
    return pl.pallas_call(
        functools.partial(inside_runs_kernel, modes=modes, taps_count=taps_count, tp_size=tp_size),
        grid_spec=pltpu.PrefetchScalarGridSpec(
            num_scalar_prefetch=1,
            grid=grid,
            in_specs=[
                pl.BlockSpec((1, rows, width), lambda k, c, t: (0, *across(k, c, t))),
                pl.BlockSpec((edge.shape[0], width), across),
                pl.BlockSpec((rows, width), across),
                pl.BlockSpec((enter.shape[0], width), across),
            ]
            + [pl.BlockSpec(tables[0].shape, whole)] * len(tables),
            out_specs=[pl.BlockSpec((rows, width), across)] * 2,
            scratch_shapes=[pltpu.VMEM((1, rows + SUBS, LANES), jnp.float32)],
        ),
        out_shape=[jax.ShapeDtypeStruct((rows, channels), jnp.float32)] * 2,
        compiler_params=params_of(),
        cost_estimate=pl.CostEstimate(
            flops=rows * channels * 25,
            bytes_accessed=rows * channels * 14,
            transcendentals=modes * channels,
        ),
        name="inside_runs",
    )(t, x, edge, source, enter, *tables)


def half_taps(taps_rows):
    return (taps_rows + 1) // 2


def half_rows(modes, taps_rows):
    return -(-(modes + half_taps(taps_rows)) // SUBS) * SUBS


def table_kernel(parity_ref, taps_ref, rate_ref, residue_ref, mine_ref, other_ref):
    lags, kinds, _ = taps_ref.shape
    modes = rate_ref.shape[0]
    rate = rate_ref[...]
    x = 2.0 * rate
    series = jnp.ones_like(x)
    for term in range(10, 1, -1):
        series = 1.0 - series * x * (1.0 / term)
    lost = jnp.where(x < 0.5, x * series, 1.0 - jnp.exp(-x))
    weight = residue_ref[...] * jnp.sqrt(lost)
    rows = [taps_ref[r // kinds, r % kinds : r % kinds + 1] for r in range(lags * kinds)]
    cut = half_taps(len(rows))

    def fill(lower_ref, upper_ref):
        lower_ref[0:modes] = rate
        upper_ref[0:modes] = weight
        for r, row in enumerate(rows):
            ref, place = (lower_ref, r) if r < cut else (upper_ref, r - cut)
            ref[modes + place : modes + place + 1] = row
        for ref, used in ((lower_ref, modes + cut), (upper_ref, modes + len(rows) - cut)):
            ref[used:] = jnp.zeros((ref.shape[0] - used, ref.shape[1]), jnp.float32)

    @pl.when(parity_ref[0] == 0)
    def _():
        fill(mine_ref, other_ref)

    @pl.when(parity_ref[0] == 1)
    def _():
        fill(other_ref, mine_ref)


def make_table(parity, taps, rate, residue):
    height = half_rows(rate.shape[0], taps.shape[0] * taps.shape[1])
    vmem = pl.BlockSpec(memory_space=pltpu.VMEM)
    return pl.pallas_call(
        table_kernel,
        in_specs=[pl.BlockSpec(memory_space=pltpu.SMEM)] + [vmem] * 3,
        out_specs=[vmem] * 2,
        out_shape=[jax.ShapeDtypeStruct((height, rate.shape[1]), jnp.float32)] * 2,
        compiler_params=params_of(),
        name="make_table",
    )(parity, taps, rate, residue)


def from_table(k, parity, tables, half, place):
    size = len(tables) // 2
    ordered = [
        jnp.where(parity == half, tables[i][place], tables[size + i][place]) for i in range(size)
    ]
    value = ordered[0]
    for other in range(1, size):
        value = jnp.where(k == other, ordered[other], value)
    return value


def block_end_kernel(t_ref, rate_ref, *refs, rows):
    ends, o_ref = refs[:-1], refs[-1]
    rate = rate_ref[...]
    total = jnp.zeros_like(rate)
    for k, end in enumerate(ends):
        later = len(ends) - 1 - (k ^ t_ref[0])
        total = total + jnp.exp(rate * (later * -rows).astype(jnp.float32)) * end[...]
    o_ref[...] = total


def pair_enters_kernel(t_ref, rate_ref, *refs, rows):
    seen, o_ref = refs[:-1], refs[-1]
    half = o_ref.shape[0]
    rate = jnp.where(t_ref[1] == 1, rate_ref[half:], rate_ref[:half])
    span = jnp.exp(rate * (-2.0 * rows))
    total = seen[-1][...]
    for one in seen[-2::-1]:
        total = total * span + one[...]
    o_ref[...] = total


def pair_kernel(t_ref, rate_ref, own_ref, mate_ref, *refs, rows):
    size = len(refs) // 2
    ends, total_ref, outs = refs[:size], refs[size], refs[size + 1 :]
    t, odd = t_ref[0], t_ref[1] == 1
    rate, own, mate = rate_ref[...], own_ref[...], mate_ref[...]
    first, second = jnp.where(odd, mate, own), jnp.where(odd, own, mate)
    total = first * jnp.exp(rate * (-1.0 * rows * size)) + second
    half = total_ref.shape[0]
    total_ref[...] = jnp.where(odd, total[half:], total[:half])
    span = jnp.exp(rate * (-1.0 * rows))
    state = jnp.where(odd, mate, 0.0)
    for place in range(size):
        mine = place ^ t
        for k in range(size):

            @pl.when(mine == k)
            def _(k=k, state=state):
                outs[k][...] = state

        end = pick(mine, ends, Ellipsis)
        state = state * span + end


def small_call(kernel, t, name, heights, *arrays, **sizes):
    vmem = pl.BlockSpec(memory_space=pltpu.VMEM)
    return pl.pallas_call(
        functools.partial(kernel, **sizes),
        in_specs=[pl.BlockSpec(memory_space=pltpu.SMEM)] + [vmem] * len(arrays),
        out_specs=[vmem] * len(heights),
        out_shape=[jax.ShapeDtypeStruct((h, arrays[0].shape[1]), jnp.float32) for h in heights],
        compiler_params=params_of(),
        name=name,
    )(t, *arrays)


def add_entering_kernel(t_ref, y_ref, q_ref, *refs, modes, size, tp_size):
    o_ref, out_s = refs[-2:]
    inside, mine_enters, other_enters, mines, others = (
        refs[i * size : (i + 1) * size] for i in range(5)
    )
    k = pl.program_id(0)
    blocks_before = t_ref[1] * tp_size + t_ref[0]
    rows, width = y_ref.shape
    run = rows // SUBS
    even = t_ref[1] == 0
    before = lax.broadcasted_iota(jnp.int32, (SUBS, LANES), 0).astype(jnp.float32) * (-1.0 * run)
    for c in range(width // LANES):
        lanes = slice(c * LANES, (c + 1) * LANES)
        mine, other = (pick(k, half, (slice(0, modes), lanes)) for half in (mines, others))
        rate, weight = jnp.where(even, mine, other), jnp.where(even, other, mine)
        decay = jnp.exp(-rate)
        one = (slice(0, modes // 2), lanes)
        mine, other = pick(k, mine_enters, one), pick(k, other_enters, one)
        enters = jnp.concatenate(
            [jnp.where(even, mine, other), jnp.where(even, other, mine)], axis=0
        )
        state = enters * jnp.exp(rate * (blocks_before * -rows).astype(jnp.float32))
        state = (state + pick(k, inside, (slice(0, modes), lanes))) * weight * decay
        terms, steps = [], []
        for n in range(modes):
            terms.append(jnp.exp(before * rate[n : n + 1]) * state[n : n + 1])
            steps.append(wide(decay[n : n + 1]))
        for j in range(run):
            place = slice(j * SUBS, (j + 1) * SUBS)
            out_s[pl.ds(j, SUBS, stride=run)] = q_ref[place, lanes] * (y_ref[place, lanes] + added(terms))
            terms = [a * b for a, b in zip(terms, steps)]
        o_ref[:, lanes] = out_s[...].astype(o_ref.dtype)


def add_entering(t, first, y, q, families, before, modes, width=2048):
    rows, channels = y.shape
    size, quarter = len(families[0]), families[0][0].shape[1]
    chunks = quarter // width
    arrays = [a for family in families for a in family]
    there = lambda k, c, t: (0, ((k + first) ^ t[0]) * chunks + c)
    across = lambda k, c, t: (0, c)
    old = [] if before is None else [before]
    return pl.pallas_call(
        functools.partial(
            add_entering_kernel, modes=modes, size=size, tp_size=channels // quarter
        ),
        grid_spec=pltpu.PrefetchScalarGridSpec(
            num_scalar_prefetch=1,
            grid=(size, chunks),
            in_specs=[pl.BlockSpec((rows, width), there)] * 2
            + [pl.BlockSpec((a.shape[0], width), across) for a in arrays]
            + [pl.BlockSpec(memory_space=pl.ANY)] * len(old),
            out_specs=pl.BlockSpec((rows, width), there),
            scratch_shapes=[pltpu.VMEM((rows, LANES), jnp.float32)],
        ),
        out_shape=jax.ShapeDtypeStruct((rows, channels), jnp.bfloat16),
        input_output_aliases={3 + len(arrays): 0} if old else {},
        compiler_params=params_of(),
        cost_estimate=pl.CostEstimate(
            flops=size * rows * quarter * 36,
            bytes_accessed=size * rows * quarter * 10,
            transcendentals=size * modes * quarter * 9,
        ),
        name="add_entering",
    )(t, y, q, *arrays, *old)


def exchange(x, axis):
    return lax.all_to_all(x, axis, split_axis=0, concat_axis=0, tiled=True)


def trade_tp(arrays):
    size = len(arrays)
    return [arrays[0]] + [
        lax.ppermute(arrays[k], "tp", [(i, i ^ k) for i in range(size)]) for k in range(1, size)
    ]


def segment_starts(lengths, tokens):
    order = jnp.arange(lengths.shape[0], dtype=jnp.int32)
    ends = jnp.sum(jnp.where(order[:, None] <= order[None, :], lengths[:, None], 0), axis=0)
    position = jnp.arange(tokens, dtype=jnp.int32)
    passed = jnp.where(ends[None, :] <= position[:, None], ends[None, :], 0)
    return jnp.max(passed, axis=1)


def by_tokens(hyena_in, attn_in, short_taps, decay_rate, residue, lengths):
    rows, kinds, channels = hyena_in.shape
    ctx_size, tp_size = lax.axis_size("ctx"), lax.axis_size("tp")
    devices = ctx_size * tp_size
    taps_count = short_taps.shape[0]
    modes = decay_rate.shape[0]
    parity = (lax.axis_index("ctx") % 2).astype(jnp.int32)
    t = jnp.stack([lax.axis_index("tp").astype(jnp.int32), parity])
    swap = [(i, i ^ 1) for i in range(ctx_size)]

    x = jnp.transpose(hyena_in, (1, 0, 2))
    edge = x[:, rows - taps_count + 1 :].reshape(kinds * (taps_count - 1), channels)
    edge = lax.ppermute(edge, ALL, [(i, i + 1) for i in range(devices - 1)])
    mine, other = make_table(parity.reshape(1), short_taps, decay_rate, residue)
    mine = trade_tp([mine] * tp_size)
    heads_out = split_heads(jnp.transpose(attn_in, (1, 0, 2)))
    heads_out, edge, *mine = lax.optimization_barrier((heads_out, edge, *mine))
    by_head = exchange(heads_out, ALL)
    tables = mine + [other] + [lax.ppermute(half, "ctx", swap) for half in mine[1:]]
    source, enter, *ends = block_states(t, x, edge, tables, modes, taps_count)
    y, q = inside_runs(t, x, edge, source, enter, tables, modes, taps_count)
    y, *ends = lax.optimization_barrier((y, *trade_tp(ends)))
    [block_end] = small_call(
        block_end_kernel, t, "block_end", [modes], decay_rate, *ends, rows=rows
    )

    mate = lax.ppermute(block_end, "ctx", swap)
    total, *inside = small_call(
        pair_kernel, t, "pair", [modes // 2] + [modes] * tp_size,
        decay_rate, block_end, mate, *ends, rows=rows,
    )
    by_head, *_ = lax.optimization_barrier((by_head, *inside, total))
    inside = trade_tp(inside)
    total, inside[1] = lax.optimization_barrier((total, inside[1]))
    seen = [
        lax.ppermute(total, "ctx", [(i, i + hop) for i in range(ctx_size - hop)])
        for hop in range(2, ctx_size, 2)
    ]

    mixed = attend(by_head, segment_starts(lengths, rows * devices))
    mixed, seen, inside = lax.optimization_barrier((mixed, seen, inside))
    [enters] = small_call(
        pair_enters_kernel, t, "pair_enters", [modes // 2], decay_rate, *seen, rows=rows * tp_size
    )
    mate_enters = lax.ppermute(enters, "ctx", swap)
    enters = trade_tp([enters] * tp_size)
    attn_out = join_heads(exchange(mixed.reshape(devices, rows, DH), ALL))
    mines, others = tables[:tp_size], tables[tp_size:]
    own = inside[:1], enters[:1], [mate_enters], mines[:1], others[:1]
    hyena_out = add_entering(t, 0, y, q, own, None, modes)
    hyena_out, *enters = lax.optimization_barrier((hyena_out, *enters[1:]))
    mate_enters = [lax.ppermute(half, "ctx", swap) for half in enters]
    rest = inside[1:], enters, mate_enters, mines[1:], others[1:]
    hyena_out = add_entering(t, 1, y, q, rest, hyena_out, modes)
    return hyena_out, attn_out


exact_mode = lax.Precision.HIGHEST


def from_behind(block, axis, distance):
    devices = range(lax.axis_size(axis))
    route = [(i - distance, i) for i in devices if i - distance in devices]
    return lax.ppermute(block, axis, route)


def carried_in(part, axis, combine, identity):
    place = lax.axis_index(axis)
    gathered = jax.tree.map(lambda a: lax.all_gather(a, axis), part)
    state = jax.tree.map(lambda a, e: jnp.zeros_like(a) + jnp.asarray(e, a.dtype), part, identity)

    def one(lap, state):
        return combine(
            state, jax.tree.map(lambda a: lax.dynamic_index_in_dim(a, lap, 0, False), gathered)
        )

    return lax.fori_loop(0, place, one, state)


def segment_of(positions, segment_ends):
    return jnp.sum((segment_ends[None, :] <= positions[:, None]).astype(jnp.int32), axis=1)


def by_channels(hyena_in, attn_in, short_taps, decay_rate, residue, lengths):
    hyena_cols, attention_cols = (
        lax.all_to_all(hyena_in, "tp", split_axis=2, concat_axis=0, tiled=True),
        lax.all_to_all(attn_in, "tp", split_axis=2, concat_axis=0, tiled=True),
    )
    block_rows = hyena_cols.shape[0]
    rim_rows = short_taps.shape[0] - 1
    edge_rows = from_behind(hyena_cols[block_rows - rim_rows :], "ctx", 1)
    extended = jnp.concatenate([edge_rows, hyena_cols], axis=0).astype(jnp.float32)
    filtered = jnp.zeros(hyena_cols.shape, jnp.float32)
    for lag in range(rim_rows + 1):
        filtered = (
            filtered + short_taps[lag] * extended[rim_rows - lag : rim_rows - lag + block_rows]
        )
    query_side = filtered[:, 0]
    source = filtered[:, 1] * filtered[:, 2]
    channels = source.shape[1]
    weight = residue * jnp.sqrt(-jnp.expm1(-2.0 * decay_rate))
    sub_length = math.gcd(32, block_rows)
    pieces = block_rows // sub_length
    offsets = jnp.arange(sub_length, dtype=jnp.float32)
    powers = jnp.exp(-offsets[:, None, None] * decay_rate[None])
    lag_values = jnp.einsum("onc,nc->oc", powers, weight, precision=exact_mode)
    lag_index = jnp.arange(sub_length, dtype=jnp.int32)
    selector = (
        lag_index[:, None, None] - lag_index[None, :, None] == lag_index[None, None, :]
    ).astype(jnp.float32)
    toeplitz = jnp.einsum("tso,oc->tsc", selector, lag_values, precision=exact_mode)
    grouped = source.reshape(pieces, sub_length, channels)
    inner = jnp.einsum("tsc,bsc->btc", toeplitz, grouped, precision=exact_mode)
    tail_powers = jnp.exp(-(sub_length - 1.0 - offsets)[:, None, None] * decay_rate[None])
    own_states = jnp.einsum("snc,bsc->bnc", tail_powers, grouped, precision=exact_mode)
    sub_decay = jnp.exp(-sub_length * decay_rate)

    def carry_states(carried, incoming):
        return (sub_decay * carried + incoming, carried)

    local_end, entering = lax.scan(carry_states, jnp.zeros_like(sub_decay), own_states)
    block_decay = jnp.exp(-block_rows * decay_rate)

    def combine(earlier, later):
        return (earlier[0] * later[0], later[0] * earlier[1] + later[1])

    _, arriving = carried_in(
        (block_decay, local_end),
        "ctx",
        combine,
        (jnp.ones_like(block_decay), jnp.zeros_like(local_end)),
    )
    starts = jnp.arange(pieces, dtype=jnp.float32) * sub_length
    all_entering = entering + jnp.exp(-starts[:, None, None] * decay_rate[None]) * arriving[None]
    rise_powers = jnp.exp(-(offsets + 1.0)[:, None, None] * decay_rate[None]) * weight[None]
    from_state = jnp.einsum("tnc,bnc->btc", rise_powers, all_entering, precision=exact_mode)
    long_conv = (inner + from_state).reshape(block_rows, channels)
    hyena_local = (query_side * long_conv).astype(jnp.bfloat16)
    head_cols = attention_cols.shape[2]
    local_heads = head_cols // DH
    queries = attention_cols[:, 0].reshape(block_rows, local_heads, DH)
    keyvals = attention_cols[:, 1:3]
    order = jnp.arange(lengths.shape[0], dtype=jnp.int32)
    segment_ends = jnp.sum(jnp.where(order[:, None] <= order[None, :], lengths[:, None], 0), axis=0)
    block_index = lax.axis_index("ctx")
    query_pos = block_index * block_rows + jnp.arange(block_rows, dtype=jnp.int32)
    query_seg = segment_of(query_pos, segment_ends)
    score_scale = 1.0 / math.sqrt(DH)

    def attend_part(softmax_state, part, key_start):
        count = part.shape[0]
        key_pos = key_start + jnp.arange(count, dtype=jnp.int32)
        key_seg = segment_of(key_pos, segment_ends)
        allowed = (
            (key_pos[None, :] <= query_pos[:, None])
            & (key_seg[None, :] == query_seg[:, None])
            & (key_pos >= 0)[None, :]
        )

        def compute(carried):
            row_top, denom, weighted = carried
            key_rows = part[:, 0].reshape(count, local_heads, DH)
            value_rows = part[:, 1].reshape(count, local_heads, DH)
            scores = (
                jnp.einsum("qhd,khd->hqk", queries, key_rows, preferred_element_type=jnp.float32)
                * score_scale
            )
            masked = jnp.where(allowed[None], scores, jnp.float32(-1e30))
            new_top = jnp.maximum(row_top, jnp.max(masked, axis=2))
            expo = jnp.where(allowed[None], jnp.exp(scores - new_top[:, :, None]), jnp.float32(0.0))
            rescale = jnp.exp(row_top - new_top)
            denom = denom * rescale + jnp.sum(expo, axis=2)
            probs = expo.astype(jnp.bfloat16)
            added = jnp.einsum(
                "hqk,khd->qhd", probs, value_rows, preferred_element_type=jnp.float32
            )
            weighted = weighted * jnp.transpose(rescale)[:, :, None] + added
            return (new_top, denom, weighted)

        def keep(carried):
            return carried

        return lax.cond(jnp.any(allowed), compute, keep, softmax_state)

    initial = (
        jnp.full((local_heads, block_rows), -1e30, jnp.float32),
        jnp.zeros((local_heads, block_rows), jnp.float32),
        jnp.zeros((block_rows, local_heads, DH), jnp.float32),
    )
    piece = lax.all_gather(keyvals, "ctx", axis=0, tiled=True)
    rows = piece.shape[0]
    step_rows = math.gcd(rows, 512)

    def advance(count, carried):
        part = lax.dynamic_slice_in_dim(piece, count * step_rows, step_rows, 0)
        return attend_part(carried, part, count * step_rows)

    final_state = lax.fori_loop(0, rows // step_rows, advance, initial)
    _, denom, weighted = final_state
    attention_local = (
        (weighted / jnp.transpose(denom)[:, :, None])
        .reshape(block_rows, head_cols)
        .astype(jnp.bfloat16)
    )
    hyena_out, attn_out = (
        lax.all_to_all(hyena_local, "tp", split_axis=0, concat_axis=1, tiled=True),
        lax.all_to_all(attention_local, "tp", split_axis=0, concat_axis=1, tiled=True),
    )
    return (hyena_out, attn_out)


def per_device(hyena_in, attn_in, short_taps, decay_rate, residue, lengths):
    rows, _, channels = hyena_in.shape
    devices = lax.axis_size("ctx") * lax.axis_size("tp")
    one_head_each = attn_in.shape[2] == devices * DH
    tp_size = lax.axis_size("tp")
    pairs = tp_size & (tp_size - 1) == 0
    pairs = pairs and lax.axis_size("ctx") >= 4 and lax.axis_size("ctx") % 2 == 0
    whole_tiles = pairs and rows % (2 * SUBS) == 0 and channels % (tp_size * 2048) == 0
    whole_tiles = whole_tiles and decay_rate.shape[0] % (2 * SUBS) == 0
    plan = by_tokens if one_head_each and whole_tiles else by_channels
    return plan(hyena_in, attn_in, short_taps, decay_rate, residue, lengths)


def solution(mesh):
    placed = (
        P(("ctx", "tp"), None, None),
        P(("ctx", "tp"), None, None),
        P(None, None, "tp"),
        P(None, "tp"),
        P(None, "tp"),
        P(),
    )
    return jax.shard_map(
        per_device,
        mesh=mesh,
        in_specs=placed,
        out_specs=(P(("ctx", "tp"), None), P(("ctx", "tp"), None)),
        check_vma=False,
    )
```

```python
import functools
import math

import jax
import jax.numpy as jnp
from jax import lax
from jax.experimental import pallas as pl
from jax.experimental.pallas import tpu as pltpu
from jax.sharding import PartitionSpec as P

DH = 128
LANES = 128
SUBS = 8
ALL = ("ctx", "tp")
VMEM_BYTES = 60 * 1024 * 1024
ATTEND_BYTES = 32 * 1024 * 1024
SMALL_BYTES = 16 * 1024 * 1024
MASKED = -1e30


def params_of(limit=VMEM_BYTES):
    return pltpu.CompilerParams(vmem_limit_bytes=limit)


def split_heads_kernel(x_ref, o_ref):
    for h in range(o_ref.shape[0]):
        o_ref[h] = x_ref[:, :, h * DH : (h + 1) * DH]


def split_heads(x, group=8):
    kinds, rows, width = x.shape
    heads = width // DH
    return pl.pallas_call(
        split_heads_kernel,
        grid=(heads // group,),
        in_specs=[pl.BlockSpec((kinds, rows, group * DH), lambda g: (0, 0, g))],
        out_specs=pl.BlockSpec((group, kinds, rows, DH), lambda g: (g, 0, 0, 0)),
        out_shape=jax.ShapeDtypeStruct((heads, kinds, rows, DH), x.dtype),
        compiler_params=params_of(),
        name="split_heads",
    )(x)


def join_heads_kernel(x_ref, o_ref):
    for h in range(x_ref.shape[0]):
        o_ref[:, h * DH : (h + 1) * DH] = x_ref[h]


def join_heads(x, group=8):
    heads, rows, _ = x.shape
    return pl.pallas_call(
        join_heads_kernel,
        grid=(heads // group,),
        in_specs=[pl.BlockSpec((group, rows, DH), lambda g: (g, 0, 0))],
        out_specs=pl.BlockSpec((rows, group * DH), lambda g: (0, g)),
        out_shape=jax.ShapeDtypeStruct((rows, heads * DH), x.dtype),
        compiler_params=params_of(ATTEND_BYTES),
        name="join_heads",
    )(x)


def attend_kernel(tile_start_ref, x_ref, start_ref, o_ref, q_s, k_s, v_s):
    tile = pl.program_id(0)
    blocks, _, rows, _ = x_ref.shape
    query_rows = o_ref.shape[0]
    scale = math.log2(math.e) / math.sqrt(DH)

    @pl.when(tile == 0)
    def _():
        @pl.loop(0, blocks)
        def _(b):
            place = pl.ds(pl.multiple_of(b * rows, rows), rows)
            q_s[place] = x_ref[b, 0]
            k_s[place] = x_ref[b, 1]
            v_s[place] = x_ref[b, 2]

    first_row = tile * query_rows
    q = q_s[pl.ds(pl.multiple_of(first_row, query_rows), query_rows)]
    start = jnp.concatenate([start_ref[...]] * (query_rows // LANES), axis=1)
    shape = (query_rows, query_rows)
    row = lax.broadcasted_iota(jnp.int32, shape, 0)
    col = lax.broadcasted_iota(jnp.int32, shape, 1)

    def step(i, carry, diagonal=False):
        top, denom, mixed = carry
        base = pl.multiple_of(i * query_rows, query_rows)
        k = k_s[pl.ds(base, query_rows)]
        v = v_s[pl.ds(base, query_rows)]
        s = lax.dot_general(q, k, (((1,), (1,)), ((), ())), preferred_element_type=jnp.float32)
        allowed = col >= start - base
        if diagonal:
            allowed = allowed & (col <= row)
        s = jnp.where(allowed, s, MASKED)
        new_top = jnp.maximum(top, jnp.max(s, axis=1, keepdims=True))
        p = jnp.exp2((s - new_top) * scale)
        rescale = jnp.exp2((top - new_top) * scale)
        denom = denom * rescale
        for c in range(query_rows // LANES):
            denom = denom + p[:, c * LANES : (c + 1) * LANES]
        mixed = mixed * rescale + jnp.dot(
            p.astype(jnp.bfloat16), v, preferred_element_type=jnp.float32
        )
        return new_top, denom, mixed

    carry = (
        jnp.full((query_rows, 1), MASKED, jnp.float32),
        jnp.zeros((query_rows, LANES), jnp.float32),
        jnp.zeros((query_rows, DH), jnp.float32),
    )
    carry = step(tile, carry, diagonal=True)
    _, denom, mixed = lax.fori_loop(tile_start_ref[tile] // query_rows, tile, step, carry)
    o_ref[...] = (mixed / jnp.sum(denom, axis=1, keepdims=True)).astype(o_ref.dtype)


def attend(x, start, query_rows=512):
    blocks, _, rows, _ = x.shape
    tokens = blocks * rows
    query_rows = math.gcd(tokens, query_rows)
    wide_start = jnp.broadcast_to(start[:, None], (tokens, LANES))
    return pl.pallas_call(
        attend_kernel,
        grid_spec=pltpu.PrefetchScalarGridSpec(
            num_scalar_prefetch=1,
            grid=(tokens // query_rows,),
            in_specs=[
                pl.BlockSpec(x.shape, lambda t, s: (0, 0, 0, 0)),
                pl.BlockSpec((query_rows, LANES), lambda t, s: (t, 0)),
            ],
            out_specs=pl.BlockSpec((query_rows, DH), lambda t, s: (t, 0)),
            scratch_shapes=[pltpu.VMEM((tokens, DH), x.dtype)] * 3,
        ),
        out_shape=jax.ShapeDtypeStruct((tokens, DH), x.dtype),
        compiler_params=params_of(ATTEND_BYTES),
        cost_estimate=pl.CostEstimate(
            flops=2 * tokens * tokens * DH,
            bytes_accessed=x.size * 2 + tokens * (DH * 2 + LANES * 4),
            transcendentals=tokens * tokens // 2,
        ),
        name="attend",
    )(start[::query_rows], x, wide_start)


def pick(k, refs, place):
    value = refs[0][place]
    for other in range(1, len(refs)):
        value = jnp.where(k == other, refs[other][place], value)
    return value


def wide(row):
    return jnp.broadcast_to(row, (SUBS, LANES))


def added(parts):
    while len(parts) > 1:
        parts = [a + b for a, b in zip(parts[::2], parts[1::2])] + (
            [parts[-1]] if len(parts) % 2 else []
        )
    return parts[0]


def filtered_runs(xs, i, taps, run):
    rim = len(taps) - 1
    seen = [xs[i, pl.ds(SUBS + j - rim, SUBS, stride=run)] for j in range(rim)]
    out = []
    for j in range(run):
        seen.append(xs[i, pl.ds(SUBS + j, SUBS, stride=run)])
        out.append(sum(taps[lag] * seen[-1 - lag] for lag in range(1, rim + 1)) + taps[0] * seen[-1])
    return out


def taps_of(k, parity, tables, modes, taps_count, kinds, spot):
    past = slice(modes, tables[0].shape[0])
    halves = [from_table(k, parity, tables, half, (past, spot)) for half in (0, 1)]
    cut = half_taps(taps_count * kinds)

    def tap(lag, i):
        half, r = divmod(lag * kinds + i, cut)
        return wide(halves[half][r : r + 1])

    return lambda i: [tap(lag, i) for lag in range(taps_count)]


def block_states_kernel(t_ref, x_ref, edge_ref, *refs, modes, taps_count, tp_size):
    tables, (source_ref, enter_ref) = refs[: 2 * tp_size], refs[2 * tp_size :][:2]
    ends, xs = refs[2 * tp_size + 2 : -1], refs[-1]
    kinds, rows, width = x_ref.shape
    k, chunk = pl.program_id(0), pl.program_id(1)
    run = rows // SUBS
    rim = taps_count - 1
    sub = lax.broadcasted_iota(jnp.int32, (SUBS, LANES), 0)
    for c in range(width // LANES):
        lanes = slice(c * LANES, (c + 1) * LANES)
        spot = pl.ds(pl.multiple_of(chunk * width + c * LANES, LANES), LANES)
        edge = edge_ref[:, lanes].astype(jnp.float32)
        for i in (1, 2):
            xs[i, SUBS - rim : SUBS] = edge[i * rim : (i + 1) * rim]
            xs[i, SUBS:] = x_ref[i, :, lanes].astype(jnp.float32)
        rate = from_table(k, t_ref[1], tables, 0, (slice(0, modes), spot))
        taps = taps_of(k, t_ref[1], tables, modes, taps_count, kinds, spot)
        decay = jnp.exp(-rate)
        decay_run = jnp.exp(rate * (-1.0 * run))
        source = [
            a * b
            for a, b in zip(filtered_runs(xs, 1, taps(1), run), filtered_runs(xs, 2, taps(2), run))
        ]
        for j in range(run):
            source_ref[j * SUBS : (j + 1) * SUBS, lanes] = source[j]

        decays = [wide(decay[n : n + 1]) for n in range(modes)]
        states = [source[0]] * modes
        for j in range(1, run):
            states = [state * d + source[j] for state, d in zip(states, decays)]
        spans = [wide(decay_run[n : n + 1]) for n in range(modes)]
        for hop in (1, 2, 4):
            states = [
                state + jnp.where(sub >= hop, span * pltpu.roll(state, hop, 0), 0.0)
                for state, span in zip(states, spans)
            ]
            spans = [span * span for span in spans]
        last = [state[SUBS - 1 : SUBS] for state in states]
        for n, state in enumerate(states):
            enter_ref[n * SUBS : (n + 1) * SUBS, lanes] = jnp.where(
                sub >= 1, pltpu.roll(state, 1, 0), 0.0
            )
        last = jnp.concatenate(last, axis=0)
        for other in range(tp_size):

            @pl.when(k == other)
            def _(other=other):
                ends[other][:, spot] = last


def inside_runs_kernel(t_ref, x_ref, edge_ref, source_ref, enter_ref, *refs, modes, taps_count, tp_size):
    tables, y_ref, q_ref, xs = refs[: 2 * tp_size], refs[-3], refs[-2], refs[-1]
    _, rows, width = x_ref.shape
    kinds = edge_ref.shape[0] // (taps_count - 1)
    k, chunk = pl.program_id(0), pl.program_id(1)
    run = rows // SUBS
    rim = taps_count - 1
    for c in range(width // LANES):
        lanes = slice(c * LANES, (c + 1) * LANES)
        spot = pl.ds(pl.multiple_of(chunk * width + c * LANES, LANES), LANES)
        xs[0, SUBS - rim : SUBS] = edge_ref[:, lanes].astype(jnp.float32)[0:rim]
        xs[0, SUBS:] = x_ref[0, :, lanes].astype(jnp.float32)
        rate = from_table(k, t_ref[1], tables, 0, (slice(0, modes), spot))
        weight = from_table(k, t_ref[1], tables, 1, (slice(0, modes), spot))
        taps = taps_of(k, t_ref[1], tables, modes, taps_count, kinds, spot)
        for j, value in enumerate(filtered_runs(xs, 0, taps(0), run)):
            q_ref[j * SUBS : (j + 1) * SUBS, lanes] = value
        decay = jnp.exp(-rate)
        power = weight
        lags = []
        for j in range(run):
            lags.append(wide(jnp.sum(power, axis=0, keepdims=True)))
            power = power * decay
        source = [source_ref[j * SUBS : (j + 1) * SUBS, lanes] for j in range(run)]
        weight = weight * decay
        terms = [
            enter_ref[n * SUBS : (n + 1) * SUBS, lanes] * wide(weight[n : n + 1])
            for n in range(modes)
        ]
        steps = [wide(decay[n : n + 1]) for n in range(modes)]
        for j in range(run):
            total = added(terms)
            for lag in range(j + 1):
                total = total + lags[lag] * source[j - lag]
            y_ref[j * SUBS : (j + 1) * SUBS, lanes] = total
            terms = [a * b for a, b in zip(terms, steps)]


def quarter_grid(tables, channels, width):
    tp_size = len(tables) // 2
    quarter = channels // tp_size
    chunks = quarter // width
    whole = lambda k, c, t: (0, 0)
    across = lambda k, c, t: (0, (k ^ t[0]) * chunks + c)
    return tp_size, quarter, (tp_size, chunks), whole, across


def block_states(t, x, edge, tables, modes, taps_count, width=2048):
    kinds, rows, channels = x.shape
    tp_size, quarter, grid, whole, across = quarter_grid(tables, channels, width)
    return pl.pallas_call(
        functools.partial(
            block_states_kernel, modes=modes, taps_count=taps_count, tp_size=tp_size
        ),
        grid_spec=pltpu.PrefetchScalarGridSpec(
            num_scalar_prefetch=1,
            grid=grid,
            in_specs=[
                pl.BlockSpec((kinds, rows, width), lambda k, c, t: (0, *across(k, c, t))),
                pl.BlockSpec((edge.shape[0], width), across),
            ]
            + [pl.BlockSpec(tables[0].shape, whole)] * len(tables),
            out_specs=[pl.BlockSpec((rows, width), across), pl.BlockSpec((modes * SUBS, width), across)]
            + [pl.BlockSpec((modes, quarter), whole)] * tp_size,
            scratch_shapes=[pltpu.VMEM((kinds, rows + SUBS, LANES), jnp.float32)],
        ),
        out_shape=[
            jax.ShapeDtypeStruct((rows, channels), jnp.float32),
            jax.ShapeDtypeStruct((modes * SUBS, channels), jnp.float32),
        ]
        + [jax.ShapeDtypeStruct((modes, quarter), jnp.float32)] * tp_size,
        compiler_params=params_of(),
        cost_estimate=pl.CostEstimate(
            flops=rows * channels * 50,
            bytes_accessed=rows * channels * 14,
            transcendentals=2 * modes * channels,
        ),
        name="block_states",
    )(t, x, edge, *tables)


def inside_runs(t, x, edge, source, enter, tables, modes, taps_count, width=2048):
    _, rows, channels = x.shape
    tp_size, _, grid, whole, across = quarter_grid(tables, channels, width)
    return pl.pallas_call(
        functools.partial(inside_runs_kernel, modes=modes, taps_count=taps_count, tp_size=tp_size),
        grid_spec=pltpu.PrefetchScalarGridSpec(
            num_scalar_prefetch=1,
            grid=grid,
            in_specs=[
                pl.BlockSpec((1, rows, width), lambda k, c, t: (0, *across(k, c, t))),
                pl.BlockSpec((edge.shape[0], width), across),
                pl.BlockSpec((rows, width), across),
                pl.BlockSpec((enter.shape[0], width), across),
            ]
            + [pl.BlockSpec(tables[0].shape, whole)] * len(tables),
            out_specs=[pl.BlockSpec((rows, width), across)] * 2,
            scratch_shapes=[pltpu.VMEM((1, rows + SUBS, LANES), jnp.float32)],
        ),
        out_shape=[jax.ShapeDtypeStruct((rows, channels), jnp.float32)] * 2,
        compiler_params=params_of(),
        cost_estimate=pl.CostEstimate(
            flops=rows * channels * 25,
            bytes_accessed=rows * channels * 14,
            transcendentals=modes * channels,
        ),
        name="inside_runs",
    )(t, x, edge, source, enter, *tables)


def half_taps(taps_rows):
    return (taps_rows + 1) // 2


def half_rows(modes, taps_rows):
    return -(-(modes + half_taps(taps_rows)) // SUBS) * SUBS


def table_kernel(parity_ref, taps_ref, rate_ref, residue_ref, mine_ref, other_ref):
    lags, kinds, _ = taps_ref.shape
    modes = rate_ref.shape[0]
    rate = rate_ref[...]
    x = 2.0 * rate
    series = jnp.ones_like(x)
    for term in range(10, 1, -1):
        series = 1.0 - series * x * (1.0 / term)
    lost = jnp.where(x < 0.5, x * series, 1.0 - jnp.exp(-x))
    weight = residue_ref[...] * jnp.sqrt(lost)
    rows = [taps_ref[r // kinds, r % kinds : r % kinds + 1] for r in range(lags * kinds)]
    cut = half_taps(len(rows))

    def fill(lower_ref, upper_ref):
        lower_ref[0:modes] = rate
        upper_ref[0:modes] = weight
        for r, row in enumerate(rows):
            ref, place = (lower_ref, r) if r < cut else (upper_ref, r - cut)
            ref[modes + place : modes + place + 1] = row
        for ref, used in ((lower_ref, modes + cut), (upper_ref, modes + len(rows) - cut)):
            ref[used:] = jnp.zeros((ref.shape[0] - used, ref.shape[1]), jnp.float32)

    @pl.when(parity_ref[0] == 0)
    def _():
        fill(mine_ref, other_ref)

    @pl.when(parity_ref[0] == 1)
    def _():
        fill(other_ref, mine_ref)


def make_table(parity, taps, rate, residue):
    height = half_rows(rate.shape[0], taps.shape[0] * taps.shape[1])
    vmem = pl.BlockSpec(memory_space=pltpu.VMEM)
    return pl.pallas_call(
        table_kernel,
        in_specs=[pl.BlockSpec(memory_space=pltpu.SMEM)] + [vmem] * 3,
        out_specs=[vmem] * 2,
        out_shape=[jax.ShapeDtypeStruct((height, rate.shape[1]), jnp.float32)] * 2,
        compiler_params=params_of(),
        name="make_table",
    )(parity, taps, rate, residue)


def from_table(k, parity, tables, half, place):
    size = len(tables) // 2
    ordered = [
        jnp.where(parity == half, tables[i][place], tables[size + i][place]) for i in range(size)
    ]
    value = ordered[0]
    for other in range(1, size):
        value = jnp.where(k == other, ordered[other], value)
    return value


def block_end_kernel(t_ref, rate_ref, *refs, rows):
    ends, o_ref = refs[:-1], refs[-1]
    rate = rate_ref[...]
    total = jnp.zeros_like(rate)
    for k, end in enumerate(ends):
        later = len(ends) - 1 - (k ^ t_ref[0])
        total = total + jnp.exp(rate * (later * -rows).astype(jnp.float32)) * end[...]
    o_ref[...] = total


def pair_enters_kernel(t_ref, rate_ref, *refs, rows):
    seen, o_ref = refs[:-1], refs[-1]
    half = o_ref.shape[0]
    rate = jnp.where(t_ref[1] == 1, rate_ref[half:], rate_ref[:half])
    span = jnp.exp(rate * (-2.0 * rows))
    total = seen[-1][...]
    for one in seen[-2::-1]:
        total = total * span + one[...]
    o_ref[...] = total


def pair_kernel(t_ref, rate_ref, own_ref, mate_ref, *refs, rows):
    size = len(refs) // 2
    ends, total_ref, outs = refs[:size], refs[size], refs[size + 1 :]
    t, odd = t_ref[0], t_ref[1] == 1
    rate, own, mate = rate_ref[...], own_ref[...], mate_ref[...]
    first, second = jnp.where(odd, mate, own), jnp.where(odd, own, mate)
    total = first * jnp.exp(rate * (-1.0 * rows * size)) + second
    half = total_ref.shape[0]
    total_ref[...] = jnp.where(odd, total[half:], total[:half])
    span = jnp.exp(rate * (-1.0 * rows))
    state = jnp.where(odd, mate, 0.0)
    for place in range(size):
        mine = place ^ t
        for k in range(size):

            @pl.when(mine == k)
            def _(k=k, state=state):
                outs[k][...] = state

        end = pick(mine, ends, Ellipsis)
        state = state * span + end


def small_call(kernel, t, name, heights, *arrays, limit=VMEM_BYTES, **sizes):
    vmem = pl.BlockSpec(memory_space=pltpu.VMEM)
    return pl.pallas_call(
        functools.partial(kernel, **sizes),
        in_specs=[pl.BlockSpec(memory_space=pltpu.SMEM)] + [vmem] * len(arrays),
        out_specs=[vmem] * len(heights),
        out_shape=[jax.ShapeDtypeStruct((h, arrays[0].shape[1]), jnp.float32) for h in heights],
        compiler_params=params_of(limit),
        name=name,
    )(t, *arrays)


def add_entering_kernel(t_ref, y_ref, q_ref, *refs, modes, size, tp_size):
    o_ref, out_s = refs[-2:]
    inside, mine_enters, other_enters, mines, others = (
        refs[i * size : (i + 1) * size] for i in range(5)
    )
    k = pl.program_id(0)
    blocks_before = t_ref[1] * tp_size + t_ref[0]
    rows, width = y_ref.shape
    run = rows // SUBS
    even = t_ref[1] == 0
    before = lax.broadcasted_iota(jnp.int32, (SUBS, LANES), 0).astype(jnp.float32) * (-1.0 * run)
    for c in range(width // LANES):
        lanes = slice(c * LANES, (c + 1) * LANES)
        mine, other = (pick(k, half, (slice(0, modes), lanes)) for half in (mines, others))
        rate, weight = jnp.where(even, mine, other), jnp.where(even, other, mine)
        decay = jnp.exp(-rate)
        one = (slice(0, modes // 2), lanes)
        mine, other = pick(k, mine_enters, one), pick(k, other_enters, one)
        enters = jnp.concatenate(
            [jnp.where(even, mine, other), jnp.where(even, other, mine)], axis=0
        )
        state = enters * jnp.exp(rate * (blocks_before * -rows).astype(jnp.float32))
        state = (state + pick(k, inside, (slice(0, modes), lanes))) * weight * decay
        terms, steps = [], []
        for n in range(modes):
            terms.append(jnp.exp(before * rate[n : n + 1]) * state[n : n + 1])
            steps.append(wide(decay[n : n + 1]))
        for j in range(run):
            place = slice(j * SUBS, (j + 1) * SUBS)
            out_s[pl.ds(j, SUBS, stride=run)] = q_ref[place, lanes] * (y_ref[place, lanes] + added(terms))
            terms = [a * b for a, b in zip(terms, steps)]
        o_ref[:, lanes] = out_s[...].astype(o_ref.dtype)


def add_entering(t, first, y, q, families, before, modes, width=2048):
    rows, channels = y.shape
    size, quarter = len(families[0]), families[0][0].shape[1]
    chunks = quarter // width
    arrays = [a for family in families for a in family]
    there = lambda k, c, t: (0, ((k + first) ^ t[0]) * chunks + c)
    across = lambda k, c, t: (0, c)
    old = [] if before is None else [before]
    return pl.pallas_call(
        functools.partial(
            add_entering_kernel, modes=modes, size=size, tp_size=channels // quarter
        ),
        grid_spec=pltpu.PrefetchScalarGridSpec(
            num_scalar_prefetch=1,
            grid=(size, chunks),
            in_specs=[pl.BlockSpec((rows, width), there)] * 2
            + [pl.BlockSpec((a.shape[0], width), across) for a in arrays]
            + [pl.BlockSpec(memory_space=pl.ANY)] * len(old),
            out_specs=pl.BlockSpec((rows, width), there),
            scratch_shapes=[pltpu.VMEM((rows, LANES), jnp.float32)],
        ),
        out_shape=jax.ShapeDtypeStruct((rows, channels), jnp.bfloat16),
        input_output_aliases={3 + len(arrays): 0} if old else {},
        compiler_params=params_of(),
        cost_estimate=pl.CostEstimate(
            flops=size * rows * quarter * 36,
            bytes_accessed=size * rows * quarter * 10,
            transcendentals=size * modes * quarter * 9,
        ),
        name="add_entering",
    )(t, y, q, *arrays, *old)


def exchange(x, axis):
    return lax.all_to_all(x, axis, split_axis=0, concat_axis=0, tiled=True)


def trade_tp(arrays):
    size = len(arrays)
    return [arrays[0]] + [
        lax.ppermute(arrays[k], "tp", [(i, i ^ k) for i in range(size)]) for k in range(1, size)
    ]


def segment_starts(lengths, tokens):
    order = jnp.arange(lengths.shape[0], dtype=jnp.int32)
    ends = jnp.sum(jnp.where(order[:, None] <= order[None, :], lengths[:, None], 0), axis=0)
    position = jnp.arange(tokens, dtype=jnp.int32)
    passed = jnp.where(ends[None, :] <= position[:, None], ends[None, :], 0)
    return jnp.max(passed, axis=1)


def by_tokens(hyena_in, attn_in, short_taps, decay_rate, residue, lengths):
    rows, kinds, channels = hyena_in.shape
    ctx_size, tp_size = lax.axis_size("ctx"), lax.axis_size("tp")
    devices = ctx_size * tp_size
    taps_count = short_taps.shape[0]
    modes = decay_rate.shape[0]
    parity = (lax.axis_index("ctx") % 2).astype(jnp.int32)
    t = jnp.stack([lax.axis_index("tp").astype(jnp.int32), parity])
    swap = [(i, i ^ 1) for i in range(ctx_size)]

    x = jnp.transpose(hyena_in, (1, 0, 2))
    edge = x[:, rows - taps_count + 1 :].reshape(kinds * (taps_count - 1), channels)
    edge = lax.ppermute(edge, ALL, [(i, i + 1) for i in range(devices - 1)])
    mine, other = make_table(parity.reshape(1), short_taps, decay_rate, residue)
    mine = trade_tp([mine] * tp_size)
    heads_out = split_heads(jnp.transpose(attn_in, (1, 0, 2)))
    heads_out, edge, *mine = lax.optimization_barrier((heads_out, edge, *mine))
    by_head = exchange(heads_out, ALL)
    tables = mine + [other] + [lax.ppermute(half, "ctx", swap) for half in mine[1:]]
    source, enter, *ends = block_states(t, x, edge, tables, modes, taps_count)
    y, q = inside_runs(t, x, edge, source, enter, tables, modes, taps_count)
    y, *ends = lax.optimization_barrier((y, *trade_tp(ends)))
    [block_end] = small_call(
        block_end_kernel, t, "block_end", [modes], decay_rate, *ends, rows=rows
    )

    mate = lax.ppermute(block_end, "ctx", swap)
    total, *inside = small_call(
        pair_kernel, t, "pair", [modes // 2] + [modes] * tp_size,
        decay_rate, block_end, mate, *ends, rows=rows,
    )
    by_head, *_ = lax.optimization_barrier((by_head, *inside, total))
    inside = trade_tp(inside)
    total, inside[1] = lax.optimization_barrier((total, inside[1]))
    seen = [
        lax.ppermute(total, "ctx", [(i, i + hop) for i in range(ctx_size - hop)])
        for hop in range(2, ctx_size, 2)
    ]

    mixed = attend(by_head, segment_starts(lengths, rows * devices))
    mixed, seen, inside = lax.optimization_barrier((mixed, seen, inside))
    [enters] = small_call(
        pair_enters_kernel, t, "pair_enters", [modes // 2], decay_rate, *seen,
        limit=SMALL_BYTES, rows=rows * tp_size,
    )
    mate_enters = lax.ppermute(enters, "ctx", swap)
    enters = trade_tp([enters] * tp_size)
    attn_out = join_heads(exchange(mixed.reshape(devices, rows, DH), ALL))
    mines, others = tables[:tp_size], tables[tp_size:]
    own = inside[:1], enters[:1], [mate_enters], mines[:1], others[:1]
    hyena_out = add_entering(t, 0, y, q, own, None, modes)
    hyena_out, *enters = lax.optimization_barrier((hyena_out, *enters[1:]))
    mate_enters = [lax.ppermute(half, "ctx", swap) for half in enters]
    rest = inside[1:], enters, mate_enters, mines[1:], others[1:]
    hyena_out = add_entering(t, 1, y, q, rest, hyena_out, modes)
    return hyena_out, attn_out


exact_mode = lax.Precision.HIGHEST


def from_behind(block, axis, distance):
    devices = range(lax.axis_size(axis))
    route = [(i - distance, i) for i in devices if i - distance in devices]
    return lax.ppermute(block, axis, route)


def carried_in(part, axis, combine, identity):
    place = lax.axis_index(axis)
    gathered = jax.tree.map(lambda a: lax.all_gather(a, axis), part)
    state = jax.tree.map(lambda a, e: jnp.zeros_like(a) + jnp.asarray(e, a.dtype), part, identity)

    def one(lap, state):
        return combine(
            state, jax.tree.map(lambda a: lax.dynamic_index_in_dim(a, lap, 0, False), gathered)
        )

    return lax.fori_loop(0, place, one, state)


def segment_of(positions, segment_ends):
    return jnp.sum((segment_ends[None, :] <= positions[:, None]).astype(jnp.int32), axis=1)


def by_channels(hyena_in, attn_in, short_taps, decay_rate, residue, lengths):
    hyena_cols, attention_cols = (
        lax.all_to_all(hyena_in, "tp", split_axis=2, concat_axis=0, tiled=True),
        lax.all_to_all(attn_in, "tp", split_axis=2, concat_axis=0, tiled=True),
    )
    block_rows = hyena_cols.shape[0]
    rim_rows = short_taps.shape[0] - 1
    edge_rows = from_behind(hyena_cols[block_rows - rim_rows :], "ctx", 1)
    extended = jnp.concatenate([edge_rows, hyena_cols], axis=0).astype(jnp.float32)
    filtered = jnp.zeros(hyena_cols.shape, jnp.float32)
    for lag in range(rim_rows + 1):
        filtered = (
            filtered + short_taps[lag] * extended[rim_rows - lag : rim_rows - lag + block_rows]
        )
    query_side = filtered[:, 0]
    source = filtered[:, 1] * filtered[:, 2]
    channels = source.shape[1]
    weight = residue * jnp.sqrt(-jnp.expm1(-2.0 * decay_rate))
    sub_length = math.gcd(32, block_rows)
    pieces = block_rows // sub_length
    offsets = jnp.arange(sub_length, dtype=jnp.float32)
    powers = jnp.exp(-offsets[:, None, None] * decay_rate[None])
    lag_values = jnp.einsum("onc,nc->oc", powers, weight, precision=exact_mode)
    lag_index = jnp.arange(sub_length, dtype=jnp.int32)
    selector = (
        lag_index[:, None, None] - lag_index[None, :, None] == lag_index[None, None, :]
    ).astype(jnp.float32)
    toeplitz = jnp.einsum("tso,oc->tsc", selector, lag_values, precision=exact_mode)
    grouped = source.reshape(pieces, sub_length, channels)
    inner = jnp.einsum("tsc,bsc->btc", toeplitz, grouped, precision=exact_mode)
    tail_powers = jnp.exp(-(sub_length - 1.0 - offsets)[:, None, None] * decay_rate[None])
    own_states = jnp.einsum("snc,bsc->bnc", tail_powers, grouped, precision=exact_mode)
    sub_decay = jnp.exp(-sub_length * decay_rate)

    def carry_states(carried, incoming):
        return (sub_decay * carried + incoming, carried)

    local_end, entering = lax.scan(carry_states, jnp.zeros_like(sub_decay), own_states)
    block_decay = jnp.exp(-block_rows * decay_rate)

    def combine(earlier, later):
        return (earlier[0] * later[0], later[0] * earlier[1] + later[1])

    _, arriving = carried_in(
        (block_decay, local_end),
        "ctx",
        combine,
        (jnp.ones_like(block_decay), jnp.zeros_like(local_end)),
    )
    starts = jnp.arange(pieces, dtype=jnp.float32) * sub_length
    all_entering = entering + jnp.exp(-starts[:, None, None] * decay_rate[None]) * arriving[None]
    rise_powers = jnp.exp(-(offsets + 1.0)[:, None, None] * decay_rate[None]) * weight[None]
    from_state = jnp.einsum("tnc,bnc->btc", rise_powers, all_entering, precision=exact_mode)
    long_conv = (inner + from_state).reshape(block_rows, channels)
    hyena_local = (query_side * long_conv).astype(jnp.bfloat16)
    head_cols = attention_cols.shape[2]
    local_heads = head_cols // DH
    queries = attention_cols[:, 0].reshape(block_rows, local_heads, DH)
    keyvals = attention_cols[:, 1:3]
    order = jnp.arange(lengths.shape[0], dtype=jnp.int32)
    segment_ends = jnp.sum(jnp.where(order[:, None] <= order[None, :], lengths[:, None], 0), axis=0)
    block_index = lax.axis_index("ctx")
    query_pos = block_index * block_rows + jnp.arange(block_rows, dtype=jnp.int32)
    query_seg = segment_of(query_pos, segment_ends)
    score_scale = 1.0 / math.sqrt(DH)

    def attend_part(softmax_state, part, key_start):
        count = part.shape[0]
        key_pos = key_start + jnp.arange(count, dtype=jnp.int32)
        key_seg = segment_of(key_pos, segment_ends)
        allowed = (
            (key_pos[None, :] <= query_pos[:, None])
            & (key_seg[None, :] == query_seg[:, None])
            & (key_pos >= 0)[None, :]
        )

        def compute(carried):
            row_top, denom, weighted = carried
            key_rows = part[:, 0].reshape(count, local_heads, DH)
            value_rows = part[:, 1].reshape(count, local_heads, DH)
            scores = (
                jnp.einsum("qhd,khd->hqk", queries, key_rows, preferred_element_type=jnp.float32)
                * score_scale
            )
            masked = jnp.where(allowed[None], scores, jnp.float32(-1e30))
            new_top = jnp.maximum(row_top, jnp.max(masked, axis=2))
            expo = jnp.where(allowed[None], jnp.exp(scores - new_top[:, :, None]), jnp.float32(0.0))
            rescale = jnp.exp(row_top - new_top)
            denom = denom * rescale + jnp.sum(expo, axis=2)
            probs = expo.astype(jnp.bfloat16)
            added = jnp.einsum(
                "hqk,khd->qhd", probs, value_rows, preferred_element_type=jnp.float32
            )
            weighted = weighted * jnp.transpose(rescale)[:, :, None] + added
            return (new_top, denom, weighted)

        def keep(carried):
            return carried

        return lax.cond(jnp.any(allowed), compute, keep, softmax_state)

    initial = (
        jnp.full((local_heads, block_rows), -1e30, jnp.float32),
        jnp.zeros((local_heads, block_rows), jnp.float32),
        jnp.zeros((block_rows, local_heads, DH), jnp.float32),
    )
    piece = lax.all_gather(keyvals, "ctx", axis=0, tiled=True)
    rows = piece.shape[0]
    step_rows = math.gcd(rows, 512)

    def advance(count, carried):
        part = lax.dynamic_slice_in_dim(piece, count * step_rows, step_rows, 0)
        return attend_part(carried, part, count * step_rows)

    final_state = lax.fori_loop(0, rows // step_rows, advance, initial)
    _, denom, weighted = final_state
    attention_local = (
        (weighted / jnp.transpose(denom)[:, :, None])
        .reshape(block_rows, head_cols)
        .astype(jnp.bfloat16)
    )
    hyena_out, attn_out = (
        lax.all_to_all(hyena_local, "tp", split_axis=0, concat_axis=1, tiled=True),
        lax.all_to_all(attention_local, "tp", split_axis=0, concat_axis=1, tiled=True),
    )
    return (hyena_out, attn_out)


def per_device(hyena_in, attn_in, short_taps, decay_rate, residue, lengths):
    rows, _, channels = hyena_in.shape
    devices = lax.axis_size("ctx") * lax.axis_size("tp")
    one_head_each = attn_in.shape[2] == devices * DH
    tp_size = lax.axis_size("tp")
    pairs = tp_size & (tp_size - 1) == 0
    pairs = pairs and lax.axis_size("ctx") >= 4 and lax.axis_size("ctx") % 2 == 0
    whole_tiles = pairs and rows % (2 * SUBS) == 0 and channels % (tp_size * 2048) == 0
    whole_tiles = whole_tiles and decay_rate.shape[0] % (2 * SUBS) == 0
    plan = by_tokens if one_head_each and whole_tiles else by_channels
    return plan(hyena_in, attn_in, short_taps, decay_rate, residue, lengths)


def solution(mesh):
    placed = (
        P(("ctx", "tp"), None, None),
        P(("ctx", "tp"), None, None),
        P(None, None, "tp"),
        P(None, "tp"),
        P(None, "tp"),
        P(),
    )
    return jax.shard_map(
        per_device,
        mesh=mesh,
        in_specs=placed,
        out_specs=(P(("ctx", "tp"), None), P(("ctx", "tp"), None)),
        check_vma=False,
    )
```

```python
import functools
import math

import jax
import jax.numpy as jnp
from jax import lax
from jax.experimental import pallas as pl
from jax.experimental.pallas import tpu as pltpu
from jax.sharding import PartitionSpec as P

DH = 128
LANES = 128
SUBS = 8
ALL = ("ctx", "tp")
VMEM_BYTES = 60 * 1024 * 1024
ATTEND_BYTES = 32 * 1024 * 1024
SMALL_BYTES = 16 * 1024 * 1024
MASKED = -1e30


def params_of(limit=VMEM_BYTES):
    return pltpu.CompilerParams(vmem_limit_bytes=limit)


def split_heads_kernel(x_ref, o_ref):
    for h in range(o_ref.shape[0]):
        o_ref[h] = x_ref[:, :, h * DH : (h + 1) * DH]


def split_heads(x, group=16):
    kinds, rows, width = x.shape
    heads = width // DH
    return pl.pallas_call(
        split_heads_kernel,
        grid=(heads // group,),
        in_specs=[pl.BlockSpec((kinds, rows, group * DH), lambda g: (0, 0, g))],
        out_specs=pl.BlockSpec((group, kinds, rows, DH), lambda g: (g, 0, 0, 0)),
        out_shape=jax.ShapeDtypeStruct((heads, kinds, rows, DH), x.dtype),
        compiler_params=params_of(),
        name="split_heads",
    )(x)


def join_heads_kernel(x_ref, o_ref):
    for h in range(x_ref.shape[0]):
        o_ref[:, h * DH : (h + 1) * DH] = x_ref[h]


def join_heads(x, group=16):
    heads, rows, _ = x.shape
    return pl.pallas_call(
        join_heads_kernel,
        grid=(heads // group,),
        in_specs=[pl.BlockSpec((group, rows, DH), lambda g: (g, 0, 0))],
        out_specs=pl.BlockSpec((rows, group * DH), lambda g: (0, g)),
        out_shape=jax.ShapeDtypeStruct((rows, heads * DH), x.dtype),
        compiler_params=params_of(ATTEND_BYTES),
        name="join_heads",
    )(x)


def attend_kernel(tile_start_ref, x_ref, start_ref, o_ref, q_s, k_s, v_s):
    tile = pl.program_id(0)
    blocks, _, rows, _ = x_ref.shape
    query_rows = o_ref.shape[0]
    scale = math.log2(math.e) / math.sqrt(DH)

    @pl.when(tile == 0)
    def _():
        @pl.loop(0, blocks)
        def _(b):
            place = pl.ds(pl.multiple_of(b * rows, rows), rows)
            q_s[place] = x_ref[b, 0]
            k_s[place] = x_ref[b, 1]
            v_s[place] = x_ref[b, 2]

    first_row = tile * query_rows
    q = q_s[pl.ds(pl.multiple_of(first_row, query_rows), query_rows)]
    start = jnp.concatenate([start_ref[...]] * (query_rows // LANES), axis=1)
    shape = (query_rows, query_rows)
    row = lax.broadcasted_iota(jnp.int32, shape, 0)
    col = lax.broadcasted_iota(jnp.int32, shape, 1)

    def step(i, carry, diagonal=False):
        top, denom, mixed = carry
        base = pl.multiple_of(i * query_rows, query_rows)
        k = k_s[pl.ds(base, query_rows)]
        v = v_s[pl.ds(base, query_rows)]
        s = lax.dot_general(q, k, (((1,), (1,)), ((), ())), preferred_element_type=jnp.float32)
        allowed = col >= start - base
        if diagonal:
            allowed = allowed & (col <= row)
        s = jnp.where(allowed, s, MASKED)
        new_top = jnp.maximum(top, jnp.max(s, axis=1, keepdims=True))
        p = jnp.exp2((s - new_top) * scale)
        rescale = jnp.exp2((top - new_top) * scale)
        denom = denom * rescale
        for c in range(query_rows // LANES):
            denom = denom + p[:, c * LANES : (c + 1) * LANES]
        mixed = mixed * rescale + jnp.dot(
            p.astype(jnp.bfloat16), v, preferred_element_type=jnp.float32
        )
        return new_top, denom, mixed

    carry = (
        jnp.full((query_rows, 1), MASKED, jnp.float32),
        jnp.zeros((query_rows, LANES), jnp.float32),
        jnp.zeros((query_rows, DH), jnp.float32),
    )
    carry = step(tile, carry, diagonal=True)
    _, denom, mixed = lax.fori_loop(tile_start_ref[tile] // query_rows, tile, step, carry)
    o_ref[...] = (mixed / jnp.sum(denom, axis=1, keepdims=True)).astype(o_ref.dtype)


def attend(x, start, query_rows=512):
    blocks, _, rows, _ = x.shape
    tokens = blocks * rows
    query_rows = math.gcd(tokens, query_rows)
    wide_start = jnp.broadcast_to(start[:, None], (tokens, LANES))
    return pl.pallas_call(
        attend_kernel,
        grid_spec=pltpu.PrefetchScalarGridSpec(
            num_scalar_prefetch=1,
            grid=(tokens // query_rows,),
            in_specs=[
                pl.BlockSpec(x.shape, lambda t, s: (0, 0, 0, 0)),
                pl.BlockSpec((query_rows, LANES), lambda t, s: (t, 0)),
            ],
            out_specs=pl.BlockSpec((query_rows, DH), lambda t, s: (t, 0)),
            scratch_shapes=[pltpu.VMEM((tokens, DH), x.dtype)] * 3,
        ),
        out_shape=jax.ShapeDtypeStruct((tokens, DH), x.dtype),
        compiler_params=params_of(ATTEND_BYTES),
        cost_estimate=pl.CostEstimate(
            flops=2 * tokens * tokens * DH,
            bytes_accessed=x.size * 2 + tokens * (DH * 2 + LANES * 4),
            transcendentals=tokens * tokens // 2,
        ),
        name="attend",
    )(start[::query_rows], x, wide_start)


def pick(k, refs, place):
    value = refs[0][place]
    for other in range(1, len(refs)):
        value = jnp.where(k == other, refs[other][place], value)
    return value


def wide(row):
    return jnp.broadcast_to(row, (SUBS, LANES))


def added(parts):
    while len(parts) > 1:
        parts = [a + b for a, b in zip(parts[::2], parts[1::2])] + (
            [parts[-1]] if len(parts) % 2 else []
        )
    return parts[0]


def filtered_runs(xs, i, taps, run):
    rim = len(taps) - 1
    seen = [xs[i, pl.ds(SUBS + j - rim, SUBS, stride=run)] for j in range(rim)]
    out = []
    for j in range(run):
        seen.append(xs[i, pl.ds(SUBS + j, SUBS, stride=run)])
        out.append(sum(taps[lag] * seen[-1 - lag] for lag in range(1, rim + 1)) + taps[0] * seen[-1])
    return out


def taps_of(k, parity, tables, modes, taps_count, kinds, spot):
    past = slice(modes, tables[0].shape[0])
    halves = [from_table(k, parity, tables, half, (past, spot)) for half in (0, 1)]
    cut = half_taps(taps_count * kinds)

    def tap(lag, i):
        half, r = divmod(lag * kinds + i, cut)
        return wide(halves[half][r : r + 1])

    return lambda i: [tap(lag, i) for lag in range(taps_count)]


def block_states_kernel(t_ref, x_ref, edge_ref, *refs, modes, taps_count, tp_size):
    tables, (source_ref, enter_ref) = refs[: 2 * tp_size], refs[2 * tp_size :][:2]
    ends, xs = refs[2 * tp_size + 2 : -1], refs[-1]
    kinds, rows, width = x_ref.shape
    k, chunk = pl.program_id(0), pl.program_id(1)
    run = rows // SUBS
    rim = taps_count - 1
    sub = lax.broadcasted_iota(jnp.int32, (SUBS, LANES), 0)
    for c in range(width // LANES):
        lanes = slice(c * LANES, (c + 1) * LANES)
        spot = pl.ds(pl.multiple_of(chunk * width + c * LANES, LANES), LANES)
        edge = edge_ref[:, lanes].astype(jnp.float32)
        for i in (1, 2):
            xs[i, SUBS - rim : SUBS] = edge[i * rim : (i + 1) * rim]
            xs[i, SUBS:] = x_ref[i, :, lanes].astype(jnp.float32)
        rate = from_table(k, t_ref[1], tables, 0, (slice(0, modes), spot))
        taps = taps_of(k, t_ref[1], tables, modes, taps_count, kinds, spot)
        decay = jnp.exp(-rate)
        decay_run = jnp.exp(rate * (-1.0 * run))
        source = [
            a * b
            for a, b in zip(filtered_runs(xs, 1, taps(1), run), filtered_runs(xs, 2, taps(2), run))
        ]
        for j in range(run):
            source_ref[j * SUBS : (j + 1) * SUBS, lanes] = source[j]

        decays = [wide(decay[n : n + 1]) for n in range(modes)]
        states = [source[0]] * modes
        for j in range(1, run):
            states = [state * d + source[j] for state, d in zip(states, decays)]
        spans = [wide(decay_run[n : n + 1]) for n in range(modes)]
        for hop in (1, 2, 4):
            states = [
                state + jnp.where(sub >= hop, span * pltpu.roll(state, hop, 0), 0.0)
                for state, span in zip(states, spans)
            ]
            spans = [span * span for span in spans]
        last = [state[SUBS - 1 : SUBS] for state in states]
        for n, state in enumerate(states):
            enter_ref[n * SUBS : (n + 1) * SUBS, lanes] = jnp.where(
                sub >= 1, pltpu.roll(state, 1, 0), 0.0
            )
        last = jnp.concatenate(last, axis=0)
        for other in range(tp_size):

            @pl.when(k == other)
            def _(other=other):
                ends[other][:, spot] = last


def inside_runs_kernel(t_ref, x_ref, edge_ref, source_ref, enter_ref, *refs, modes, taps_count, tp_size):
    tables, y_ref, q_ref, xs = refs[: 2 * tp_size], refs[-3], refs[-2], refs[-1]
    _, rows, width = x_ref.shape
    kinds = edge_ref.shape[0] // (taps_count - 1)
    k, chunk = pl.program_id(0), pl.program_id(1)
    run = rows // SUBS
    rim = taps_count - 1
    for c in range(width // LANES):
        lanes = slice(c * LANES, (c + 1) * LANES)
        spot = pl.ds(pl.multiple_of(chunk * width + c * LANES, LANES), LANES)
        xs[0, SUBS - rim : SUBS] = edge_ref[:, lanes].astype(jnp.float32)[0:rim]
        xs[0, SUBS:] = x_ref[0, :, lanes].astype(jnp.float32)
        rate = from_table(k, t_ref[1], tables, 0, (slice(0, modes), spot))
        weight = from_table(k, t_ref[1], tables, 1, (slice(0, modes), spot))
        taps = taps_of(k, t_ref[1], tables, modes, taps_count, kinds, spot)
        for j, value in enumerate(filtered_runs(xs, 0, taps(0), run)):
            q_ref[j * SUBS : (j + 1) * SUBS, lanes] = value
        decay = jnp.exp(-rate)
        power = weight
        lags = []
        for j in range(run):
            lags.append(wide(jnp.sum(power, axis=0, keepdims=True)))
            power = power * decay
        source = [source_ref[j * SUBS : (j + 1) * SUBS, lanes] for j in range(run)]
        weight = weight * decay
        terms = [
            enter_ref[n * SUBS : (n + 1) * SUBS, lanes] * wide(weight[n : n + 1])
            for n in range(modes)
        ]
        steps = [wide(decay[n : n + 1]) for n in range(modes)]
        for j in range(run):
            total = added(terms)
            for lag in range(j + 1):
                total = total + lags[lag] * source[j - lag]
            y_ref[j * SUBS : (j + 1) * SUBS, lanes] = total
            terms = [a * b for a, b in zip(terms, steps)]


def quarter_grid(tables, channels, width):
    tp_size = len(tables) // 2
    quarter = channels // tp_size
    chunks = quarter // width
    whole = lambda k, c, t: (0, 0)
    across = lambda k, c, t: (0, (k ^ t[0]) * chunks + c)
    return tp_size, quarter, (tp_size, chunks), whole, across


def block_states(t, x, edge, tables, modes, taps_count, width=2048):
    kinds, rows, channels = x.shape
    tp_size, quarter, grid, whole, across = quarter_grid(tables, channels, width)
    return pl.pallas_call(
        functools.partial(
            block_states_kernel, modes=modes, taps_count=taps_count, tp_size=tp_size
        ),
        grid_spec=pltpu.PrefetchScalarGridSpec(
            num_scalar_prefetch=1,
            grid=grid,
            in_specs=[
                pl.BlockSpec((kinds, rows, width), lambda k, c, t: (0, *across(k, c, t))),
                pl.BlockSpec((edge.shape[0], width), across),
            ]
            + [pl.BlockSpec(tables[0].shape, whole)] * len(tables),
            out_specs=[pl.BlockSpec((rows, width), across), pl.BlockSpec((modes * SUBS, width), across)]
            + [pl.BlockSpec((modes, quarter), whole)] * tp_size,
            scratch_shapes=[pltpu.VMEM((kinds, rows + SUBS, LANES), jnp.float32)],
        ),
        out_shape=[
            jax.ShapeDtypeStruct((rows, channels), jnp.float32),
            jax.ShapeDtypeStruct((modes * SUBS, channels), jnp.float32),
        ]
        + [jax.ShapeDtypeStruct((modes, quarter), jnp.float32)] * tp_size,
        compiler_params=params_of(),
        cost_estimate=pl.CostEstimate(
            flops=rows * channels * 50,
            bytes_accessed=rows * channels * 14,
            transcendentals=2 * modes * channels,
        ),
        name="block_states",
    )(t, x, edge, *tables)


def inside_runs(t, x, edge, source, enter, tables, modes, taps_count, width=2048):
    _, rows, channels = x.shape
    tp_size, _, grid, whole, across = quarter_grid(tables, channels, width)
    return pl.pallas_call(
        functools.partial(inside_runs_kernel, modes=modes, taps_count=taps_count, tp_size=tp_size),
        grid_spec=pltpu.PrefetchScalarGridSpec(
            num_scalar_prefetch=1,
            grid=grid,
            in_specs=[
                pl.BlockSpec((1, rows, width), lambda k, c, t: (0, *across(k, c, t))),
                pl.BlockSpec((edge.shape[0], width), across),
                pl.BlockSpec((rows, width), across),
                pl.BlockSpec((enter.shape[0], width), across),
            ]
            + [pl.BlockSpec(tables[0].shape, whole)] * len(tables),
            out_specs=[pl.BlockSpec((rows, width), across)] * 2,
            scratch_shapes=[pltpu.VMEM((1, rows + SUBS, LANES), jnp.float32)],
        ),
        out_shape=[jax.ShapeDtypeStruct((rows, channels), jnp.float32)] * 2,
        compiler_params=params_of(),
        cost_estimate=pl.CostEstimate(
            flops=rows * channels * 25,
            bytes_accessed=rows * channels * 14,
            transcendentals=modes * channels,
        ),
        name="inside_runs",
    )(t, x, edge, source, enter, *tables)


def half_taps(taps_rows):
    return (taps_rows + 1) // 2


def half_rows(modes, taps_rows):
    return -(-(modes + half_taps(taps_rows)) // SUBS) * SUBS


def table_kernel(parity_ref, taps_ref, rate_ref, residue_ref, mine_ref, other_ref):
    lags, kinds, _ = taps_ref.shape
    modes = rate_ref.shape[0]
    rate = rate_ref[...]
    x = 2.0 * rate
    series = jnp.ones_like(x)
    for term in range(10, 1, -1):
        series = 1.0 - series * x * (1.0 / term)
    lost = jnp.where(x < 0.5, x * series, 1.0 - jnp.exp(-x))
    weight = residue_ref[...] * jnp.sqrt(lost)
    rows = [taps_ref[r // kinds, r % kinds : r % kinds + 1] for r in range(lags * kinds)]
    cut = half_taps(len(rows))

    def fill(lower_ref, upper_ref):
        lower_ref[0:modes] = rate
        upper_ref[0:modes] = weight
        for r, row in enumerate(rows):
            ref, place = (lower_ref, r) if r < cut else (upper_ref, r - cut)
            ref[modes + place : modes + place + 1] = row
        for ref, used in ((lower_ref, modes + cut), (upper_ref, modes + len(rows) - cut)):
            ref[used:] = jnp.zeros((ref.shape[0] - used, ref.shape[1]), jnp.float32)

    @pl.when(parity_ref[0] == 0)
    def _():
        fill(mine_ref, other_ref)

    @pl.when(parity_ref[0] == 1)
    def _():
        fill(other_ref, mine_ref)


def make_table(parity, taps, rate, residue):
    height = half_rows(rate.shape[0], taps.shape[0] * taps.shape[1])
    vmem = pl.BlockSpec(memory_space=pltpu.VMEM)
    return pl.pallas_call(
        table_kernel,
        in_specs=[pl.BlockSpec(memory_space=pltpu.SMEM)] + [vmem] * 3,
        out_specs=[vmem] * 2,
        out_shape=[jax.ShapeDtypeStruct((height, rate.shape[1]), jnp.float32)] * 2,
        compiler_params=params_of(),
        name="make_table",
    )(parity, taps, rate, residue)


def from_table(k, parity, tables, half, place):
    size = len(tables) // 2
    ordered = [
        jnp.where(parity == half, tables[i][place], tables[size + i][place]) for i in range(size)
    ]
    value = ordered[0]
    for other in range(1, size):
        value = jnp.where(k == other, ordered[other], value)
    return value


def block_end_kernel(t_ref, rate_ref, *refs, rows):
    ends, o_ref = refs[:-1], refs[-1]
    rate = rate_ref[...]
    total = jnp.zeros_like(rate)
    for k, end in enumerate(ends):
        later = len(ends) - 1 - (k ^ t_ref[0])
        total = total + jnp.exp(rate * (later * -rows).astype(jnp.float32)) * end[...]
    o_ref[...] = total


def pair_enters_kernel(t_ref, rate_ref, *refs, rows):
    seen, o_ref = refs[:-1], refs[-1]
    half = o_ref.shape[0]
    rate = jnp.where(t_ref[1] == 1, rate_ref[half:], rate_ref[:half])
    span = jnp.exp(rate * (-2.0 * rows))
    total = seen[-1][...]
    for one in seen[-2::-1]:
        total = total * span + one[...]
    o_ref[...] = total


def pair_kernel(t_ref, rate_ref, own_ref, mate_ref, *refs, rows):
    size = len(refs) // 2
    ends, total_ref, outs = refs[:size], refs[size], refs[size + 1 :]
    t, odd = t_ref[0], t_ref[1] == 1
    rate, own, mate = rate_ref[...], own_ref[...], mate_ref[...]
    first, second = jnp.where(odd, mate, own), jnp.where(odd, own, mate)
    total = first * jnp.exp(rate * (-1.0 * rows * size)) + second
    half = total_ref.shape[0]
    total_ref[...] = jnp.where(odd, total[half:], total[:half])
    span = jnp.exp(rate * (-1.0 * rows))
    state = jnp.where(odd, mate, 0.0)
    for place in range(size):
        mine = place ^ t
        for k in range(size):

            @pl.when(mine == k)
            def _(k=k, state=state):
                outs[k][...] = state

        end = pick(mine, ends, Ellipsis)
        state = state * span + end


def small_call(kernel, t, name, heights, *arrays, limit=VMEM_BYTES, **sizes):
    vmem = pl.BlockSpec(memory_space=pltpu.VMEM)
    return pl.pallas_call(
        functools.partial(kernel, **sizes),
        in_specs=[pl.BlockSpec(memory_space=pltpu.SMEM)] + [vmem] * len(arrays),
        out_specs=[vmem] * len(heights),
        out_shape=[jax.ShapeDtypeStruct((h, arrays[0].shape[1]), jnp.float32) for h in heights],
        compiler_params=params_of(limit),
        name=name,
    )(t, *arrays)


def add_entering_kernel(t_ref, y_ref, q_ref, *refs, modes, size, tp_size):
    o_ref, out_s = refs[-2:]
    inside, mine_enters, other_enters, mines, others = (
        refs[i * size : (i + 1) * size] for i in range(5)
    )
    k = pl.program_id(0)
    blocks_before = t_ref[1] * tp_size + t_ref[0]
    rows, width = y_ref.shape
    run = rows // SUBS
    even = t_ref[1] == 0
    before = lax.broadcasted_iota(jnp.int32, (SUBS, LANES), 0).astype(jnp.float32) * (-1.0 * run)
    for c in range(width // LANES):
        lanes = slice(c * LANES, (c + 1) * LANES)
        mine, other = (pick(k, half, (slice(0, modes), lanes)) for half in (mines, others))
        rate, weight = jnp.where(even, mine, other), jnp.where(even, other, mine)
        decay = jnp.exp(-rate)
        one = (slice(0, modes // 2), lanes)
        mine, other = pick(k, mine_enters, one), pick(k, other_enters, one)
        enters = jnp.concatenate(
            [jnp.where(even, mine, other), jnp.where(even, other, mine)], axis=0
        )
        state = enters * jnp.exp(rate * (blocks_before * -rows).astype(jnp.float32))
        state = (state + pick(k, inside, (slice(0, modes), lanes))) * weight * decay
        terms, steps = [], []
        for n in range(modes):
            terms.append(jnp.exp(before * rate[n : n + 1]) * state[n : n + 1])
            steps.append(wide(decay[n : n + 1]))
        for j in range(run):
            place = slice(j * SUBS, (j + 1) * SUBS)
            out_s[pl.ds(j, SUBS, stride=run)] = q_ref[place, lanes] * (y_ref[place, lanes] + added(terms))
            terms = [a * b for a, b in zip(terms, steps)]
        o_ref[:, lanes] = out_s[...].astype(o_ref.dtype)


def add_entering(t, first, y, q, families, before, modes, width=2048):
    rows, channels = y.shape
    size, quarter = len(families[0]), families[0][0].shape[1]
    chunks = quarter // width
    arrays = [a for family in families for a in family]
    there = lambda k, c, t: (0, ((k + first) ^ t[0]) * chunks + c)
    across = lambda k, c, t: (0, c)
    old = [] if before is None else [before]
    return pl.pallas_call(
        functools.partial(
            add_entering_kernel, modes=modes, size=size, tp_size=channels // quarter
        ),
        grid_spec=pltpu.PrefetchScalarGridSpec(
            num_scalar_prefetch=1,
            grid=(size, chunks),
            in_specs=[pl.BlockSpec((rows, width), there)] * 2
            + [pl.BlockSpec((a.shape[0], width), across) for a in arrays]
            + [pl.BlockSpec(memory_space=pl.ANY)] * len(old),
            out_specs=pl.BlockSpec((rows, width), there),
            scratch_shapes=[pltpu.VMEM((rows, LANES), jnp.float32)],
        ),
        out_shape=jax.ShapeDtypeStruct((rows, channels), jnp.bfloat16),
        input_output_aliases={3 + len(arrays): 0} if old else {},
        compiler_params=params_of(),
        cost_estimate=pl.CostEstimate(
            flops=size * rows * quarter * 36,
            bytes_accessed=size * rows * quarter * 10,
            transcendentals=size * modes * quarter * 9,
        ),
        name="add_entering",
    )(t, y, q, *arrays, *old)


def exchange(x, axis):
    return lax.all_to_all(x, axis, split_axis=0, concat_axis=0, tiled=True)


def trade_tp(arrays):
    size = len(arrays)
    return [arrays[0]] + [
        lax.ppermute(arrays[k], "tp", [(i, i ^ k) for i in range(size)]) for k in range(1, size)
    ]


def segment_starts(lengths, tokens):
    order = jnp.arange(lengths.shape[0], dtype=jnp.int32)
    ends = jnp.sum(jnp.where(order[:, None] <= order[None, :], lengths[:, None], 0), axis=0)
    position = jnp.arange(tokens, dtype=jnp.int32)
    passed = jnp.where(ends[None, :] <= position[:, None], ends[None, :], 0)
    return jnp.max(passed, axis=1)


def by_tokens(hyena_in, attn_in, short_taps, decay_rate, residue, lengths):
    rows, kinds, channels = hyena_in.shape
    ctx_size, tp_size = lax.axis_size("ctx"), lax.axis_size("tp")
    devices = ctx_size * tp_size
    taps_count = short_taps.shape[0]
    modes = decay_rate.shape[0]
    parity = (lax.axis_index("ctx") % 2).astype(jnp.int32)
    t = jnp.stack([lax.axis_index("tp").astype(jnp.int32), parity])
    swap = [(i, i ^ 1) for i in range(ctx_size)]

    x = jnp.transpose(hyena_in, (1, 0, 2))
    edge = x[:, rows - taps_count + 1 :].reshape(kinds * (taps_count - 1), channels)
    edge = lax.ppermute(edge, ALL, [(i, i + 1) for i in range(devices - 1)])
    mine, other = make_table(parity.reshape(1), short_taps, decay_rate, residue)
    mine = trade_tp([mine] * tp_size)
    heads_out = split_heads(jnp.transpose(attn_in, (1, 0, 2)))
    heads_out, edge, *mine = lax.optimization_barrier((heads_out, edge, *mine))
    by_head = exchange(heads_out, ALL)
    tables = mine + [other] + [lax.ppermute(half, "ctx", swap) for half in mine[1:]]
    source, enter, *ends = block_states(t, x, edge, tables, modes, taps_count)
    y, q = inside_runs(t, x, edge, source, enter, tables, modes, taps_count)
    y, *ends = lax.optimization_barrier((y, *trade_tp(ends)))
    [block_end] = small_call(
        block_end_kernel, t, "block_end", [modes], decay_rate, *ends, rows=rows
    )

    mate = lax.ppermute(block_end, "ctx", swap)
    total, *inside = small_call(
        pair_kernel, t, "pair", [modes // 2] + [modes] * tp_size,
        decay_rate, block_end, mate, *ends, rows=rows,
    )
    by_head, *_ = lax.optimization_barrier((by_head, *inside, total))
    inside = trade_tp(inside)
    total, inside[1] = lax.optimization_barrier((total, inside[1]))
    seen = [
        lax.ppermute(total, "ctx", [(i, i + hop) for i in range(ctx_size - hop)])
        for hop in range(2, ctx_size, 2)
    ]

    mixed = attend(by_head, segment_starts(lengths, rows * devices))
    mixed, seen, inside = lax.optimization_barrier((mixed, seen, inside))
    [enters] = small_call(
        pair_enters_kernel, t, "pair_enters", [modes // 2], decay_rate, *seen,
        limit=SMALL_BYTES, rows=rows * tp_size,
    )
    mate_enters = lax.ppermute(enters, "ctx", swap)
    enters = trade_tp([enters] * tp_size)
    attn_out = join_heads(exchange(mixed.reshape(devices, rows, DH), ALL))
    mines, others = tables[:tp_size], tables[tp_size:]
    own = inside[:1], enters[:1], [mate_enters], mines[:1], others[:1]
    hyena_out = add_entering(t, 0, y, q, own, None, modes)
    hyena_out, *enters = lax.optimization_barrier((hyena_out, *enters[1:]))
    mate_enters = [lax.ppermute(half, "ctx", swap) for half in enters]
    rest = inside[1:], enters, mate_enters, mines[1:], others[1:]
    hyena_out = add_entering(t, 1, y, q, rest, hyena_out, modes)
    return hyena_out, attn_out


exact_mode = lax.Precision.HIGHEST


def from_behind(block, axis, distance):
    devices = range(lax.axis_size(axis))
    route = [(i - distance, i) for i in devices if i - distance in devices]
    return lax.ppermute(block, axis, route)


def carried_in(part, axis, combine, identity):
    place = lax.axis_index(axis)
    gathered = jax.tree.map(lambda a: lax.all_gather(a, axis), part)
    state = jax.tree.map(lambda a, e: jnp.zeros_like(a) + jnp.asarray(e, a.dtype), part, identity)

    def one(lap, state):
        return combine(
            state, jax.tree.map(lambda a: lax.dynamic_index_in_dim(a, lap, 0, False), gathered)
        )

    return lax.fori_loop(0, place, one, state)


def segment_of(positions, segment_ends):
    return jnp.sum((segment_ends[None, :] <= positions[:, None]).astype(jnp.int32), axis=1)


def by_channels(hyena_in, attn_in, short_taps, decay_rate, residue, lengths):
    hyena_cols, attention_cols = (
        lax.all_to_all(hyena_in, "tp", split_axis=2, concat_axis=0, tiled=True),
        lax.all_to_all(attn_in, "tp", split_axis=2, concat_axis=0, tiled=True),
    )
    block_rows = hyena_cols.shape[0]
    rim_rows = short_taps.shape[0] - 1
    edge_rows = from_behind(hyena_cols[block_rows - rim_rows :], "ctx", 1)
    extended = jnp.concatenate([edge_rows, hyena_cols], axis=0).astype(jnp.float32)
    filtered = jnp.zeros(hyena_cols.shape, jnp.float32)
    for lag in range(rim_rows + 1):
        filtered = (
            filtered + short_taps[lag] * extended[rim_rows - lag : rim_rows - lag + block_rows]
        )
    query_side = filtered[:, 0]
    source = filtered[:, 1] * filtered[:, 2]
    channels = source.shape[1]
    weight = residue * jnp.sqrt(-jnp.expm1(-2.0 * decay_rate))
    sub_length = math.gcd(32, block_rows)
    pieces = block_rows // sub_length
    offsets = jnp.arange(sub_length, dtype=jnp.float32)
    powers = jnp.exp(-offsets[:, None, None] * decay_rate[None])
    lag_values = jnp.einsum("onc,nc->oc", powers, weight, precision=exact_mode)
    lag_index = jnp.arange(sub_length, dtype=jnp.int32)
    selector = (
        lag_index[:, None, None] - lag_index[None, :, None] == lag_index[None, None, :]
    ).astype(jnp.float32)
    toeplitz = jnp.einsum("tso,oc->tsc", selector, lag_values, precision=exact_mode)
    grouped = source.reshape(pieces, sub_length, channels)
    inner = jnp.einsum("tsc,bsc->btc", toeplitz, grouped, precision=exact_mode)
    tail_powers = jnp.exp(-(sub_length - 1.0 - offsets)[:, None, None] * decay_rate[None])
    own_states = jnp.einsum("snc,bsc->bnc", tail_powers, grouped, precision=exact_mode)
    sub_decay = jnp.exp(-sub_length * decay_rate)

    def carry_states(carried, incoming):
        return (sub_decay * carried + incoming, carried)

    local_end, entering = lax.scan(carry_states, jnp.zeros_like(sub_decay), own_states)
    block_decay = jnp.exp(-block_rows * decay_rate)

    def combine(earlier, later):
        return (earlier[0] * later[0], later[0] * earlier[1] + later[1])

    _, arriving = carried_in(
        (block_decay, local_end),
        "ctx",
        combine,
        (jnp.ones_like(block_decay), jnp.zeros_like(local_end)),
    )
    starts = jnp.arange(pieces, dtype=jnp.float32) * sub_length
    all_entering = entering + jnp.exp(-starts[:, None, None] * decay_rate[None]) * arriving[None]
    rise_powers = jnp.exp(-(offsets + 1.0)[:, None, None] * decay_rate[None]) * weight[None]
    from_state = jnp.einsum("tnc,bnc->btc", rise_powers, all_entering, precision=exact_mode)
    long_conv = (inner + from_state).reshape(block_rows, channels)
    hyena_local = (query_side * long_conv).astype(jnp.bfloat16)
    head_cols = attention_cols.shape[2]
    local_heads = head_cols // DH
    queries = attention_cols[:, 0].reshape(block_rows, local_heads, DH)
    keyvals = attention_cols[:, 1:3]
    order = jnp.arange(lengths.shape[0], dtype=jnp.int32)
    segment_ends = jnp.sum(jnp.where(order[:, None] <= order[None, :], lengths[:, None], 0), axis=0)
    block_index = lax.axis_index("ctx")
    query_pos = block_index * block_rows + jnp.arange(block_rows, dtype=jnp.int32)
    query_seg = segment_of(query_pos, segment_ends)
    score_scale = 1.0 / math.sqrt(DH)

    def attend_part(softmax_state, part, key_start):
        count = part.shape[0]
        key_pos = key_start + jnp.arange(count, dtype=jnp.int32)
        key_seg = segment_of(key_pos, segment_ends)
        allowed = (
            (key_pos[None, :] <= query_pos[:, None])
            & (key_seg[None, :] == query_seg[:, None])
            & (key_pos >= 0)[None, :]
        )

        def compute(carried):
            row_top, denom, weighted = carried
            key_rows = part[:, 0].reshape(count, local_heads, DH)
            value_rows = part[:, 1].reshape(count, local_heads, DH)
            scores = (
                jnp.einsum("qhd,khd->hqk", queries, key_rows, preferred_element_type=jnp.float32)
                * score_scale
            )
            masked = jnp.where(allowed[None], scores, jnp.float32(-1e30))
            new_top = jnp.maximum(row_top, jnp.max(masked, axis=2))
            expo = jnp.where(allowed[None], jnp.exp(scores - new_top[:, :, None]), jnp.float32(0.0))
            rescale = jnp.exp(row_top - new_top)
            denom = denom * rescale + jnp.sum(expo, axis=2)
            probs = expo.astype(jnp.bfloat16)
            added = jnp.einsum(
                "hqk,khd->qhd", probs, value_rows, preferred_element_type=jnp.float32
            )
            weighted = weighted * jnp.transpose(rescale)[:, :, None] + added
            return (new_top, denom, weighted)

        def keep(carried):
            return carried

        return lax.cond(jnp.any(allowed), compute, keep, softmax_state)

    initial = (
        jnp.full((local_heads, block_rows), -1e30, jnp.float32),
        jnp.zeros((local_heads, block_rows), jnp.float32),
        jnp.zeros((block_rows, local_heads, DH), jnp.float32),
    )
    piece = lax.all_gather(keyvals, "ctx", axis=0, tiled=True)
    rows = piece.shape[0]
    step_rows = math.gcd(rows, 512)

    def advance(count, carried):
        part = lax.dynamic_slice_in_dim(piece, count * step_rows, step_rows, 0)
        return attend_part(carried, part, count * step_rows)

    final_state = lax.fori_loop(0, rows // step_rows, advance, initial)
    _, denom, weighted = final_state
    attention_local = (
        (weighted / jnp.transpose(denom)[:, :, None])
        .reshape(block_rows, head_cols)
        .astype(jnp.bfloat16)
    )
    hyena_out, attn_out = (
        lax.all_to_all(hyena_local, "tp", split_axis=0, concat_axis=1, tiled=True),
        lax.all_to_all(attention_local, "tp", split_axis=0, concat_axis=1, tiled=True),
    )
    return (hyena_out, attn_out)


def per_device(hyena_in, attn_in, short_taps, decay_rate, residue, lengths):
    rows, _, channels = hyena_in.shape
    devices = lax.axis_size("ctx") * lax.axis_size("tp")
    one_head_each = attn_in.shape[2] == devices * DH
    tp_size = lax.axis_size("tp")
    pairs = tp_size & (tp_size - 1) == 0
    pairs = pairs and lax.axis_size("ctx") >= 4 and lax.axis_size("ctx") % 2 == 0
    whole_tiles = pairs and rows % (2 * SUBS) == 0 and channels % (tp_size * 2048) == 0
    whole_tiles = whole_tiles and decay_rate.shape[0] % (2 * SUBS) == 0
    plan = by_tokens if one_head_each and whole_tiles else by_channels
    return plan(hyena_in, attn_in, short_taps, decay_rate, residue, lengths)


def solution(mesh):
    placed = (
        P(("ctx", "tp"), None, None),
        P(("ctx", "tp"), None, None),
        P(None, None, "tp"),
        P(None, "tp"),
        P(None, "tp"),
        P(),
    )
    return jax.shard_map(
        per_device,
        mesh=mesh,
        in_specs=placed,
        out_specs=(P(("ctx", "tp"), None), P(("ctx", "tp"), None)),
        check_vma=False,
    )
```
